256 devices in a mesh: dp: 128 (over y_lo, x, z, core), tensor: 2 (over y_hi).
Axes of the slice: x: 4, y: 4 (y_hi: 2, y_lo: 2; y = y_hi * 2 + y_lo), z: 8, core: 2. Of those that a mesh axis runs over, the one named last changes fastest.
Arguments:
- images: bfloat16 [32768, 2048], P('dp'), may hold values from -24 to 24
- texts: bfloat16 [32768, 4096], P('dp', 'tensor'), may hold values from -6 to 6
- head: bfloat16 [2048, 4096], P(None, 'tensor'), may hold values from -0.125 to 0.125
- pair_mask: int32 [128, 4], P('dp'), may hold values 0 or 1
- labels: int32 [32768], P('dp'), may hold values from 0 to 1023
- logit_scale: float32 [1], replicated, may hold values from 8 to 16
- logit_bias: float32 [1], replicated, may hold values from -3 to -1
Outputs:
- grad_images: bfloat16 [32768, 2048], P('dp', 'tensor')
- grad_texts: bfloat16 [32768, 4096], P('dp', 'tensor')
- grad_head: float32 [2048, 4096], P('dp', 'tensor')
The draws below stay inside these ranges and needn't reach their ends.
All inputs are finite; a program needn't handle non-finite values. No bound on the sum of `pair_mask` on one device may be relied on, other than what follows from the above.
Results may differ from the reference program's by a relative error of at most 0.0063.
Values may be sent and summed in bfloat16 or wider, within the bound.
No kernel may reach another device: no remote copies, remote signals or barrier semaphores. Data moves between devices by JAX's collectives and lax.ppermute only.
A program may use at most 128 MiB of HBM per device.

```python
import jax
import jax.numpy as jnp
from jax import lax

D_IN = 2048
D = 4096
ROWS = 256
STEPS = 4
BLOCKS = 128
IMAGES = 32768
TEXTS = 32768


def plant(array, key, low, largest):
    spot = [jax.random.randint(jax.random.fold_in(key, axis), (), 0, length) for axis, length in enumerate(array.shape)]
    widest = array.shape.index(max(array.shape))
    next_to = spot[:widest] + [(spot[widest] + 1) % array.shape[widest]] + spot[widest + 1:]
    return array.at[tuple(spot)].set(low).at[tuple(next_to)].set(largest)


def spiked(drawn, stream_key, source, target, blocks, factor):
    owner, partner = [(jnp.arange(drawn.shape[dim]) // (drawn.shape[dim] // blocks)).reshape([-1 if axis == dim else 1 for axis in range(drawn.ndim)]) for dim in (source, target)]
    chosen = jax.random.permutation(stream_key, blocks)[partner]
    strong = (owner == chosen) | (owner == (partner + blocks // 2) % blocks)
    return jnp.where(strong, factor * drawn, drawn)


def steps_of(rng, dims, shards, smallest, high):
    def one(position, parts):
        draws = jax.random.uniform(jax.random.fold_in(jax.random.fold_in(rng, 6), position), (parts,), jnp.float32, smallest / len(shards), high / len(shards))
        return jnp.repeat(jnp.exp(draws), dims[position] // parts).reshape((-1,) + (1,) * (len(dims) - position - 1))

    level = one(*shards[0])
    for cut in shards[1:]:
        level = level * one(*cut)
    return level


def centred(own_key, dims, width, limit, pieces=(), kind=jnp.bfloat16):
    drawn = jax.random.normal(own_key, dims, jnp.float32) * width
    if len(pieces) > 0:
        drawn = steps_of(own_key, dims, pieces, -0.22, 0.18) * drawn
    return jnp.clip(drawn, min=-limit, max=limit).astype(kind)


def gaussian_with(stream_key, dims, scale, reach, shards, heavy, held_as=jnp.bfloat16):
    array = scale * jax.random.normal(stream_key, dims, jnp.float32)
    if shards:
        array = array * steps_of(stream_key, dims, shards, -0.22, 0.18)
    return jnp.clip(spiked(array, jax.random.fold_in(stream_key, 3), *heavy), -reach, reach).astype(held_as)


def setup_inputs(seed: int = 0) -> dict:
    streams_of = jax.random.split(jax.random.key(seed), 8)
    return {
        "images": gaussian_with(streams_of[0], (IMAGES, D_IN), 1.0, 24.0, ((0, 128),), (0, 1, 128, 5.5)),
        "texts": centred(streams_of[1], (TEXTS, D), 1.0, 6.0, ((0, 128), (1, 2))),
        "head": centred(streams_of[2], (D_IN, D), D_IN ** -0.5, 0.125, ((1, 2),)),
        "pair_mask": plant((jax.random.randint(streams_of[3], (BLOCKS, STEPS), 0, 2) < 1).astype(jnp.int32), jax.random.fold_in(streams_of[3], 1), 0, 1),
        "labels": plant(jax.random.randint(streams_of[4], (IMAGES,), 0, STEPS * ROWS), jax.random.fold_in(streams_of[4], 1), 0, (STEPS * ROWS) - 1).astype(jnp.int32),
        "logit_scale": jnp.clip(jax.random.uniform(streams_of[5], (1,), jnp.float32, 8.0, 16.0), 8.0, 16.0),
        "logit_bias": jnp.clip(jax.random.uniform(streams_of[6], (1,), jnp.float32, -3.0, -1.0), -3.0, -1.0),
    }


EPSILON = 1e-06
LOSS_WEIGHT = 16.0

def reference(images, texts, head, pair_mask, labels, logit_scale, logit_bias):
    projected = jnp.dot(images, head, preferred_element_type=jnp.float32)
    inverse_image = lax.rsqrt(lax.optimization_barrier(jnp.sum(projected * projected, axis=1, keepdims=True)) + EPSILON)
    unit_image_f = projected * inverse_image
    unit_image = unit_image_f.astype(jnp.bfloat16)
    text_float = texts.astype(jnp.float32)
    inverse_text = lax.rsqrt(lax.optimization_barrier(jnp.sum(text_float * text_float, axis=1, keepdims=True)) + EPSILON)
    unit_text_f = text_float * inverse_text
    unit_text = unit_text_f.astype(jnp.bfloat16)
    image_blocks = unit_image.astype(jnp.float32).reshape(BLOCKS, ROWS, D)
    text_blocks = unit_text.astype(jnp.float32).reshape(BLOCKS, ROWS, D)
    label_blocks = labels.reshape(BLOCKS, ROWS, 1)
    columns = jnp.arange(ROWS, dtype=jnp.int32)[None, None, :]
    scale_value = logit_scale[0]
    bias_value = logit_bias[0]
    image_pull = jnp.zeros((BLOCKS, ROWS, D), jnp.float32)
    text_pull = jnp.zeros((BLOCKS, ROWS, D), jnp.float32)
    for offset in range(STEPS):
        current = jnp.roll(text_blocks, offset, axis=0)
        scores = jnp.einsum('brd,bcd->brc', image_blocks, current, precision=lax.Precision.HIGHEST)
        logits = scale_value * scores + bias_value
        label_sign = jnp.where(label_blocks == offset * ROWS + columns, 1.0, -1.0).astype(jnp.float32)
        weight = pair_mask[:, offset].astype(jnp.float32)[:, None, None]
        coefficient = -LOSS_WEIGHT * scale_value * weight * label_sign * jax.nn.sigmoid(-label_sign * logits)
        coefficient = coefficient.astype(jnp.bfloat16).astype(jnp.float32)
        image_pull = image_pull + jnp.einsum('brc,bcd->brd', coefficient, current, precision=lax.Precision.HIGHEST)
        text_term = jnp.einsum('brc,brd->bcd', coefficient, image_blocks, precision=lax.Precision.HIGHEST)
        text_pull = text_pull + jnp.roll(text_term, -offset, axis=0)
    image_pull = image_pull.reshape(IMAGES, D)
    text_pull = text_pull.reshape(TEXTS, D)
    dot_image = lax.optimization_barrier(jnp.sum(unit_image_f * image_pull, axis=1, keepdims=True))
    dot_text = lax.optimization_barrier(jnp.sum(unit_text_f * text_pull, axis=1, keepdims=True))
    grad_unit = ((image_pull - unit_image_f * dot_image) * inverse_image).astype(jnp.bfloat16)
    grad_texts = ((text_pull - unit_text_f * dot_text) * inverse_text).astype(jnp.bfloat16)
    grad_images = jnp.dot(grad_unit, head.T, preferred_element_type=jnp.float32).astype(jnp.bfloat16)
    grad_head = jnp.dot(images.T, grad_unit, preferred_element_type=jnp.float32)
    return (grad_images, grad_texts, grad_head)
```

```python
import jax
import jax.numpy as jnp
from jax import lax
from jax.sharding import PartitionSpec as P

EPSILON = 1e-06
LOSS_WEIGHT = 16.0
YS, XS, ZS, CORES = 2, 4, 8, 2
SPLIT = 1280

F32 = jnp.float32
BF16 = jnp.bfloat16


def place(index):
    return index // (XS * ZS * CORES), index // (ZS * CORES) % XS, index // CORES % ZS, index % CORES


def index_of(y, x, z, core):
    return (((y % YS) * XS + x % XS) * ZS + z % ZS) * CORES + core % CORES


def route(target):
    return [(i, target(i) % (YS * XS * ZS * CORES)) for i in range(YS * XS * ZS * CORES)]


def send(block, target):
    return lax.ppermute(block, "dp", route(target))


def swap_tensor(block):
    return lax.ppermute(block, "tensor", [(0, 1), (1, 0)])


def over_x(distance):
    def target(i):
        y, x, z, core = place(i)
        return index_of(y, x + distance, z, core)

    return target


def over_z(distance):
    def target(i):
        y, x, z, core = place(i)
        return index_of(y, x, z + distance, core)

    return target


def over_y(i):
    y, x, z, core = place(i)
    return index_of(y + 1, x, z, core)


def other_core(i):
    return i ^ 1


def dot(a, b, left, right):
    return lax.dot_general(a, b, (((left,), (right,)), ((), ())), preferred_element_type=F32)


def turn(array, axis, start):
    return lax.dynamic_slice_in_dim(
        jnp.concatenate([array, array], axis=axis), start, array.shape[axis], axis=axis
    )


def per_device(images, texts, head, pair_mask, labels, logit_scale, logit_bias):
    row_count = images.shape[0]
    me = lax.axis_index("dp")
    here_y, here_x, here_z, core = place(me)
    half = lax.axis_index("tensor")
    scale_value = logit_scale[0]
    bias_value = logit_bias[0]

    near_text = send(texts, lambda i: i + 2)
    cross_text = send(near_text, other_core)
    far_text = send(
        jnp.where(core == 0, texts, near_text), lambda i: i + 1
    )
    images_pair = send(images, other_core)

    projected = jnp.dot(images, head, preferred_element_type=F32)
    projected_b = projected.astype(BF16)
    near_image = send(projected_b, lambda i: i - 2)
    cross_image = send(near_image, other_core)
    far_image = send(jnp.where(core == 1, projected_b, near_image), lambda i: i - 1)

    text_float = texts.astype(F32)
    square_image = jnp.sum(projected * projected, axis=1)
    square_text = jnp.sum(text_float * text_float, axis=1)
    squares = jnp.stack([square_image, square_text])
    squares = squares + swap_tensor(squares)
    inverses = lax.rsqrt(squares + EPSILON)
    inverse_image = inverses[0][:, None]
    inverse_text = inverses[1][:, None]
    inverse_own = inverses[1:2]
    inverse_near = send(inverse_own, lambda i: i + 2)
    inverse_cross = send(inverse_own, lambda i: i + 1 if i % 2 else i + 3)
    inverse_far = send(inverse_own, lambda i: i + 3 if i % 2 else i + 1)

    columns = jnp.arange(row_count, dtype=jnp.int32)[None, :]

    def tile(block, inverse, offset):
        partial = dot(projected_b, block, 1, 1)
        scores = (partial + swap_tensor(partial.astype(BF16)).astype(F32)) * inverse_image * inverse
        logits = scale_value * scores + bias_value
        sign = jnp.where(labels[:, None] == offset * row_count + columns, 1.0, -1.0).astype(F32)
        weight = lax.dynamic_index_in_dim(pair_mask[0], offset, keepdims=False).astype(F32)
        coefficient = (-LOSS_WEIGHT * scale_value * weight) * sign * jax.nn.sigmoid(-sign * logits)
        pulled = dot((coefficient * inverse).astype(BF16), block, 1, 0)
        inner = jnp.sum(coefficient * scores, axis=1, keepdims=True)
        return pulled, inner, (coefficient * inverse_image).astype(BF16)

    own_pull, own_inner, own_coefficient = tile(texts, inverse_own, 0)
    near_pull, near_inner, near_coefficient = tile(near_text, inverse_near, 2)
    cross_pull, cross_inner, cross_coefficient = tile(cross_text, inverse_cross, 1 + 2 * core)
    far_pull, far_inner, far_coefficient = tile(far_text, inverse_far, 3 - 2 * core)

    image_pull = own_pull + near_pull + cross_pull + far_pull
    dot_image = own_inner + near_inner + cross_inner + far_inner
    grad_unit = (
        (image_pull - projected * (inverse_image * dot_image)) * inverse_image
    ).astype(BF16)

    grad_pair = jnp.concatenate([grad_unit, send(grad_unit, other_core)], axis=0)
    turned = jnp.concatenate([images, images_pair], axis=0).T
    depth = turned.shape[1]
    unit = turned.shape[0] // (YS * XS * ZS * CORES)
    turned = turned.reshape(YS, XS, ZS, CORES, unit, depth)
    turned = lax.dynamic_index_in_dim(turned, core, axis=3, keepdims=False)
    turned = turn(turn(turn(turned, 0, here_y), 1, here_x), 2, here_z)
    by_x = turned.transpose(1, 2, 0, 3, 4).reshape(XS, ZS * YS * unit, depth)
    by_z = turned.transpose(2, 1, 0, 3, 4).reshape(ZS, XS * YS * unit, depth)
    grad_a, grad_b = grad_pair[:, :SPLIT], grad_pair[:, SPLIT:]

    def exchange(pieces, over):
        got = [send(piece.astype(BF16), over(d)) for d, piece in pieces if d]
        total = dict(pieces)[0].astype(F32)
        for part in got:
            total = total + part.astype(F32)
        return total

    part_a = exchange([(d, dot(by_x[d], grad_a, 1, 0)) for d in (1, 3, 2, 0)], over_x)
    part_b = exchange([(d, dot(by_z[d], grad_b, 1, 0)) for d in (1, 7, 2, 6, 3, 5, 4, 0)], over_z)
    part_a = part_a.astype(BF16).reshape(ZS, YS * unit, -1)
    part_a = exchange([(d, part_a[d]) for d in (1, 7, 2, 6, 3, 5, 4, 0)], over_z)
    part_b = part_b.astype(BF16).reshape(XS, YS * unit, -1)
    part_b = exchange([(d, part_b[d]) for d in (1, 3, 2, 0)], over_x)
    both = jnp.concatenate([part_a, part_b], axis=1)
    grad_head = both[:unit] + send(both[unit:].astype(BF16), over_y).astype(F32)

    near_back = send(near_coefficient, lambda i: i - 2)
    cross_back = send(cross_coefficient, lambda i: i - 3 if i % 2 else i - 1)
    far_back = send(far_coefficient, lambda i: i - 1 if i % 2 else i - 3)
    text_pull = (
        dot(own_coefficient, projected_b, 0, 0)
        + dot(near_back, near_image, 0, 0)
        + dot(cross_back, cross_image, 0, 0)
        + dot(far_back, far_image, 0, 0)
    )
    unit_text = text_float * inverse_text
    dot_text = jnp.sum(unit_text * text_pull, axis=1)
    dot_text = (dot_text + swap_tensor(dot_text))[:, None]
    grad_texts = ((text_pull - unit_text * dot_text) * inverse_text).astype(BF16)

    span = head.shape[0] // 2
    head_here = lax.dynamic_slice_in_dim(head, half * span, span, axis=0)
    head_there = lax.dynamic_slice_in_dim(head, (1 - half) * span, span, axis=0)
    there = swap_tensor(dot(grad_unit, head_there, 1, 1).astype(BF16))
    grad_images = (dot(grad_unit, head_here, 1, 1) + there.astype(F32)).astype(BF16)
    return (grad_images, grad_texts, grad_head)


def solution(mesh):
    return jax.shard_map(
        per_device,
        mesh=mesh,
        in_specs=(
            P("dp", None),
            P("dp", "tensor"),
            P(None, "tensor"),
            P("dp", None),
            P("dp"),
            P(),
            P(),
        ),
        out_specs=(P("dp", "tensor"), P("dp", "tensor"), P("dp", "tensor")),
        check_vma=False,
    )
```

```python
import jax
import jax.numpy as jnp
from jax import lax
from jax.sharding import PartitionSpec as P

EPSILON = 1e-06
LOSS_WEIGHT = 16.0
YS, XS, ZS, CORES = 2, 4, 8, 2
SPLIT = 1024

F32 = jnp.float32
BF16 = jnp.bfloat16


def place(index):
    return index // (XS * ZS * CORES), index // (ZS * CORES) % XS, index // CORES % ZS, index % CORES


def index_of(y, x, z, core):
    return (((y % YS) * XS + x % XS) * ZS + z % ZS) * CORES + core % CORES


def route(target):
    return [(i, target(i) % (YS * XS * ZS * CORES)) for i in range(YS * XS * ZS * CORES)]


def send(block, target):
    return lax.ppermute(block, "dp", route(target))


def swap_tensor(block):
    return lax.ppermute(block, "tensor", [(0, 1), (1, 0)])


def over_x(distance):
    def target(i):
        y, x, z, core = place(i)
        return index_of(y, x + distance, z, core)

    return target


def over_z(distance):
    def target(i):
        y, x, z, core = place(i)
        return index_of(y, x, z + distance, core)

    return target


def over_y(i):
    y, x, z, core = place(i)
    return index_of(y + 1, x, z, core)


def other_core(i):
    return i ^ 1


def dot(a, b, left, right):
    return lax.dot_general(a, b, (((left,), (right,)), ((), ())), preferred_element_type=F32)


def turn(array, axis, start):
    return lax.dynamic_slice_in_dim(
        jnp.concatenate([array, array], axis=axis), start, array.shape[axis], axis=axis
    )


def after(value, *earlier):
    return lax.optimization_barrier((value,) + earlier)[0]


def per_device(images, texts, head, pair_mask, labels, logit_scale, logit_bias):
    row_count = images.shape[0]
    me = lax.axis_index("dp")
    core = me & 1
    here_x = (me >> 4) & (XS - 1)
    here_y = me >> 6
    half = lax.axis_index("tensor")
    first_core = core == 0
    scale_value = logit_scale[0]
    bias_value = logit_bias[0]
    columns = jnp.arange(row_count, dtype=jnp.int32)[None, :]

    near_text = send(texts, lambda i: i + 2)
    images_pair = send(images, other_core)
    text_float = texts.astype(F32)
    square_text = jnp.sum(text_float * text_float, axis=1)

    projected = jnp.dot(images, head, preferred_element_type=F32)
    projected_b = projected.astype(BF16)
    near_image = send(projected_b, lambda i: i - 2)
    squares = jnp.stack([jnp.sum(projected * projected, axis=1), square_text])
    inverses = lax.rsqrt(squares + swap_tensor(squares) + EPSILON)
    inverse_image = inverses[0].reshape(row_count, 1)
    inverse_own = inverses[1:]
    inverse_text = inverse_own.reshape(row_count, 1)

    turned = jnp.concatenate([images, images_pair], axis=0).T
    depth = turned.shape[1]
    unit = turned.shape[0] // (YS * XS * ZS * CORES)
    turned = turned.reshape(YS, XS, ZS, CORES, unit, depth)
    turned = lax.dynamic_index_in_dim(turned, core, axis=3, keepdims=False)
    turned = turn(turn(turned, 0, here_y), 1, here_x)

    def tile(scores, inverse, offset, weight):
        scores = scores * inverse_image * inverse
        logits = scale_value * scores + bias_value
        sign = jnp.where(labels[:, None] == offset * row_count + columns, 1.0, -1.0).astype(F32)
        coefficient = (
            (-LOSS_WEIGHT * scale_value * weight.astype(F32)) * sign * jax.nn.sigmoid(-sign * logits)
        )
        inner = jnp.sum(coefficient * scores, axis=1, keepdims=True)
        return (coefficient * inverse).astype(BF16), inner, (coefficient * inverse_image).astype(BF16)

    mask = pair_mask[0]
    own_part = dot(projected_b, texts, 1, 1)
    own_scores = own_part + swap_tensor(own_part.astype(BF16)).astype(F32)
    own_weight, own_inner, own_back = tile(own_scores, inverse_own, 0, mask[0])
    own_pull = dot(own_weight, texts, 1, 0)

    inverse_sent = after(inverse_own, turned, own_pull, own_back)
    inverse_near = send(inverse_sent, lambda i: i + 2)
    inverse_cross = send(inverse_sent, lambda i: i + 1 if i % 2 else i + 3)
    inverse_far = send(inverse_sent, lambda i: i + 3 if i % 2 else i + 1)
    near_text = after(near_text, inverse_near, inverse_cross, inverse_far)
    forward = jnp.where(first_core, texts, near_text)
    far_text = send(forward, lambda i: i + 1)
    cross_text = send(after(near_text, forward), other_core)
    near_part = dot(projected_b, near_text, 1, 1)
    image_forward = jnp.where(first_core, near_image, projected_b)
    far_image = send(image_forward, lambda i: i - 1)
    cross_image = send(near_image, other_core)
    cross_text = after(cross_text, near_part, image_forward)
    two_part = jnp.concatenate([near_part, dot(projected_b, cross_text, 1, 1)], axis=0)
    two_scores = two_part + swap_tensor(two_part.astype(BF16)).astype(F32)
    far_part = dot(projected_b, far_text, 1, 1)
    two_scores = after(two_scores, far_part, cross_image, far_image)
    near_weight, near_inner, near_back = tile(two_scores[:row_count], inverse_near, 2, mask[2])
    cross_weight, cross_inner, cross_back = tile(
        two_scores[row_count:], inverse_cross, 1 + 2 * core, jnp.where(first_core, mask[1], mask[3])
    )
    some_pull = own_pull + dot(near_weight, near_text, 1, 0) + dot(cross_weight, cross_text, 1, 0)

    far_scores = far_part + swap_tensor(far_part.astype(BF16)).astype(F32)
    far_scores = after(far_scores, some_pull, near_back, cross_back)
    far_weight, far_inner, far_back = tile(
        far_scores, inverse_far, 3 - 2 * core, jnp.where(first_core, mask[3], mask[1])
    )
    image_pull = some_pull + dot(far_weight, far_text, 1, 0)
    dot_image = own_inner + near_inner + cross_inner + far_inner
    grad_unit = (
        (image_pull - projected * (inverse_image * dot_image)) * inverse_image
    ).astype(BF16)

    grad_pair = jnp.concatenate([grad_unit, send(grad_unit, other_core)], axis=0)
    grad_a, grad_b = grad_pair[:, :SPLIT], grad_pair[:, SPLIT:]
    by_x = [turned[:, d].reshape(YS * ZS * unit, depth) for d in range(XS)]
    by_y = [turned[d].reshape(XS * ZS * unit, depth) for d in range(YS)]

    sends_a = {d: dot(by_x[d], grad_a, 1, 0).astype(BF16) for d in (2, 1, 3)}
    send_b = dot(by_y[1], grad_b, 1, 0).astype(BF16)
    gots_a = [send(piece, over_x(d)) for d, piece in sends_a.items()]
    got_b = send(send_b, over_y)
    stay_a = dot(by_x[0], grad_a, 1, 0)
    stay_b = dot(by_y[0], grad_b, 1, 0)
    part_a = stay_a
    for got in gots_a:
        part_a = part_a + got.astype(F32)
    part_a = part_a.reshape(YS, ZS * unit, -1)
    part_b = (stay_b + got_b.astype(F32)).astype(BF16).reshape(XS, ZS * unit, -1)
    gots_b = [send(part_b[d], over_x(d)) for d in (2, 1, 3)]
    got_a = send(part_a[1].astype(BF16), over_y)
    last_a = part_a[0] + got_a.astype(F32)
    last_b = part_b[0].astype(F32)
    for got in gots_b:
        last_b = last_b + got.astype(F32)
    last = jnp.concatenate([last_a, last_b], axis=1).astype(BF16).reshape(ZS, unit, -1)
    line = [
        [index_of(y, x, z, c) for z in range(ZS)]
        for y in range(YS)
        for x in range(XS)
        for c in range(CORES)
    ]
    last = lax.all_to_all(last, "dp", 0, 0, axis_index_groups=line, tiled=True)
    grad_head = jnp.sum(last.astype(F32), axis=0)

    near_back, cross_back, far_back, own_back, grad_late = lax.optimization_barrier(
        (near_back, cross_back, far_back, own_back, grad_unit)
        + (send_b, *sends_a.values())
    )[:5]
    near_back = send(near_back, lambda i: i - 2)
    cross_back = send(cross_back, lambda i: i - 3 if i % 2 else i - 1)
    far_back = send(far_back, lambda i: i - 1 if i % 2 else i - 3)
    text_pull = (
        dot(own_back, projected_b, 0, 0)
        + dot(near_back, near_image, 0, 0)
        + dot(cross_back, cross_image, 0, 0)
        + dot(far_back, far_image, 0, 0)
    )
    unit_text = text_float * inverse_text
    dot_text = jnp.sum(unit_text * text_pull, axis=1)
    dot_text = (dot_text + swap_tensor(dot_text))[:, None]
    grad_texts = ((text_pull - unit_text * dot_text) * inverse_text).astype(BF16)

    span = head.shape[0] // 2
    head_here = lax.dynamic_slice_in_dim(head, half * span, span, axis=0)
    head_there = lax.dynamic_slice_in_dim(head, (1 - half) * span, span, axis=0)
    there = swap_tensor(dot(grad_late, head_there, 1, 1).astype(BF16))
    grad_images = (dot(grad_late, head_here, 1, 1) + there.astype(F32)).astype(BF16)
    return (grad_images, grad_texts, grad_head)


def solution(mesh):
    return jax.shard_map(
        per_device,
        mesh=mesh,
        in_specs=(
            P("dp", None),
            P("dp", "tensor"),
            P(None, "tensor"),
            P("dp", None),
            P("dp"),
            P(),
            P(),
        ),
        out_specs=(P("dp", "tensor"), P("dp", "tensor"), P("dp", "tensor")),
        check_vma=False,
    )
```

```python
import jax
import jax.numpy as jnp
from jax import lax
from jax.sharding import PartitionSpec as P

EPSILON = 1e-06
LOSS_WEIGHT = 16.0
YS, XS, ZS, CORES = 2, 4, 8, 2
SPLIT = 1024

F32 = jnp.float32
BF16 = jnp.bfloat16


def place(index):
    return index // (XS * ZS * CORES), index // (ZS * CORES) % XS, index // CORES % ZS, index % CORES


def index_of(y, x, z, core):
    return (((y % YS) * XS + x % XS) * ZS + z % ZS) * CORES + core % CORES


def route(target):
    return [(i, target(i) % (YS * XS * ZS * CORES)) for i in range(YS * XS * ZS * CORES)]


def send(block, target):
    return lax.ppermute(block, "dp", route(target))


def swap_tensor(block):
    return lax.ppermute(block, "tensor", [(0, 1), (1, 0)])


def over_x(distance):
    def target(i):
        y, x, z, core = place(i)
        return index_of(y, x + distance, z, core)

    return target


def over_z(distance):
    def target(i):
        y, x, z, core = place(i)
        return index_of(y, x, z + distance, core)

    return target


def over_y(i):
    y, x, z, core = place(i)
    return index_of(y + 1, x, z, core)


def other_core(i):
    return i ^ 1


def dot(a, b, left, right):
    return lax.dot_general(a, b, (((left,), (right,)), ((), ())), preferred_element_type=F32)


def turn(array, axis, start):
    return lax.dynamic_slice_in_dim(
        jnp.concatenate([array, array], axis=axis), start, array.shape[axis], axis=axis
    )


def nothing(*arrays):
    return jnp.sum(sum(array[:8, :128].astype(F32) for array in arrays)) * 0.0


def per_device(images, texts, head, pair_mask, labels, logit_scale, logit_bias):
    row_count = images.shape[0]
    me = lax.axis_index("dp")
    core = me & 1
    here_x = (me >> 4) & (XS - 1)
    here_y = me >> 6
    half = lax.axis_index("tensor")
    first_core = core == 0
    columns = jnp.arange(row_count, dtype=jnp.int32)[None, :]

    near_text = send(texts, lambda i: i + 2)
    near_image = send(images, lambda i: i - 2)

    unit = images.shape[1] // (YS * XS * ZS * CORES)
    turned = images.T.reshape(YS, XS, ZS, CORES, unit, row_count)
    turned_own = jnp.where(first_core, turned[:, :, :, 0], turned[:, :, :, 1])
    turned_pair = send(jnp.where(first_core, turned[:, :, :, 1], turned[:, :, :, 0]), other_core)
    turned_own = turn(turn(turned_own, 0, here_y), 1, here_x)
    turned_pair = turn(turn(turned_pair, 0, here_y), 1, here_x)

    text_float = texts.astype(F32)
    projected = jnp.dot(images, head, preferred_element_type=F32)
    projected_b = projected.astype(BF16)
    squares = jnp.stack([jnp.sum(projected * projected, axis=1), jnp.sum(text_float * text_float, axis=1)])
    squares_there = swap_tensor(squares)
    own_part = dot(projected_b, texts, 1, 1)
    own_there = swap_tensor(own_part.astype(BF16))

    forward = jnp.where(first_core, texts, near_text)
    far_text = send(forward, lambda i: i + 1)
    cross_text = send(near_text, other_core)
    image_forward = jnp.where(first_core, near_image, images)
    far_image = send(image_forward, lambda i: i - 1)
    cross_image = send(near_image, other_core)

    near_part = dot(projected_b, near_text, 1, 1)
    inverses = lax.rsqrt(squares + squares_there + (EPSILON + nothing(near_part)))
    inverse_image = inverses[0].reshape(row_count, 1)
    inverse_own = inverses[1:]
    inverse_text = inverse_own.reshape(row_count, 1)
    inverse_near = send(inverse_own, lambda i: i + 2)
    inverse_cross = send(inverse_own, lambda i: i + 1 if i % 2 else i + 3)
    inverse_far = send(inverse_own, lambda i: i + 3 if i % 2 else i + 1)

    def tile(scores, inverse, offset, weight, scale):
        scores = scores * inverse_image * inverse
        logits = scale * scores + logit_bias[0]
        sign = jnp.where(labels[:, None] == offset * row_count + columns, 1.0, -1.0).astype(F32)
        coefficient = (
            (-LOSS_WEIGHT * scale * weight.astype(F32)) * sign * jax.nn.sigmoid(-sign * logits)
        )
        inner = jnp.sum(coefficient * scores, axis=1, keepdims=True)
        return coefficient, (coefficient * inverse).astype(BF16), inner

    mask = pair_mask[0]
    own_scores = own_part + own_there.astype(F32)
    own_coefficient, own_weight, own_inner = tile(
        own_scores, inverse_own, 0, mask[0], logit_scale[0]
    )
    own_pull = dot(own_weight, texts, 1, 0)

    two_part = jnp.concatenate(
        [near_part, dot(projected_b, cross_text, 1, 1)], axis=0
    )
    two_scores = two_part + swap_tensor(two_part.astype(BF16)).astype(F32)
    far_part = dot(projected_b, far_text, 1, 1)
    far_sent = far_part.astype(BF16)
    far_scores = far_part + swap_tensor(far_sent).astype(F32)

    scale_two = logit_scale[0] + nothing(far_sent, far_image, cross_image)
    near_coefficient, near_weight, near_inner = tile(
        two_scores[:row_count], inverse_near, 2, mask[2], scale_two
    )
    cross_coefficient, cross_weight, cross_inner = tile(
        two_scores[row_count:],
        inverse_cross,
        1 + 2 * core,
        jnp.where(first_core, mask[1], mask[3]),
        scale_two,
    )
    some_pull = own_pull + dot(near_weight, near_text, 1, 0) + dot(cross_weight, cross_text, 1, 0)
    scale_far = logit_scale[0] + nothing(some_pull)
    far_coefficient, far_weight, far_inner = tile(
        far_scores, inverse_far, 3 - 2 * core, jnp.where(first_core, mask[3], mask[1]), scale_far
    )
    image_pull = some_pull + dot(far_weight, far_text, 1, 0)
    dot_image = own_inner + near_inner + cross_inner + far_inner
    grad_unit = (
        (image_pull - projected * (inverse_image * dot_image)) * inverse_image
    ).astype(BF16)

    grad_pair = send(grad_unit, other_core)

    def product(left, right, columns_of):
        depth = left[0].shape[-1]
        return sum(
            dot(a.reshape(-1, depth), b[:, columns_of], 1, 0) for a, b in zip(left, right)
        )

    both = (grad_unit, grad_pair)
    part, rest = slice(0, SPLIT), slice(SPLIT, None)
    by_x = [(turned_own[:, d], turned_pair[:, d]) for d in range(XS)]
    by_y = [(turned_own[d], turned_pair[d]) for d in range(YS)]
    sends_a = {d: product(by_x[d], both, part).astype(BF16) for d in (2, 1, 3)}
    send_b = product(by_y[1], both, rest).astype(BF16)
    gots_a = [send(piece, over_x(d)) for d, piece in sends_a.items()]
    got_b = send(send_b, over_y)
    part_a = product(by_x[0], both, part)
    for got in gots_a:
        part_a = part_a + got.astype(F32)
    part_a = part_a.reshape(YS, ZS * unit, -1)
    part_b = (product(by_y[0], both, rest) + got_b.astype(F32)).astype(BF16)
    part_b = part_b.reshape(XS, ZS * unit, -1)
    gots_b = [send(part_b[d], over_x(d)) for d in (2, 1, 3)]
    got_a = send(part_a[1].astype(BF16), over_y)
    last_a = part_a[0] + got_a.astype(F32)
    last_b = part_b[0].astype(F32)
    for got in gots_b:
        last_b = last_b + got.astype(F32)
    last = jnp.concatenate([last_a, last_b], axis=1).astype(BF16).reshape(ZS, unit, -1)
    line = [
        [index_of(y, x, z, c) for z in range(ZS)]
        for y in range(YS)
        for x in range(XS)
        for c in range(CORES)
    ]
    last = lax.all_to_all(last, "dp", 0, 0, axis_index_groups=line, tiled=True)
    grad_head = jnp.sum(last.astype(F32), axis=0)

    zero = nothing(send_b, *sends_a.values()).astype(jnp.int32)
    span = head.shape[0] // 2
    head_here = lax.dynamic_slice_in_dim(head, half * span + zero, span, axis=0)
    head_there = lax.dynamic_slice_in_dim(head, (1 - half) * span + zero, span, axis=0)
    sent = dot(grad_unit, head_there, 1, 1).astype(BF16)
    there = swap_tensor(sent)
    grad_images = (dot(grad_unit, head_here, 1, 1) + there.astype(F32)).astype(BF16)

    inverse_late = inverse_image + nothing(there)
    near_back = send((near_coefficient * inverse_late).astype(BF16), lambda i: i - 2)
    cross_back = send(
        (cross_coefficient * inverse_late).astype(BF16), lambda i: i - 3 if i % 2 else i - 1
    )
    far_back = send(
        (far_coefficient * inverse_late).astype(BF16), lambda i: i - 1 if i % 2 else i - 3
    )
    pulled = (
        dot((own_coefficient * inverse_late).astype(BF16), images, 0, 0)
        + dot(near_back, near_image, 0, 0)
        + dot(cross_back, cross_image, 0, 0)
        + dot(far_back, far_image, 0, 0)
    )
    pulled_high = pulled.astype(BF16)
    pulled_low = (pulled - pulled_high.astype(F32)).astype(BF16)
    text_pull = dot(pulled_high, head, 1, 0) + dot(pulled_low, head, 1, 0)
    unit_text = text_float * inverse_text
    dot_text = jnp.sum(unit_text * text_pull, axis=1)
    dot_text = (dot_text + swap_tensor(dot_text))[:, None]
    grad_texts = ((text_pull - unit_text * dot_text) * inverse_text).astype(BF16)
    return (grad_images, grad_texts, grad_head)


def solution(mesh):
    return jax.shard_map(
        per_device,
        mesh=mesh,
        in_specs=(
            P("dp", None),
            P("dp", "tensor"),
            P(None, "tensor"),
            P("dp", None),
            P("dp"),
            P(),
            P(),
        ),
        out_specs=(P("dp", "tensor"), P("dp", "tensor"), P("dp", "tensor")),
        check_vma=False,
    )
```

```python
import jax
import jax.numpy as jnp
from jax import lax
from jax.experimental import pallas as pl
from jax.experimental.pallas import tpu as pltpu
from jax.sharding import PartitionSpec as P

EPSILON = 1e-06
LOSS_WEIGHT = 16.0
YS, XS, ZS, CORES = 2, 4, 8, 2

F32 = jnp.float32
BF16 = jnp.bfloat16


def place(index):
    return index // (XS * ZS * CORES), index // (ZS * CORES) % XS, index // CORES % ZS, index % CORES


def index_of(y, x, z, core):
    return (((y % YS) * XS + x % XS) * ZS + z % ZS) * CORES + core % CORES


def route(target):
    return [(i, target(i) % (YS * XS * ZS * CORES)) for i in range(YS * XS * ZS * CORES)]


def send(block, target):
    return lax.ppermute(block, "dp", route(target))


def swap_tensor(block):
    return lax.ppermute(block, "tensor", [(0, 1), (1, 0)])


def over_x(distance):
    def target(i):
        y, x, z, core = place(i)
        return index_of(y, x + distance, z, core)

    return target


def over_z(distance):
    def target(i):
        y, x, z, core = place(i)
        return index_of(y, x, z + distance, core)

    return target


def over_y(i):
    y, x, z, core = place(i)
    return index_of(y + 1, x, z, core)


def other_core(i):
    return i ^ 1


def dot(a, b, left, right):
    return lax.dot_general(a, b, (((left,), (right,)), ((), ())), preferred_element_type=F32)


EXTRA = 16


def nothing(*refs):
    pass


def gate(value, *earlier):
    spec = pl.BlockSpec(memory_space=pl.ANY)
    return pl.pallas_call(
        nothing,
        out_shape=jax.ShapeDtypeStruct(value.shape, value.dtype),
        in_specs=[spec] * (1 + len(earlier)),
        out_specs=spec,
        input_output_aliases={0: 0},
    )(value, *earlier)


def call(kernel, outs, ins, operands, grid=None, scratch=(), vmem=24, cost=0):
    shapes = [jax.ShapeDtypeStruct(shape, dtype) for shape, dtype, _ in outs]
    return pl.pallas_call(
        kernel,
        out_shape=shapes,
        grid=grid or (1,),
        in_specs=ins,
        out_specs=[spec for _, _, spec in outs],
        scratch_shapes=list(scratch),
        compiler_params=pltpu.CompilerParams(vmem_limit_bytes=vmem * 1024 * 1024),
        cost_estimate=pl.CostEstimate(flops=cost, bytes_accessed=cost // 512, transcendentals=0),
    )(*operands)


def whole(shape):
    return pl.BlockSpec(shape, lambda j: (0,) * len(shape))


def strip(rows, columns):
    return pl.BlockSpec((rows, columns), lambda j: (0, j))


SCALAR = pl.BlockSpec(memory_space=pltpu.SMEM)
LATER = pl.BlockSpec(memory_space=pl.ANY)


def diagonal(n):
    return lax.broadcasted_iota(jnp.int32, (n, n), 0) == lax.broadcasted_iota(jnp.int32, (n, n), 1)


def to_row(column):
    return jnp.sum(jnp.where(diagonal(column.shape[0]), column, 0.0), axis=0, keepdims=True)


def to_column(row):
    return jnp.sum(jnp.where(diagonal(row.shape[1]), row, 0.0), axis=1, keepdims=True)


def message(part, *rows):
    n = part.shape[1]
    line = lax.broadcasted_iota(jnp.int32, (EXTRA, n), 0)
    extra = jnp.zeros((EXTRA, n), F32)
    for k, row in enumerate(rows):
        high = row.astype(BF16).astype(F32)
        extra = jnp.where(line == 2 * k, high, jnp.where(line == 2 * k + 1, row - high, extra))
    return jnp.concatenate([part.astype(BF16), extra.astype(BF16)], axis=0)


def row_of(extra, k):
    extra = extra.astype(F32)
    return extra[2 * k : 2 * k + 1] + extra[2 * k + 1 : 2 * k + 2]


def square_sum(block):
    block = block.astype(F32)
    return jnp.sum(block * block, axis=1, keepdims=True)


def project_kernel(images, head, texts, projected, projected_b, part, sent, squares, own):
    step = pl.program_id(0)
    product = jnp.dot(images[...], head[...], preferred_element_type=F32)
    projected[...] = product
    rounded = product.astype(BF16)
    projected_b[...] = rounded
    score = dot(rounded, texts[...], 1, 1)
    square_text = square_sum(texts[...])
    square_image = square_sum(product)

    @pl.when(step == 0)
    def _():
        part[...] = score
        own[:, 0:1] = square_text
        own[:, 1:2] = square_image

    @pl.when(step > 0)
    def _():
        part[...] += score
        own[:, 0:1] += square_text
        own[:, 1:2] += square_image

    @pl.when(step == pl.num_programs(0) - 1)
    def _():
        text_row, image_row = to_row(own[:, 0:1]), to_row(own[:, 1:2])
        line = lax.broadcasted_iota(jnp.int32, squares.shape, 0)
        squares[...] = jnp.where(line == 0, text_row, image_row)
        sent[...] = message(part[...], text_row, image_row)


def two_kernel(rounded, near, cross, parts, sent, squares):
    for k, text in enumerate((near, cross)):
        parts[k] = dot(rounded[...], text[...], 1, 1)
        row = to_row(square_sum(text[...]))
        squares[k] = jnp.broadcast_to(row, squares.shape[1:])
        sent[k] = message(parts[k], row)


def far_kernel(core, rounded, first, second, far, part, sent, squares):
    @pl.when(core[0] == 0)
    def _():
        far[...] = first[...]

    @pl.when(core[0] != 0)
    def _():
        far[...] = second[...]

    part[...] = dot(rounded[...], far[...], 1, 1)
    row = to_row(square_sum(far[...]))
    squares[...] = jnp.broadcast_to(row, squares.shape)
    sent[...] = message(part[...], row)


def coefficients(part, there, square_row, inverse_image, labels, offset, mask, scale, bias):
    n = part.shape[0]
    inverse = lax.rsqrt(square_row + row_of(there[n:], 0) + EPSILON)
    scores = (part + there[:n].astype(F32)) * inverse_image * inverse
    logits = scale * scores + bias
    columns = lax.broadcasted_iota(jnp.int32, (n, n), 1) + offset * n
    sign = jnp.where(labels == columns, 1.0, -1.0)
    weight = mask.astype(F32)
    result = (-LOSS_WEIGHT * scale * weight) * sign * jax.nn.sigmoid(-sign * logits)
    inner = jnp.sum(result * scores, axis=1, keepdims=True)
    back = (result * inverse_image).T.astype(BF16)
    return (result * inverse).astype(BF16), inner, back, inverse


def some_kernel(
    core, scale, bias, mask, labels, own_part, own_there, own_squares, parts, theres, squares,
    texts, near, cross, later, pull, backs, inner, inverses, weights,
):
    @pl.when(pl.program_id(0) == 0)
    def _():
        n = own_part.shape[0]
        image_row = own_squares[1:2, :] + row_of(own_there[n:, :], 1)
        inverse_image = to_column(lax.rsqrt(image_row + EPSILON))
        label = to_column(labels[...].astype(F32)).astype(jnp.int32)
        rest = (inverse_image, label)
        total = jnp.zeros((n, 1), F32)
        which = 1 + 2 * core[0]
        tiles = (
            (own_part[...], own_there[...], own_squares[0:1, :], 0),
            (parts[0], theres[0], squares[0][0:1], 2),
            (parts[1], theres[1], squares[1][0:1], which),
        )
        for k, (part, there, row, offset) in enumerate(tiles):
            weight, dots, back, inverse = coefficients(
                part, there, row, *rest, offset, mask[0, offset], scale[0], bias[0]
            )
            weights[k] = weight
            backs[k] = back
            total = total + dots
            if k == 0:
                inverses[:, 1:2] = to_column(inverse)
        inner[...] = total
        inverses[:, 0:1] = inverse_image

    pull[...] = (
        dot(weights[0], texts[...], 1, 0)
        + dot(weights[1], near[...], 1, 0)
        + dot(weights[2], cross[...], 1, 0)
    )


def unit_kernel(
    core, scale, bias, mask, labels, part, there, squares, far, pull, inner, inverses, projected,
    later_a, later_b, unit, back, weight, factor,
):
    @pl.when(pl.program_id(0) == 0)
    def _():
        inverse_image = inverses[:, 0:1]
        label = to_column(labels[...].astype(F32)).astype(jnp.int32)
        offset = 3 - 2 * core[0]
        weights, dots, backs, _ = coefficients(
            part[...], there[...], squares[0:1, :], inverse_image, label, offset,
            mask[0, offset], scale[0], bias[0],
        )
        weight[...] = weights
        back[...] = backs
        factor[...] = inverse_image * (inner[...] + dots)

    total = pull[...] + dot(weight[...], far[...], 1, 0)
    unit[...] = ((total - projected[...] * factor[...]) * inverses[:, 0:1]).astype(BF16)


def turned_kernel(place_ref, images, mine, theirs, turned):
    turned[...] = images[...].astype(F32).T.astype(BF16)
    unit = mine.shape[0] // (YS * XS * ZS)
    core, here_x, here_y = place_ref[0], place_ref[1], place_ref[2]
    for dy in range(YS):
        for dx in range(XS):
            x, y = (here_x + dx) & (XS - 1), (here_y + dy) & (YS - 1)
            for z in range(ZS):
                to = ((dy * XS + dx) * ZS + z) * unit
                block = ((y * XS + x) * ZS + z) * CORES
                for whose, out in ((core, mine), (1 - core, theirs)):
                    start = pl.multiple_of((block + whose) * unit, unit)
                    out[to : to + unit, :] = turned[pl.ds(start, unit), :]


def head_kernel(mine, theirs, own, pair, a1, a2, a3, stay_a, send_b, stay_b):
    product = dot(mine[...], own[...], 1, 0) + dot(theirs[...], pair[...], 1, 0)
    slab = product.shape[0] // (YS * XS)

    @pl.when(pl.program_id(0) < pl.num_programs(0) // 2)
    def _():
        for dx, out in enumerate((stay_a, a1, a2, a3)):
            for dy in range(YS):
                start = (dy * XS + dx) * slab
                out[dy * slab : (dy + 1) * slab, :] = product[start : start + slab].astype(out.dtype)

    @pl.when(pl.program_id(0) >= pl.num_programs(0) // 2)
    def _():
        stay_b[...] = product[: XS * slab]
        send_b[...] = product[XS * slab :].astype(BF16)


def there_kernel(half, unit, head, out):
    out[...] = dot(unit[...], head[...], 1, 1).astype(BF16)


def here_kernel(half, unit, head, there, out):
    out[...] = (dot(unit[...], head[...], 1, 1) + there[...].astype(F32)).astype(BF16)


def relay_kernel(backs, back, later, near, cross, far):
    near[...] = backs[1]
    cross[...] = backs[2]
    far[...] = back[...]


def gather_kernel(backs, near_back, cross_back, far_back, own, near, cross, first, second, high, low):
    total = (
        dot(backs[0], own[...], 1, 0)
        + dot(near_back[...], near[...], 1, 0)
        + dot(cross_back[...], cross[...], 1, 0)
        + dot(far_back[...], first[...], 1, 0)
        + dot(far_back[...], second[...], 1, 0)
    )
    rounded = total.astype(BF16)
    high[...] = rounded
    low[...] = (total - rounded.astype(F32)).astype(BF16)


def pull_kernel(high, low, head, texts, inverses, pull, inner, column):
    step = pl.program_id(0)
    total = dot(high[...], head[...], 1, 0) + dot(low[...], head[...], 1, 0)
    pull[...] = total
    unit = texts[...].astype(F32) * inverses[:, 1:2]
    dots = jnp.sum(unit * total, axis=1, keepdims=True)

    @pl.when(step == 0)
    def _():
        column[...] = dots

    @pl.when(step > 0)
    def _():
        column[...] += dots

    @pl.when(step == pl.num_programs(0) - 1)
    def _():
        inner[...] = to_row(column[...])


def text_kernel(pull, texts, inverses, inner, there, out):
    inverse = inverses[:, 1:2]
    unit = texts[...].astype(F32) * inverse
    out[...] = ((pull[...] - unit * to_column(inner[...] + there[...])) * inverse).astype(BF16)


def per_device(images, texts, head, pair_mask, labels, logit_scale, logit_bias):
    rows, depth = images.shape
    width = texts.shape[1]
    steps = 4
    piece = width // steps
    me = lax.axis_index("dp")
    core = (me & 1)[None]
    where = jnp.stack([me & 1, (me >> 4) & (XS - 1), me >> 6])
    half = lax.axis_index("tensor")[None]
    labels = labels.reshape(1, rows)
    tile, square = (rows + EXTRA, rows), (rows, rows)

    near_text = send(texts, lambda i: i + 2)
    near_image = send(images, lambda i: i - 2)
    count = YS * XS * ZS * CORES
    odd_up = [(i, (i + 1) % count) for i in range(1, count, 2)]
    even_up = [(i, i + 1) for i in range(0, count, 2)]
    odd_down = [(i, i - 1) for i in range(1, count, 2)]
    even_down = [(i, (i - 1) % count) for i in range(0, count, 2)]
    far_second = lax.ppermute(texts, "dp", even_up)
    far_image_second = lax.ppermute(images, "dp", odd_down)

    mine, theirs = call(
        turned_kernel,
        [((depth // CORES, rows), BF16, whole((depth // CORES, rows)))] * 2,
        [SCALAR, whole((rows, depth))],
        (where, images),
        scratch=[pltpu.VMEM((depth, rows), BF16)],
        cost=rows * depth * width,
    )
    theirs = send(theirs, other_core)

    projected, projected_b, own_part, own_sent, own_squares = call(
        project_kernel,
        [
            ((rows, width), F32, strip(rows, piece)),
            ((rows, width), BF16, strip(rows, piece)),
            (square, F32, whole(square)),
            (tile, BF16, whole(tile)),
            ((8, rows), F32, whole((8, rows))),
        ],
        [whole((rows, depth)), strip(depth, piece), strip(rows, piece)],
        (images, head, texts),
        grid=(steps,),
        scratch=[pltpu.VMEM((rows, 128), F32)],
        cost=2 * rows * depth * width,
    )
    own_there = swap_tensor(own_sent)
    far_second = gate(far_second, own_there, theirs, mine, far_image_second)
    near_text = gate(near_text, far_second)

    far_first = lax.ppermute(near_text, "dp", odd_up)
    cross_text = send(near_text, other_core)
    far_image_first = lax.ppermute(near_image, "dp", even_down)
    cross_image = send(near_image, other_core)

    full = whole((rows, width))
    parts, two_sent, two_squares = call(
        two_kernel,
        [
            ((2, *square), F32, whole((2, *square))),
            ((2, *tile), BF16, whole((2, *tile))),
            ((2, 8, rows), F32, whole((2, 8, rows))),
        ],
        [full, full, full],
        (projected_b, near_text, cross_text),
    )
    two_there = swap_tensor(two_sent)
    far_text, far_part, far_sent, far_squares = call(
        far_kernel,
        [
            ((rows, width), BF16, full),
            (square, F32, whole(square)),
            (tile, BF16, whole(tile)),
            ((8, rows), F32, whole((8, rows))),
        ],
        [SCALAR, full, full, full],
        (core, projected_b, far_first, far_second),
    )
    far_there = swap_tensor(far_sent)

    scalars = [SCALAR] * 4
    known = (core, logit_scale, logit_bias, pair_mask, labels)
    some_pull, backs, inner, inverses = call(
        some_kernel,
        [
            ((rows, width), F32, strip(rows, piece)),
            ((3, *square), BF16, whole((3, *square))),
            ((rows, 1), F32, whole((rows, 1))),
            ((rows, 2), F32, whole((rows, 2))),
        ],
        scalars
        + [whole((1, rows)), whole(square), whole(tile), whole((8, rows))]
        + [whole((2, *square)), whole((2, *tile)), whole((2, 8, rows))]
        + [strip(rows, piece)] * 3
        + [LATER],
        known
        + (own_part, own_there, own_squares, parts, two_there, two_squares)
        + (texts, near_text, cross_text, far_sent),
        grid=(steps,),
        scratch=[pltpu.VMEM((3, *square), BF16)],
    )
    grad_unit, far_back = call(
        unit_kernel,
        [((rows, width), BF16, strip(rows, piece)), (square, BF16, whole(square))],
        scalars
        + [whole((1, rows)), whole(square), whole(tile), whole((8, rows))]
        + [strip(rows, piece), strip(rows, piece), whole((rows, 1)), whole((rows, 2))]
        + [strip(rows, piece), LATER, LATER],
        known
        + (far_part, far_there, far_squares, far_text, some_pull, inner, inverses, projected)
        + (far_image_first, cross_image),
        grid=(steps,),
        scratch=[pltpu.VMEM(square, BF16), pltpu.VMEM((rows, 1), F32)],
    )

    grad_pair = send(grad_unit, other_core)
    lines = depth // CORES
    parts_of = 2 * steps
    slab = width // parts_of
    first_half = lambda j: (0, jnp.minimum(j, steps - 1))
    second_half = lambda j: (0, jnp.maximum(j - steps, 0))
    a_spec = pl.BlockSpec((lines // XS, slab), first_half)
    b_spec = pl.BlockSpec((lines // YS, slab), second_half)
    a_shape, b_shape = (lines // XS, width // 2), (lines // YS, width // 2)
    send_1, send_2, send_3, stay_a, send_b, stay_b = call(
        head_kernel,
        [(a_shape, BF16, a_spec)] * 3
        + [(a_shape, F32, a_spec), (b_shape, BF16, b_spec), (b_shape, F32, b_spec)],
        [whole((lines, rows))] * 2 + [strip(rows, slab)] * 2,
        (mine, theirs, grad_unit, grad_pair),
        grid=(parts_of,),
    )
    got_b = send(send_b, over_y)
    gots_a = [send(piece_, over_x(d)) for d, piece_ in ((2, send_2), (1, send_1), (3, send_3))]
    span = depth // 2
    chunk = span // steps

    def image_call(kernel, dtype, other, extra, operands):
        return pl.pallas_call(
            kernel,
            out_shape=jax.ShapeDtypeStruct((rows, span), dtype),
            grid_spec=pltpu.PrefetchScalarGridSpec(
                num_scalar_prefetch=1,
                grid=(steps,),
                in_specs=[
                    pl.BlockSpec((rows, width), lambda j, half: (0, 0)),
                    pl.BlockSpec((chunk, width), lambda j, half: ((half[0] ^ other) * steps + j, 0)),
                ]
                + [pl.BlockSpec((rows, chunk), lambda j, half: (0, j))] * extra,
                out_specs=pl.BlockSpec((rows, chunk), lambda j, half: (0, j)),
            ),
            compiler_params=pltpu.CompilerParams(vmem_limit_bytes=24 * 1024 * 1024),
        )(half, *operands)

    there = swap_tensor(image_call(there_kernel, BF16, 1, 0, (grad_unit, head)))
    grad_images = image_call(here_kernel, BF16, 0, 1, (grad_unit, head, there))

    near_back, cross_back, far_back = call(
        relay_kernel,
        [(square, BF16, whole(square))] * 3,
        [whole((3, *square)), whole(square), LATER],
        (backs, far_back, there),
    )

    gots_a[2] = gate(gots_a[2], grad_images, near_back)
    part_a = stay_a
    for got in gots_a:
        part_a = part_a + got.astype(F32)
    part_a = part_a.reshape(YS, lines // (YS * XS), -1)
    part_b = (stay_b + got_b.astype(F32)).astype(BF16).reshape(XS, lines // (YS * XS), -1)
    gots_b = [send(part_b[d], over_x(d)) for d in (2, 1, 3)]

    near_back = send(near_back, lambda i: i - 2)
    cross_back = send(cross_back, lambda i: i - 3 if i % 2 else i - 1)
    far_back = send(far_back, lambda i: i - 1 if i % 2 else i - 3)
    deep = depth // steps
    high, low = call(
        gather_kernel,
        [((rows, depth), BF16, strip(rows, deep))] * 2,
        [whole((3, *square))] + [whole(square)] * 3 + [strip(rows, deep)] * 5,
        (backs, near_back, cross_back, far_back)
        + (images, near_image, cross_image, far_image_first, far_image_second),
        grid=(steps,),
    )
    text_pull, dot_text = call(
        pull_kernel,
        [((rows, width), F32, strip(rows, piece)), ((1, rows), F32, whole((1, rows)))],
        [whole((rows, depth))] * 2
        + [strip(depth, piece), strip(rows, piece), whole((rows, 2))],
        (high, low, head, texts, inverses),
        grid=(steps,),
        scratch=[pltpu.VMEM((rows, 1), F32)],
    )
    got_a = send(part_a[1].astype(BF16), over_y)
    gots_b[2] = gate(gots_b[2], text_pull)
    last_a = part_a[0] + got_a.astype(F32)
    last_b = part_b[0].astype(F32)
    for got in gots_b:
        last_b = last_b + got.astype(F32)
    last = jnp.concatenate([last_a, last_b], axis=1).astype(BF16)
    last = last.reshape(ZS, lines // (YS * XS * ZS), -1)
    line = [
        [index_of(y, x, z, c) for z in range(ZS)]
        for y in range(YS)
        for x in range(XS)
        for c in range(CORES)
    ]
    last = lax.all_to_all(last, "dp", 0, 0, axis_index_groups=line, tiled=True)
    grad_head = jnp.sum(last.astype(F32), axis=0)

    grad_texts = call(
        text_kernel,
        [((rows, width), BF16, strip(rows, piece))],
        [strip(rows, piece)] * 2 + [whole((rows, 2)), whole((1, rows)), whole((1, rows))],
        (text_pull, texts, inverses, dot_text, swap_tensor(dot_text)),
        grid=(steps,),
    )[0]
    return (grad_images, grad_texts, grad_head)


def solution(mesh):
    return jax.shard_map(
        per_device,
        mesh=mesh,
        in_specs=(
            P("dp", None),
            P("dp", "tensor"),
            P(None, "tensor"),
            P("dp", None),
            P("dp"),
            P(),
            P(),
        ),
        out_specs=(P("dp", "tensor"), P("dp", "tensor"), P("dp", "tensor")),
        check_vma=False,
    )
```

```python
import jax
import jax.numpy as jnp
from jax import lax
from jax.experimental import pallas as pl
from jax.experimental.pallas import tpu as pltpu
from jax.sharding import PartitionSpec as P

EPSILON = 1e-06
LOSS_WEIGHT = 16.0
YS, XS, ZS, CORES = 2, 4, 8, 2

F32 = jnp.float32
BF16 = jnp.bfloat16


def place(index):
    return index // (XS * ZS * CORES), index // (ZS * CORES) % XS, index // CORES % ZS, index % CORES


def index_of(y, x, z, core):
    return (((y % YS) * XS + x % XS) * ZS + z % ZS) * CORES + core % CORES


def route(target):
    return [(i, target(i) % (YS * XS * ZS * CORES)) for i in range(YS * XS * ZS * CORES)]


def send(block, target):
    return lax.ppermute(block, "dp", route(target))


def swap_tensor(block):
    return lax.ppermute(block, "tensor", [(0, 1), (1, 0)])


def over_x(distance):
    def target(i):
        y, x, z, core = place(i)
        return index_of(y, x + distance, z, core)

    return target


def over_z(distance):
    def target(i):
        y, x, z, core = place(i)
        return index_of(y, x, z + distance, core)

    return target


def over_y(i):
    y, x, z, core = place(i)
    return index_of(y + 1, x, z, core)


def other_core(i):
    return i ^ 1


def dot(a, b, left, right):
    return lax.dot_general(a, b, (((left,), (right,)), ((), ())), preferred_element_type=F32)


EXTRA = 16


def nothing(*refs):
    pass


def gate(value, *earlier):
    spec = pl.BlockSpec(memory_space=pl.ANY)
    return pl.pallas_call(
        nothing,
        out_shape=jax.ShapeDtypeStruct(value.shape, value.dtype),
        in_specs=[spec] * (1 + len(earlier)),
        out_specs=spec,
        input_output_aliases={0: 0},
        compiler_params=pltpu.CompilerParams(vmem_limit_bytes=48 * 1024 * 1024),
    )(value, *earlier)


def call(kernel, outs, ins, operands, grid=None, scratch=(), vmem=48, cost=0):
    shapes = [jax.ShapeDtypeStruct(shape, dtype) for shape, dtype, _ in outs]
    return pl.pallas_call(
        kernel,
        out_shape=shapes,
        grid=grid or (1,),
        in_specs=ins,
        out_specs=[spec for _, _, spec in outs],
        scratch_shapes=list(scratch),
        compiler_params=pltpu.CompilerParams(vmem_limit_bytes=vmem * 1024 * 1024),
        cost_estimate=pl.CostEstimate(flops=cost, bytes_accessed=cost // 512, transcendentals=0),
    )(*operands)


def whole(shape):
    return pl.BlockSpec(shape, lambda j: (0,) * len(shape))


def strip(rows, columns):
    return pl.BlockSpec((rows, columns), lambda j: (0, j))


SCALAR = pl.BlockSpec(memory_space=pltpu.SMEM)
LATER = pl.BlockSpec(memory_space=pl.ANY)


def diagonal(n):
    return lax.broadcasted_iota(jnp.int32, (n, n), 0) == lax.broadcasted_iota(jnp.int32, (n, n), 1)


def to_row(column):
    return jnp.sum(jnp.where(diagonal(column.shape[0]), column, 0.0), axis=0, keepdims=True)


def to_column(row):
    return jnp.sum(jnp.where(diagonal(row.shape[1]), row, 0.0), axis=1, keepdims=True)


def message(part, *rows):
    n = part.shape[1]
    line = lax.broadcasted_iota(jnp.int32, (EXTRA, n), 0)
    extra = jnp.zeros((EXTRA, n), F32)
    for k, row in enumerate(rows):
        high = row.astype(BF16).astype(F32)
        extra = jnp.where(line == 2 * k, high, jnp.where(line == 2 * k + 1, row - high, extra))
    return jnp.concatenate([part.astype(BF16), extra.astype(BF16)], axis=0)


def row_of(extra, k):
    extra = extra.astype(F32)
    return extra[2 * k : 2 * k + 1] + extra[2 * k + 1 : 2 * k + 2]


def square_sum(block):
    block = block.astype(F32)
    return jnp.sum(block * block, axis=1, keepdims=True)


def project_kernel(images, head, texts, projected, projected_b, part, sent, squares, own):
    step = pl.program_id(0)
    product = jnp.dot(images[...], head[...], preferred_element_type=F32)
    projected[...] = product
    rounded = product.astype(BF16)
    projected_b[...] = rounded
    score = dot(rounded, texts[...], 1, 1)
    square_text = square_sum(texts[...])
    square_image = square_sum(product)

    @pl.when(step == 0)
    def _():
        part[...] = score
        own[:, 0:1] = square_text
        own[:, 1:2] = square_image

    @pl.when(step > 0)
    def _():
        part[...] += score
        own[:, 0:1] += square_text
        own[:, 1:2] += square_image

    @pl.when(step == pl.num_programs(0) - 1)
    def _():
        text_row, image_row = to_row(own[:, 0:1]), to_row(own[:, 1:2])
        line = lax.broadcasted_iota(jnp.int32, squares.shape, 0)
        squares[...] = jnp.where(line == 0, text_row, image_row)
        sent[...] = message(part[...], text_row, image_row)


def tile_kernel(rounded, text, part, sent, squares):
    part[...] = dot(rounded[...], text[...], 1, 1)
    row = to_row(square_sum(text[...]))
    squares[...] = jnp.broadcast_to(row, squares.shape)
    sent[...] = message(part[...], row)


def far_kernel(core, rounded, first, second, far, part, sent, squares):
    @pl.when(core[0] == 0)
    def _():
        far[...] = first[...]

    @pl.when(core[0] != 0)
    def _():
        far[...] = second[...]

    part[...] = dot(rounded[...], far[...], 1, 1)
    row = to_row(square_sum(far[...]))
    squares[...] = jnp.broadcast_to(row, squares.shape)
    sent[...] = message(part[...], row)


def coefficients(part, there, square_row, inverse_image, labels, offset, mask, scale, bias):
    n = part.shape[0]
    inverse = lax.rsqrt(square_row + row_of(there[n:], 0) + EPSILON)
    scores = (part + there[:n].astype(F32)) * inverse_image * inverse
    logits = scale * scores + bias
    columns = lax.broadcasted_iota(jnp.int32, (n, n), 1) + offset * n
    sign = jnp.where(labels == columns, 1.0, -1.0)
    weight = mask.astype(F32)
    result = (-LOSS_WEIGHT * scale * weight) * sign * jax.nn.sigmoid(-sign * logits)
    inner = jnp.sum(result * scores, axis=1, keepdims=True)
    back = (result * inverse_image).T.astype(BF16)
    return (result * inverse).astype(BF16), inner, back, inverse


def some_kernel(
    core, scale, bias, mask, labels, own_part, own_there, own_squares,
    near_part, near_there, near_squares, cross_part, cross_there, cross_squares,
    texts, near, cross, later, pull, backs, inner, inverses, weights,
):
    @pl.when(pl.program_id(0) == 0)
    def _():
        n = own_part.shape[0]
        image_row = own_squares[1:2, :] + row_of(own_there[n:, :], 1)
        inverse_image = to_column(lax.rsqrt(image_row + EPSILON))
        label = to_column(labels[...].astype(F32)).astype(jnp.int32)
        rest = (inverse_image, label)
        total = jnp.zeros((n, 1), F32)
        which = 1 + 2 * core[0]
        tiles = (
            (own_part[...], own_there[...], own_squares[0:1, :], 0),
            (near_part[...], near_there[...], near_squares[0:1, :], 2),
            (cross_part[...], cross_there[...], cross_squares[0:1, :], which),
        )
        for k, (part, there, row, offset) in enumerate(tiles):
            weight, dots, back, inverse = coefficients(
                part, there, row, *rest, offset, mask[0, offset], scale[0], bias[0]
            )
            weights[k] = weight
            backs[k] = back
            total = total + dots
            if k == 0:
                inverses[:, 1:2] = to_column(inverse)
        inner[...] = total
        inverses[:, 0:1] = inverse_image

    pull[...] = (
        dot(weights[0], texts[...], 1, 0)
        + dot(weights[1], near[...], 1, 0)
        + dot(weights[2], cross[...], 1, 0)
    )


def unit_kernel(
    core, scale, bias, mask, labels, part, there, squares, far, pull, inner, inverses, projected,
    later_a, later_b, unit, back, weight, factor,
):
    @pl.when(pl.program_id(0) == 0)
    def _():
        inverse_image = inverses[:, 0:1]
        label = to_column(labels[...].astype(F32)).astype(jnp.int32)
        offset = 3 - 2 * core[0]
        weights, dots, backs, _ = coefficients(
            part[...], there[...], squares[0:1, :], inverse_image, label, offset,
            mask[0, offset], scale[0], bias[0],
        )
        weight[...] = weights
        back[...] = backs
        factor[...] = inverse_image * (inner[...] + dots)

    total = pull[...] + dot(weight[...], far[...], 1, 0)
    unit[...] = ((total - projected[...] * factor[...]) * inverses[:, 0:1]).astype(BF16)


def turned_kernel(place_ref, images, mine, theirs, turned):
    turned[...] = images[...].astype(F32).T.astype(BF16)
    unit = mine.shape[0] // (YS * XS * ZS)
    core, here_x, here_y = place_ref[0], place_ref[1], place_ref[2]
    for dy in range(YS):
        for dx in range(XS):
            x, y = (here_x + dx) & (XS - 1), (here_y + dy) & (YS - 1)
            for z in range(ZS):
                to = ((dy * XS + dx) * ZS + z) * unit
                block = ((y * XS + x) * ZS + z) * CORES
                for whose, out in ((core, mine), (1 - core, theirs)):
                    start = pl.multiple_of((block + whose) * unit, unit)
                    out[to : to + unit, :] = turned[pl.ds(start, unit), :]


def send_kernel(mine, theirs, own, pair, a1, a2, a3, send_b):
    slab = mine.shape[0] // (YS * XS)

    def product(start, stop):
        low, high = start * slab, stop * slab
        return dot(mine[low:high, :], own[...], 1, 0) + dot(theirs[low:high, :], pair[...], 1, 0)

    @pl.when(pl.program_id(0) < pl.num_programs(0) // 2)
    def _():
        for dy in range(YS):
            total = product(dy * XS + 1, dy * XS + XS).astype(BF16)
            for k, out in enumerate((a1, a2, a3)):
                out[dy * slab : (dy + 1) * slab, :] = total[k * slab : (k + 1) * slab]

    @pl.when(pl.program_id(0) >= pl.num_programs(0) // 2)
    def _():
        send_b[...] = product(XS, 2 * XS).astype(BF16)


def sum_a_kernel(mine, theirs, own, pair, g1, g2, g3, keep, sent):
    slab = mine.shape[0] // (YS * XS)
    for dy in range(YS):
        rows = slice(dy * XS * slab, (dy * XS + 1) * slab)
        total = dot(mine[rows, :], own[...], 1, 0) + dot(theirs[rows, :], pair[...], 1, 0)
        for got in (g1, g2, g3):
            total = total + got[dy * slab : (dy + 1) * slab, :].astype(F32)
        if dy == 0:
            keep[...] = total
        else:
            sent[...] = total.astype(BF16)


def sum_b_kernel(mine, theirs, own, pair, got, later, keep, s1, s2, s3):
    slab = mine.shape[0] // (YS * XS)
    rows = slice(0, XS * slab)
    total = dot(mine[rows, :], own[...], 1, 0) + dot(theirs[rows, :], pair[...], 1, 0)
    total = total + got[...].astype(F32)
    keep[...] = total[:slab]
    for k, out in enumerate((s1, s2, s3)):
        out[...] = total[(k + 1) * slab : (k + 2) * slab].astype(BF16)


def last_kernel(keep_a, got_a, keep_b, g1, g2, g3, out):
    middle = keep_a.shape[1]
    out[:, :middle] = (keep_a[...] + got_a[...].astype(F32)).astype(BF16)
    total = keep_b[...]
    for got in (g1, g2, g3):
        total = total + got[...].astype(F32)
    out[:, middle:] = total.astype(BF16)


def line_kernel(blocks, out):
    total = blocks[0].astype(F32)
    for k in range(1, blocks.shape[0]):
        total = total + blocks[k].astype(F32)
    out[...] = total


def there_kernel(half, unit, head, later, out):
    out[...] = dot(unit[...], head[...], 1, 1).astype(BF16)


def here_kernel(half, unit, head, there, out):
    out[...] = (dot(unit[...], head[...], 1, 1) + there[...].astype(F32)).astype(BF16)


def relay_kernel(backs, back, later, near, cross, far):
    near[...] = backs[1]
    cross[...] = backs[2]
    far[...] = back[...]


def gather_kernel(backs, near_back, cross_back, far_back, own, near, cross, first, second, high, low):
    total = (
        dot(backs[0], own[...], 1, 0)
        + dot(near_back[...], near[...], 1, 0)
        + dot(cross_back[...], cross[...], 1, 0)
        + dot(far_back[...], first[...], 1, 0)
        + dot(far_back[...], second[...], 1, 0)
    )
    rounded = total.astype(BF16)
    high[...] = rounded
    low[...] = (total - rounded.astype(F32)).astype(BF16)


def pull_kernel(high, low, head, texts, inverses, pull, inner, column):
    step = pl.program_id(0)
    total = dot(high[...], head[...], 1, 0) + dot(low[...], head[...], 1, 0)
    pull[...] = total
    unit = texts[...].astype(F32) * inverses[:, 1:2]
    dots = jnp.sum(unit * total, axis=1, keepdims=True)

    @pl.when(step == 0)
    def _():
        column[...] = dots

    @pl.when(step > 0)
    def _():
        column[...] += dots

    @pl.when(step == pl.num_programs(0) - 1)
    def _():
        inner[...] = to_row(column[...])


def text_kernel(pull, texts, inverses, inner, there, out):
    inverse = inverses[:, 1:2]
    unit = texts[...].astype(F32) * inverse
    out[...] = ((pull[...] - unit * to_column(inner[...] + there[...])) * inverse).astype(BF16)


def per_device(images, texts, head, pair_mask, labels, logit_scale, logit_bias):
    rows, depth = images.shape
    width = texts.shape[1]
    steps = 4
    piece = width // steps
    me = lax.axis_index("dp")
    core = (me & 1)[None]
    where = jnp.stack([me & 1, (me >> 4) & (XS - 1), me >> 6])
    half = lax.axis_index("tensor")[None]
    labels = labels.reshape(1, rows)
    tile, square = (rows + EXTRA, rows), (rows, rows)

    near_text = send(texts, lambda i: i + 2)
    near_image = send(images, lambda i: i - 2)
    count = YS * XS * ZS * CORES
    odd_up = [(i, (i + 1) % count) for i in range(1, count, 2)]
    even_up = [(i, i + 1) for i in range(0, count, 2)]
    odd_down = [(i, i - 1) for i in range(1, count, 2)]
    even_down = [(i, (i - 1) % count) for i in range(0, count, 2)]
    far_second = lax.ppermute(texts, "dp", even_up)
    far_image_second = lax.ppermute(images, "dp", odd_down)

    mine, theirs = call(
        turned_kernel,
        [((depth // CORES, rows), BF16, whole((depth // CORES, rows)))] * 2,
        [SCALAR, whole((rows, depth))],
        (where, images),
        scratch=[pltpu.VMEM((depth, rows), BF16)],
        cost=rows * depth * width,
    )
    theirs = send(theirs, other_core)

    projected, projected_b, own_part, own_sent, own_squares = call(
        project_kernel,
        [
            ((rows, width), F32, strip(rows, piece)),
            ((rows, width), BF16, strip(rows, piece)),
            (square, F32, whole(square)),
            (tile, BF16, whole(tile)),
            ((8, rows), F32, whole((8, rows))),
        ],
        [whole((rows, depth)), strip(depth, piece), strip(rows, piece)],
        (images, head, texts),
        grid=(steps,),
        scratch=[pltpu.VMEM((rows, 128), F32)],
        cost=2 * rows * depth * width,
    )
    own_there = swap_tensor(own_sent)
    far_second = gate(far_second, own_sent, theirs, mine, far_image_second)
    near_text = gate(near_text, far_second)

    far_first = lax.ppermute(near_text, "dp", odd_up)
    cross_text = send(near_text, other_core)
    near_image = gate(near_image, own_there)
    far_image_first = lax.ppermute(near_image, "dp", even_down)
    cross_image = send(near_image, other_core)

    full = whole((rows, width))
    tile_outs = [
        (square, F32, whole(square)),
        (tile, BF16, whole(tile)),
        ((8, rows), F32, whole((8, rows))),
    ]
    near_part, near_sent, near_squares = call(
        tile_kernel, tile_outs, [full, full], (projected_b, near_text)
    )
    near_there = swap_tensor(near_sent)
    cross_part, cross_sent, cross_squares = call(
        tile_kernel, tile_outs, [full, full], (projected_b, cross_text)
    )
    cross_there = swap_tensor(cross_sent)
    far_text, far_part, far_sent, far_squares = call(
        far_kernel,
        [((rows, width), BF16, full)] + tile_outs,
        [SCALAR, full, full, full],
        (core, projected_b, far_first, far_second),
    )
    far_there = swap_tensor(far_sent)

    scalars = [SCALAR] * 4
    known = (core, logit_scale, logit_bias, pair_mask, labels)
    some_pull, backs, inner, inverses = call(
        some_kernel,
        [
            ((rows, width), F32, strip(rows, piece)),
            ((3, *square), BF16, whole((3, *square))),
            ((rows, 1), F32, whole((rows, 1))),
            ((rows, 2), F32, whole((rows, 2))),
        ],
        scalars
        + [whole((1, rows))]
        + [whole(square), whole(tile), whole((8, rows))] * 3
        + [strip(rows, piece)] * 3
        + [LATER],
        known
        + (own_part, own_there, own_squares, near_part, near_there, near_squares)
        + (cross_part, cross_there, cross_squares)
        + (texts, near_text, cross_text, far_sent),
        grid=(steps,),
        scratch=[pltpu.VMEM((3, *square), BF16)],
    )
    grad_unit, far_back = call(
        unit_kernel,
        [((rows, width), BF16, strip(rows, piece)), (square, BF16, whole(square))],
        scalars
        + [whole((1, rows)), whole(square), whole(tile), whole((8, rows))]
        + [strip(rows, piece), strip(rows, piece), whole((rows, 1)), whole((rows, 2))]
        + [strip(rows, piece), LATER, LATER],
        known
        + (far_part, far_there, far_squares, far_text, some_pull, inner, inverses, projected)
        + (far_image_first, cross_image),
        grid=(steps,),
        scratch=[pltpu.VMEM(square, BF16), pltpu.VMEM((rows, 1), F32)],
    )

    grad_pair = send(grad_unit, other_core)
    lines = depth // CORES
    parts_of = 2 * steps
    slab = width // parts_of
    first_half = lambda j: (0, jnp.minimum(j, steps - 1))
    second_half = lambda j: (0, jnp.maximum(j - steps, 0))
    a_spec = pl.BlockSpec((lines // XS, slab), first_half)
    b_spec = pl.BlockSpec((lines // YS, slab), second_half)
    a_shape, b_shape = (lines // XS, width // 2), (lines // YS, width // 2)
    sides = (mine, theirs, grad_unit, grad_pair)
    side_specs = [whole((lines, rows))] * 2
    send_1, send_2, send_3, send_b = call(
        send_kernel,
        [(a_shape, BF16, a_spec)] * 3 + [(b_shape, BF16, b_spec)],
        side_specs + [strip(rows, slab)] * 2,
        sides,
        grid=(parts_of,),
    )
    got_b = send(send_b, over_y)
    gots_a = [send(block, over_x(d)) for d, block in ((2, send_2), (1, send_1), (3, send_3))]

    span = depth // 2
    chunk = span // steps

    def image_call(kernel, dtype, other, extra, operands):
        return pl.pallas_call(
            kernel,
            out_shape=jax.ShapeDtypeStruct((rows, span), dtype),
            grid_spec=pltpu.PrefetchScalarGridSpec(
                num_scalar_prefetch=1,
                grid=(steps,),
                in_specs=[
                    pl.BlockSpec((rows, width), lambda j, half: (0, 0)),
                    pl.BlockSpec((chunk, width), lambda j, half: ((half[0] ^ other) * steps + j, 0)),
                ]
                + extra,
                out_specs=pl.BlockSpec((rows, chunk), lambda j, half: (0, j)),
            ),
            compiler_params=pltpu.CompilerParams(vmem_limit_bytes=48 * 1024 * 1024),
        )(half, *operands)

    there = image_call(there_kernel, BF16, 1, [LATER], (grad_unit, head, send_b))

    near_back, cross_back, far_back = call(
        relay_kernel,
        [(square, BF16, whole(square))] * 3,
        [whole((3, *square)), whole(square), LATER],
        (backs, far_back, send_b),
    )

    near_back = send(near_back, lambda i: i - 2)
    cross_back = send(cross_back, lambda i: i - 3 if i % 2 else i - 1)
    far_back = send(far_back, lambda i: i - 1 if i % 2 else i - 3)
    deep = depth // steps
    high, low = call(
        gather_kernel,
        [((rows, depth), BF16, strip(rows, deep))] * 2,
        [whole((3, *square))] + [whole(square)] * 3 + [strip(rows, deep)] * 5,
        (backs, near_back, cross_back, far_back)
        + (images, near_image, cross_image, far_image_first, far_image_second),
        grid=(steps,),
    )
    gots_a[2] = gate(gots_a[2], high)
    short = lines // (YS * XS)
    keep_shape, keep_spec = (short, width // 2), strip(short, slab)
    keep_a, sent_a = call(
        sum_a_kernel,
        [(keep_shape, F32, keep_spec), (keep_shape, BF16, keep_spec)],
        side_specs + [strip(rows, slab)] * 2 + [strip(lines // XS, slab)] * 3,
        (*sides, *gots_a),
        grid=(steps,),
    )
    got_a = send(sent_a, over_y)
    second = pl.BlockSpec((rows, slab), lambda j: (0, j + steps))
    keep_b, *sends_b = call(
        sum_b_kernel,
        [(keep_shape, F32, keep_spec)] + [(keep_shape, BF16, keep_spec)] * 3,
        side_specs + [second] * 2 + [strip(lines // YS, slab), LATER],
        (*sides, got_b, sent_a),
        grid=(steps,),
    )
    gots_b = [send(sends_b[d - 1], over_x(d)) for d in (2, 1, 3)]
    there = swap_tensor(gate(there, keep_b))
    text_pull, dot_text = call(
        pull_kernel,
        [((rows, width), F32, strip(rows, piece)), ((1, rows), F32, whole((1, rows)))],
        [whole((rows, depth))] * 2
        + [strip(depth, piece), strip(rows, piece), whole((rows, 2))],
        (high, low, head, texts, inverses),
        grid=(steps,),
        scratch=[pltpu.VMEM((rows, 1), F32)],
    )
    dot_there = swap_tensor(dot_text)
    gots_b[2] = gate(gots_b[2], text_pull)
    last = call(
        last_kernel,
        [((short, width), BF16, whole((short, width)))],
        [whole(keep_shape)] * 6,
        (keep_a, got_a, keep_b, *gots_b),
    )[0]
    last = gate(last, there, dot_there).reshape(ZS, short // ZS, width)
    line = [
        [index_of(y, x, z, c) for z in range(ZS)]
        for y in range(YS)
        for x in range(XS)
        for c in range(CORES)
    ]
    last = lax.all_to_all(last, "dp", 0, 0, axis_index_groups=line, tiled=True)
    grad_head = call(
        line_kernel,
        [((short // ZS, width), F32, whole((short // ZS, width)))],
        [whole(last.shape)],
        (last,),
    )[0]
    piece_spec = pl.BlockSpec((rows, chunk), lambda j, half: (0, j))
    grad_images = image_call(here_kernel, BF16, 0, [piece_spec], (grad_unit, head, there))

    grad_texts = call(
        text_kernel,
        [((rows, width), BF16, strip(rows, piece))],
        [strip(rows, piece)] * 2 + [whole((rows, 2)), whole((1, rows)), whole((1, rows))],
        (text_pull, texts, inverses, dot_text, dot_there),
        grid=(steps,),
    )[0]
    return (grad_images, grad_texts, grad_head)


def solution(mesh):
    return jax.shard_map(
        per_device,
        mesh=mesh,
        in_specs=(
            P("dp", None),
            P("dp", "tensor"),
            P(None, "tensor"),
            P("dp", None),
            P("dp"),
            P(),
            P(),
        ),
        out_specs=(P("dp", "tensor"), P("dp", "tensor"), P("dp", "tensor")),
        check_vma=False,
    )
```

```python
import jax
import jax.numpy as jnp
from jax import lax
from jax.experimental import pallas as pl
from jax.experimental.pallas import tpu as pltpu
from jax.sharding import PartitionSpec as P

EPSILON = 1e-06
LOSS_WEIGHT = 16.0
YS, XS, ZS, CORES = 2, 4, 8, 2

F32 = jnp.float32
BF16 = jnp.bfloat16


def place(index):
    return index // (XS * ZS * CORES), index // (ZS * CORES) % XS, index // CORES % ZS, index % CORES


def index_of(y, x, z, core):
    return (((y % YS) * XS + x % XS) * ZS + z % ZS) * CORES + core % CORES


def route(target):
    return [(i, target(i) % (YS * XS * ZS * CORES)) for i in range(YS * XS * ZS * CORES)]


def send(block, target):
    return lax.ppermute(block, "dp", route(target))


def swap_tensor(block):
    return lax.ppermute(block, "tensor", [(0, 1), (1, 0)])


def over_x(distance):
    def target(i):
        y, x, z, core = place(i)
        return index_of(y, x + distance, z, core)

    return target


def over_z(distance):
    def target(i):
        y, x, z, core = place(i)
        return index_of(y, x, z + distance, core)

    return target


def over_y(i):
    y, x, z, core = place(i)
    return index_of(y + 1, x, z, core)


def other_core(i):
    return i ^ 1


def dot(a, b, left, right):
    return lax.dot_general(a, b, (((left,), (right,)), ((), ())), preferred_element_type=F32)


EXTRA = 16


def nothing(*refs):
    pass


def gate(value, *earlier):
    spec = pl.BlockSpec(memory_space=pl.ANY)
    return pl.pallas_call(
        nothing,
        out_shape=jax.ShapeDtypeStruct(value.shape, value.dtype),
        in_specs=[spec] * (1 + len(earlier)),
        out_specs=spec,
        input_output_aliases={0: 0},
        compiler_params=pltpu.CompilerParams(vmem_limit_bytes=48 * 1024 * 1024),
    )(value, *earlier)


def call(kernel, outs, ins, operands, grid=None, scratch=(), vmem=48, cost=0):
    shapes = [jax.ShapeDtypeStruct(shape, dtype) for shape, dtype, _ in outs]
    return pl.pallas_call(
        kernel,
        out_shape=shapes,
        grid=grid or (1,),
        in_specs=ins,
        out_specs=[spec for _, _, spec in outs],
        scratch_shapes=list(scratch),
        compiler_params=pltpu.CompilerParams(vmem_limit_bytes=vmem * 1024 * 1024),
        cost_estimate=pl.CostEstimate(flops=cost, bytes_accessed=cost // 512, transcendentals=0),
    )(*operands)


def whole(shape):
    return pl.BlockSpec(shape, lambda j: (0,) * len(shape))


def strip(rows, columns):
    return pl.BlockSpec((rows, columns), lambda j: (0, j))


SCALAR = pl.BlockSpec(memory_space=pltpu.SMEM)
LATER = pl.BlockSpec(memory_space=pl.ANY)


def diagonal(n):
    return lax.broadcasted_iota(jnp.int32, (n, n), 0) == lax.broadcasted_iota(jnp.int32, (n, n), 1)


def to_row(column):
    return jnp.sum(jnp.where(diagonal(column.shape[0]), column, 0.0), axis=0, keepdims=True)


def to_column(row):
    return jnp.sum(jnp.where(diagonal(row.shape[1]), row, 0.0), axis=1, keepdims=True)


def message(part, *rows):
    n = part.shape[1]
    line = lax.broadcasted_iota(jnp.int32, (EXTRA, n), 0)
    extra = jnp.zeros((EXTRA, n), F32)
    for k, row in enumerate(rows):
        high = row.astype(BF16).astype(F32)
        extra = jnp.where(line == 2 * k, high, jnp.where(line == 2 * k + 1, row - high, extra))
    return jnp.concatenate([part.astype(BF16), extra.astype(BF16)], axis=0)


def row_of(extra, k):
    extra = extra.astype(F32)
    return extra[2 * k : 2 * k + 1] + extra[2 * k + 1 : 2 * k + 2]


def square_sum(block):
    block = block.astype(F32)
    return jnp.sum(block * block, axis=1, keepdims=True)


def project_kernel(images, head, texts, projected, projected_b, part, sent, squares, own):
    step = pl.program_id(0)
    product = jnp.dot(images[...], head[...], preferred_element_type=F32)
    projected[...] = product
    rounded = product.astype(BF16)
    projected_b[...] = rounded
    score = dot(rounded, texts[...], 1, 1)
    square_text = square_sum(texts[...])
    square_image = square_sum(product)

    @pl.when(step == 0)
    def _():
        part[...] = score
        own[:, 0:1] = square_text
        own[:, 1:2] = square_image

    @pl.when(step > 0)
    def _():
        part[...] += score
        own[:, 0:1] += square_text
        own[:, 1:2] += square_image

    @pl.when(step == pl.num_programs(0) - 1)
    def _():
        text_row, image_row = to_row(own[:, 0:1]), to_row(own[:, 1:2])
        line = lax.broadcasted_iota(jnp.int32, squares.shape, 0)
        squares[...] = jnp.where(line == 0, text_row, image_row)
        sent[...] = message(part[...], text_row, image_row)


def tile_kernel(rounded, text, part, sent, squares):
    part[...] = dot(rounded[...], text[...], 1, 1)
    row = to_row(square_sum(text[...]))
    squares[...] = jnp.broadcast_to(row, squares.shape)
    sent[...] = message(part[...], row)


def near_kernel(rounded, text, before, part, sent, squares):
    part[...] = dot(rounded[...], text[...], 1, 1)
    row = to_row(square_sum(text[...]))
    squares[...] = jnp.broadcast_to(row, squares.shape)
    sent[0] = before[...]
    sent[1] = message(part[...], row)


def far_kernel(core, rounded, first, second, far, part, sent, squares):
    @pl.when(core[0] == 0)
    def _():
        far[...] = first[...]

    @pl.when(core[0] != 0)
    def _():
        far[...] = second[...]

    part[...] = dot(rounded[...], far[...], 1, 1)
    row = to_row(square_sum(far[...]))
    squares[...] = jnp.broadcast_to(row, squares.shape)
    sent[...] = message(part[...], row)


def coefficients(part, there, square_row, inverse_image, labels, offset, mask, scale, bias):
    n = part.shape[0]
    inverse = lax.rsqrt(square_row + row_of(there[n:], 0) + EPSILON)
    scores = (part + there[:n].astype(F32)) * inverse_image * inverse
    logits = scale * scores + bias
    columns = lax.broadcasted_iota(jnp.int32, (n, n), 1) + offset * n
    sign = jnp.where(labels == columns, 1.0, -1.0)
    weight = mask.astype(F32)
    result = (-LOSS_WEIGHT * scale * weight) * sign * jax.nn.sigmoid(-sign * logits)
    inner = jnp.sum(result * scores, axis=1, keepdims=True)
    back = result * inverse_image
    return (result * inverse).astype(BF16), inner, back, inverse


def some_kernel(
    core, scale, bias, mask, labels, own_part, own_squares, near_part, near_there, near_squares,
    cross_part, cross_there, cross_squares, texts, near, cross, later,
    pull, own_back, near_back, cross_back, inner, inverses, weights,
):
    @pl.when(pl.program_id(0) == 0)
    def _():
        n = own_part.shape[0]
        image_row = own_squares[1:2, :] + row_of(near_there[0][n:], 1)
        inverse_image = to_column(lax.rsqrt(image_row + EPSILON))
        label = to_column(labels[...].astype(F32)).astype(jnp.int32)
        rest = (inverse_image, label)
        total = jnp.zeros((n, 1), F32)
        which = 1 + 2 * core[0]
        tiles = (
            (own_part[...], near_there[0], own_squares[0:1, :], 0, own_back),
            (near_part[...], near_there[1], near_squares[0:1, :], 2, near_back),
            (cross_part[...], cross_there[...], cross_squares[0:1, :], which, cross_back),
        )
        for k, (part, there, row, offset, out) in enumerate(tiles):
            weight, dots, back, inverse = coefficients(
                part, there, row, *rest, offset, mask[0, offset], scale[0], bias[0]
            )
            weights[k] = weight
            out[...] = back.T.astype(BF16)
            total = total + dots
            if k == 0:
                inverses[:, 1:2] = to_column(inverse)
        inner[...] = total
        inverses[:, 0:1] = inverse_image

    pull[...] = (
        dot(weights[0], texts[...], 1, 0)
        + dot(weights[1], near[...], 1, 0)
        + dot(weights[2], cross[...], 1, 0)
    )


def unit_kernel(
    core, scale, bias, mask, labels, part, there, squares, far, pull, inner, inverses, projected,
    later_a, later_b, unit, back, weight, factor,
):
    @pl.when(pl.program_id(0) == 0)
    def _():
        inverse_image = inverses[:, 0:1]
        label = to_column(labels[...].astype(F32)).astype(jnp.int32)
        offset = 3 - 2 * core[0]
        weights, dots, backs, _ = coefficients(
            part[...], there[...], squares[0:1, :], inverse_image, label, offset,
            mask[0, offset], scale[0], bias[0],
        )
        weight[...] = weights
        back[...] = backs.astype(BF16)
        factor[...] = inverse_image * (inner[...] + dots)

    total = pull[...] + dot(weight[...], far[...], 1, 0)
    unit[...] = ((total - projected[...] * factor[...]) * inverses[:, 0:1]).astype(BF16)


def turned_kernel(place_ref, images, mine, theirs, turned):
    turned[...] = images[...].astype(F32).T.astype(BF16)
    unit = mine.shape[0] // (YS * XS * ZS)
    core, here_x, here_y = place_ref[0], place_ref[1], place_ref[2]
    for dy in range(YS):
        for dx in range(XS):
            x, y = (here_x + dx) & (XS - 1), (here_y + dy) & (YS - 1)
            for z in range(ZS):
                to = ((dy * XS + dx) * ZS + z) * unit
                block = ((y * XS + x) * ZS + z) * CORES
                for whose, out in ((core, mine), (1 - core, theirs)):
                    start = pl.multiple_of((block + whose) * unit, unit)
                    out[to : to + unit, :] = turned[pl.ds(start, unit), :]


def send_kernel(mine, theirs, own, pair, a1, a2, a3, send_b, left, right):
    slab = mine.shape[0] // (YS * XS)
    many = (XS - 1) * slab

    @pl.when(pl.program_id(0) == 0)
    def _():
        for dy in range(YS):
            rows = slice((dy * XS + 1) * slab, (dy * XS + XS) * slab)
            left[dy * many : (dy + 1) * many, :] = mine[rows, :]
            right[dy * many : (dy + 1) * many, :] = theirs[rows, :]

    @pl.when(pl.program_id(0) < pl.num_programs(0) // 2)
    def _():
        total = dot(left[...], own[...], 1, 0) + dot(right[...], pair[...], 1, 0)
        total = total.astype(BF16)
        for dy in range(YS):
            for k, out in enumerate((a1, a2, a3)):
                start = dy * many + k * slab
                out[dy * slab : (dy + 1) * slab, :] = total[start : start + slab]

    @pl.when(pl.program_id(0) >= pl.num_programs(0) // 2)
    def _():
        rows = slice(XS * slab, 2 * XS * slab)
        total = dot(mine[rows, :], own[...], 1, 0) + dot(theirs[rows, :], pair[...], 1, 0)
        send_b[...] = total.astype(BF16)


def sum_a_kernel(mine, theirs, own, pair, g1, g2, g3, keep, sent):
    slab = mine.shape[0] // (YS * XS)
    for dy in range(YS):
        rows = slice(dy * XS * slab, (dy * XS + 1) * slab)
        total = dot(mine[rows, :], own[...], 1, 0) + dot(theirs[rows, :], pair[...], 1, 0)
        for got in (g1, g2, g3):
            total = total + got[dy * slab : (dy + 1) * slab, :].astype(F32)
        if dy == 0:
            keep[...] = total
        else:
            sent[...] = total.astype(BF16)


def sum_b_kernel(mine, theirs, own, pair, got, later, keep, s1, s2, s3):
    slab = mine.shape[0] // (YS * XS)
    rows = slice(0, XS * slab)
    total = dot(mine[rows, :], own[...], 1, 0) + dot(theirs[rows, :], pair[...], 1, 0)
    total = total + got[...].astype(F32)
    keep[...] = total[:slab]
    for k, out in enumerate((s1, s2, s3)):
        out[...] = total[(k + 1) * slab : (k + 2) * slab].astype(BF16)


def last_kernel(keep_a, got_a, keep_b, g1, g2, g3, out):
    middle = keep_a.shape[1]
    out[:, :middle] = (keep_a[...] + got_a[...].astype(F32)).astype(BF16)
    total = keep_b[...]
    for got in (g1, g2, g3):
        total = total + got[...].astype(F32)
    out[:, middle:] = total.astype(BF16)


def line_kernel(blocks, out):
    total = blocks[0].astype(F32)
    for k in range(1, blocks.shape[0]):
        total = total + blocks[k].astype(F32)
    out[...] = total


def there_kernel(half, unit, head, later, out):
    out[...] = dot(unit[...], head[...], 1, 1).astype(BF16)


def here_kernel(half, unit, head, there, out):
    out[...] = (dot(unit[...], head[...], 1, 1) + there[...].astype(F32)).astype(BF16)


def gather_kernel(
    own_back, near_back, cross_back, far_back, own, near, cross, first, second, high, low
):
    far_turned = far_back[...].astype(F32).T.astype(BF16)
    total = (
        dot(own_back[...], own[...], 1, 0)
        + dot(near_back[...], near[...], 1, 0)
        + dot(cross_back[...], cross[...], 1, 0)
        + dot(far_turned, first[...], 1, 0)
        + dot(far_turned, second[...], 1, 0)
    )
    rounded = total.astype(BF16)
    high[...] = rounded
    low[...] = (total - rounded.astype(F32)).astype(BF16)


def pull_kernel(high, low, head, texts, inverses, pull, inner, column):
    step = pl.program_id(0)
    total = dot(high[...], head[...], 1, 0) + dot(low[...], head[...], 1, 0)
    pull[...] = total
    unit = texts[...].astype(F32) * inverses[:, 1:2]
    dots = jnp.sum(unit * total, axis=1, keepdims=True)

    @pl.when(step == 0)
    def _():
        column[...] = dots

    @pl.when(step > 0)
    def _():
        column[...] += dots

    @pl.when(step == pl.num_programs(0) - 1)
    def _():
        inner[...] = to_row(column[...])


def text_kernel(pull, texts, inverses, inner, there, out):
    inverse = inverses[:, 1:2]
    unit = texts[...].astype(F32) * inverse
    out[...] = ((pull[...] - unit * to_column(inner[...] + there[...])) * inverse).astype(BF16)


def per_device(images, texts, head, pair_mask, labels, logit_scale, logit_bias):
    rows, depth = images.shape
    width = texts.shape[1]
    steps = 4
    piece = width // steps
    me = lax.axis_index("dp")
    core = (me & 1)[None]
    where = jnp.stack([me & 1, (me >> 4) & (XS - 1), me >> 6])
    half = lax.axis_index("tensor")[None]
    labels = labels.reshape(1, rows)
    tile, square = (rows + EXTRA, rows), (rows, rows)

    near_text = send(texts, lambda i: i + 2)
    near_image = send(images, lambda i: i - 2)
    count = YS * XS * ZS * CORES
    odd_up = [(i, (i + 1) % count) for i in range(1, count, 2)]
    even_up = [(i, i + 1) for i in range(0, count, 2)]
    odd_down = [(i, i - 1) for i in range(1, count, 2)]
    even_down = [(i, (i - 1) % count) for i in range(0, count, 2)]

    mine, theirs = call(
        turned_kernel,
        [((depth // CORES, rows), BF16, whole((depth // CORES, rows)))] * 2,
        [SCALAR, whole((rows, depth))],
        (where, images),
        scratch=[pltpu.VMEM((depth, rows), BF16)],
    )
    theirs = send(theirs, other_core)

    projected, projected_b, own_part, own_sent, own_squares = call(
        project_kernel,
        [
            ((rows, width), F32, strip(rows, piece)),
            ((rows, width), BF16, strip(rows, piece)),
            (square, F32, whole(square)),
            (tile, BF16, whole(tile)),
            ((8, rows), F32, whole((8, rows))),
        ],
        [whole((rows, depth)), strip(depth, piece), strip(rows, piece)],
        (images, head, texts),
        grid=(steps,),
        scratch=[pltpu.VMEM((rows, 128), F32)],
    )
    far_second = lax.ppermute(texts, "dp", even_up)
    far_image_second = lax.ppermute(images, "dp", odd_down)
    near_text = gate(near_text, own_sent, theirs, mine)
    near_image = gate(near_image, far_second, far_image_second)
    far_first = lax.ppermute(near_text, "dp", odd_up)
    cross_text = send(near_text, other_core)
    far_image_first = lax.ppermute(near_image, "dp", even_down)
    cross_image = send(near_image, other_core)

    full = whole((rows, width))
    tile_outs = [
        (square, F32, whole(square)),
        (tile, BF16, whole(tile)),
        ((8, rows), F32, whole((8, rows))),
    ]
    pair_out = ((2, *tile), BF16, whole((2, *tile)))
    near_part, near_sent, near_squares = call(
        near_kernel,
        [tile_outs[0], pair_out, tile_outs[2]],
        [full, full, whole(tile)],
        (projected_b, near_text, own_sent),
    )
    near_there = swap_tensor(near_sent)
    cross_part, cross_sent, cross_squares = call(
        tile_kernel, tile_outs, [full, full], (projected_b, cross_text)
    )
    cross_there = swap_tensor(cross_sent)
    far_text, far_part, far_sent, far_squares = call(
        far_kernel,
        [((rows, width), BF16, full)] + tile_outs,
        [SCALAR, full, full, full],
        (core, projected_b, far_first, far_second),
    )
    far_there = swap_tensor(far_sent)

    scalars = [SCALAR] * 4
    known = (core, logit_scale, logit_bias, pair_mask, labels)
    halves = 2
    wide = width // halves
    some_pull, own_back, near_back, cross_back, inner, inverses = call(
        some_kernel,
        [
            ((rows, width), F32, strip(rows, wide)),
            (square, BF16, whole(square)),
            (square, BF16, whole(square)),
            (square, BF16, whole(square)),
            ((rows, 1), F32, whole((rows, 1))),
            ((rows, 2), F32, whole((rows, 2))),
        ],
        scalars
        + [whole((1, rows))]
        + [whole(square), whole((8, rows))]
        + [whole(square), whole((2, *tile)), whole((8, rows))]
        + [whole(square), whole(tile), whole((8, rows))]
        + [strip(rows, wide)] * 3
        + [LATER],
        known
        + (own_part, own_squares, near_part, near_there, near_squares)
        + (cross_part, cross_there, cross_squares)
        + (texts, near_text, cross_text, far_sent),
        grid=(halves,),
        scratch=[pltpu.VMEM((3, *square), BF16)],
    )
    grad_unit, far_back = call(
        unit_kernel,
        [((rows, width), BF16, strip(rows, wide)), (square, BF16, whole(square))],
        scalars
        + [whole((1, rows)), whole(square), whole(tile), whole((8, rows))]
        + [strip(rows, wide), strip(rows, wide), whole((rows, 1)), whole((rows, 2))]
        + [strip(rows, wide), LATER, LATER],
        known
        + (far_part, far_there, far_squares, far_text, some_pull, inner, inverses, projected)
        + (far_image_first, cross_image),
        grid=(halves,),
        scratch=[pltpu.VMEM(square, BF16), pltpu.VMEM((rows, 1), F32)],
    )

    grad_pair = send(grad_unit, other_core)
    lines = depth // CORES
    parts_of = 2 * halves
    slab = width // parts_of
    first_half = lambda j: (0, jnp.minimum(j, halves - 1))
    second_half = lambda j: (0, jnp.maximum(j - halves, 0))
    a_spec = pl.BlockSpec((lines // XS, slab), first_half)
    b_spec = pl.BlockSpec((lines // YS, slab), second_half)
    a_shape, b_shape = (lines // XS, width // 2), (lines // YS, width // 2)
    sides = (mine, theirs, grad_unit, grad_pair)
    side_specs = [whole((lines, rows))] * 2
    send_1, send_2, send_3, send_b = call(
        send_kernel,
        [(a_shape, BF16, a_spec)] * 3 + [(b_shape, BF16, b_spec)],
        side_specs + [strip(rows, slab)] * 2,
        sides,
        grid=(parts_of,),
        scratch=[pltpu.VMEM((lines // XS * (XS - 1), rows), BF16)] * 2,
    )
    got_b = send(send_b, over_y)
    gots_a = [send(block, over_x(d)) for d, block in ((2, send_2), (1, send_1), (3, send_3))]

    span = depth // 2
    chunk = span // steps

    def image_call(kernel, dtype, other, extra, operands):
        return pl.pallas_call(
            kernel,
            out_shape=jax.ShapeDtypeStruct((rows, span), dtype),
            grid_spec=pltpu.PrefetchScalarGridSpec(
                num_scalar_prefetch=1,
                grid=(steps,),
                in_specs=[
                    pl.BlockSpec((rows, width), lambda j, half: (0, 0)),
                    pl.BlockSpec((chunk, width), lambda j, half: ((half[0] ^ other) * steps + j, 0)),
                ]
                + extra,
                out_specs=pl.BlockSpec((rows, chunk), lambda j, half: (0, j)),
            ),
            compiler_params=pltpu.CompilerParams(vmem_limit_bytes=48 * 1024 * 1024),
        )(half, *operands)

    there = image_call(there_kernel, BF16, 1, [LATER], (grad_unit, head, send_b))

    near_back = send(gate(near_back, send_b), lambda i: i - 2)
    cross_back = send(gate(cross_back, send_b), lambda i: i - 3 if i % 2 else i - 1)
    far_back = send(gate(far_back, send_b), lambda i: i - 1 if i % 2 else i - 3)
    deep = depth // halves
    high, low = call(
        gather_kernel,
        [((rows, depth), BF16, strip(rows, deep))] * 2,
        [whole(square)] * 4 + [strip(rows, deep)] * 5,
        (own_back, near_back, cross_back, far_back)
        + (images, near_image, cross_image, far_image_first, far_image_second),
        grid=(halves,),
    )
    text_pull, dot_text = call(
        pull_kernel,
        [((rows, width), F32, strip(rows, piece)), ((1, rows), F32, whole((1, rows)))],
        [whole((rows, depth))] * 2
        + [strip(depth, piece), strip(rows, piece), whole((rows, 2))],
        (high, low, head, texts, inverses),
        grid=(steps,),
        scratch=[pltpu.VMEM((rows, 1), F32)],
    )
    gots_a[2] = gate(gots_a[2], high)
    short = lines // (YS * XS)
    keep_shape, keep_spec = (short, width // 2), strip(short, slab)
    keep_a, sent_a = call(
        sum_a_kernel,
        [(keep_shape, F32, keep_spec), (keep_shape, BF16, keep_spec)],
        side_specs + [strip(rows, slab)] * 2 + [strip(lines // XS, slab)] * 3,
        (*sides, *gots_a),
        grid=(halves,),
    )
    got_a = send(sent_a, over_y)
    second = pl.BlockSpec((rows, slab), lambda j: (0, j + halves))
    keep_b, *sends_b = call(
        sum_b_kernel,
        [(keep_shape, F32, keep_spec)] + [(keep_shape, BF16, keep_spec)] * 3,
        side_specs + [second] * 2 + [strip(lines // YS, slab), LATER],
        (*sides, got_b, sent_a),
        grid=(halves,),
    )
    gots_b = [send(sends_b[d - 1], over_x(d)) for d in (2, 1, 3)]
    there = swap_tensor(gate(there, keep_b))
    dot_there = swap_tensor(dot_text)
    gots_b[2] = gate(gots_b[2], text_pull)
    last = call(
        last_kernel,
        [((short, width), BF16, whole((short, width)))],
        [whole(keep_shape)] * 6,
        (keep_a, got_a, keep_b, *gots_b),
    )[0]
    last = gate(last, there, dot_there).reshape(ZS, short // ZS, width)
    line = [
        [index_of(y, x, z, c) for z in range(ZS)]
        for y in range(YS)
        for x in range(XS)
        for c in range(CORES)
    ]
    last = lax.all_to_all(last, "dp", 0, 0, axis_index_groups=line, tiled=True)
    grad_head = call(
        line_kernel,
        [((short // ZS, width), F32, whole((short // ZS, width)))],
        [whole(last.shape)],
        (last,),
    )[0]
    piece_spec = pl.BlockSpec((rows, chunk), lambda j, half: (0, j))
    grad_images = image_call(here_kernel, BF16, 0, [piece_spec], (grad_unit, head, there))

    grad_texts = call(
        text_kernel,
        [((rows, width), BF16, strip(rows, piece))],
        [strip(rows, piece)] * 2 + [whole((rows, 2)), whole((1, rows)), whole((1, rows))],
        (text_pull, texts, inverses, dot_text, dot_there),
        grid=(steps,),
    )[0]
    return (grad_images, grad_texts, grad_head)


def solution(mesh):
    return jax.shard_map(
        per_device,
        mesh=mesh,
        in_specs=(
            P("dp", None),
            P("dp", "tensor"),
            P(None, "tensor"),
            P("dp", None),
            P("dp"),
            P(),
            P(),
        ),
        out_specs=(P("dp", "tensor"), P("dp", "tensor"), P("dp", "tensor")),
        check_vma=False,
    )
```

```python
import jax
import jax.numpy as jnp
from jax import lax
from jax.experimental import pallas as pl
from jax.experimental.pallas import tpu as pltpu
from jax.sharding import PartitionSpec as P

EPSILON = 1e-06
LOSS_WEIGHT = 16.0
YS, XS, ZS, CORES = 2, 4, 8, 2

F32 = jnp.float32
BF16 = jnp.bfloat16


def place(index):
    return index // (XS * ZS * CORES), index // (ZS * CORES) % XS, index // CORES % ZS, index % CORES


def index_of(y, x, z, core):
    return (((y % YS) * XS + x % XS) * ZS + z % ZS) * CORES + core % CORES


def route(target):
    return [(i, target(i) % (YS * XS * ZS * CORES)) for i in range(YS * XS * ZS * CORES)]


def send(block, target):
    return lax.ppermute(block, "dp", route(target))


def swap_tensor(block):
    return lax.ppermute(block, "tensor", [(0, 1), (1, 0)])


def over_x(distance):
    def target(i):
        y, x, z, core = place(i)
        return index_of(y, x + distance, z, core)

    return target


def over_z(distance):
    def target(i):
        y, x, z, core = place(i)
        return index_of(y, x, z + distance, core)

    return target


def over_y(i):
    y, x, z, core = place(i)
    return index_of(y + 1, x, z, core)


def other_core(i):
    return i ^ 1


def dot(a, b, left, right):
    return lax.dot_general(a, b, (((left,), (right,)), ((), ())), preferred_element_type=F32)


EXTRA = 16


def nothing(*refs):
    pass


def gate(value, *earlier):
    spec = pl.BlockSpec(memory_space=pl.ANY)
    return pl.pallas_call(
        nothing,
        out_shape=jax.ShapeDtypeStruct(value.shape, value.dtype),
        in_specs=[spec] * (1 + len(earlier)),
        out_specs=spec,
        input_output_aliases={0: 0},
        compiler_params=pltpu.CompilerParams(vmem_limit_bytes=48 * 1024 * 1024),
    )(value, *earlier)


def call(kernel, outs, ins, operands, grid=None, scratch=(), vmem=48, cost=0):
    shapes = [jax.ShapeDtypeStruct(shape, dtype) for shape, dtype, _ in outs]
    return pl.pallas_call(
        kernel,
        out_shape=shapes,
        grid=grid or (1,),
        in_specs=ins,
        out_specs=[spec for _, _, spec in outs],
        scratch_shapes=list(scratch),
        compiler_params=pltpu.CompilerParams(vmem_limit_bytes=vmem * 1024 * 1024),
        cost_estimate=pl.CostEstimate(flops=cost, bytes_accessed=cost // 512, transcendentals=0),
    )(*operands)


def whole(shape):
    return pl.BlockSpec(shape, lambda j: (0,) * len(shape))


def strip(rows, columns):
    return pl.BlockSpec((rows, columns), lambda j: (0, j))


SCALAR = pl.BlockSpec(memory_space=pltpu.SMEM)
LATER = pl.BlockSpec(memory_space=pl.ANY)


def diagonal(n):
    return lax.broadcasted_iota(jnp.int32, (n, n), 0) == lax.broadcasted_iota(jnp.int32, (n, n), 1)


def to_row(column):
    return jnp.sum(jnp.where(diagonal(column.shape[0]), column, 0.0), axis=0, keepdims=True)


def to_column(row):
    return jnp.sum(jnp.where(diagonal(row.shape[1]), row, 0.0), axis=1, keepdims=True)


def message(part, *rows):
    n = part.shape[1]
    line = lax.broadcasted_iota(jnp.int32, (EXTRA, n), 0)
    extra = jnp.zeros((EXTRA, n), F32)
    for k, row in enumerate(rows):
        high = row.astype(BF16).astype(F32)
        extra = jnp.where(line == 2 * k, high, jnp.where(line == 2 * k + 1, row - high, extra))
    return jnp.concatenate([part.astype(BF16), extra.astype(BF16)], axis=0)


def row_of(extra, k):
    extra = extra.astype(F32)
    return extra[2 * k : 2 * k + 1] + extra[2 * k + 1 : 2 * k + 2]


def square_sum(block):
    block = block.astype(F32)
    return jnp.sum(block * block, axis=1, keepdims=True)


def project_kernel(images, head, texts, projected, projected_b, part, sent, squares, own):
    step = pl.program_id(0)
    product = jnp.dot(images[...], head[...], preferred_element_type=F32)
    projected[...] = product
    rounded = product.astype(BF16)
    projected_b[...] = rounded
    score = dot(rounded, texts[...], 1, 1)
    square_text = square_sum(texts[...])
    square_image = square_sum(product)

    @pl.when(step == 0)
    def _():
        part[...] = score
        own[:, 0:1] = square_text
        own[:, 1:2] = square_image

    @pl.when(step > 0)
    def _():
        part[...] += score
        own[:, 0:1] += square_text
        own[:, 1:2] += square_image

    @pl.when(step == pl.num_programs(0) - 1)
    def _():
        text_row, image_row = to_row(own[:, 0:1]), to_row(own[:, 1:2])
        line = lax.broadcasted_iota(jnp.int32, squares.shape, 0)
        squares[...] = jnp.where(line == 0, text_row, image_row)
        sent[...] = message(part[...], text_row, image_row)


def tile_kernel(rounded, text, part, sent, squares):
    part[...] = dot(rounded[...], text[...], 1, 1)
    row = to_row(square_sum(text[...]))
    squares[...] = jnp.broadcast_to(row, squares.shape)
    sent[...] = message(part[...], row)


def near_kernel(rounded, text, before, part, sent, squares):
    part[...] = dot(rounded[...], text[...], 1, 1)
    row = to_row(square_sum(text[...]))
    squares[...] = jnp.broadcast_to(row, squares.shape)
    sent[0] = before[...]
    sent[1] = message(part[...], row)


def far_kernel(core, rounded, first, second, far, part, sent, squares):
    @pl.when(core[0] == 0)
    def _():
        far[...] = first[...]

    @pl.when(core[0] != 0)
    def _():
        far[...] = second[...]

    part[...] = dot(rounded[...], far[...], 1, 1)
    row = to_row(square_sum(far[...]))
    squares[...] = jnp.broadcast_to(row, squares.shape)
    sent[...] = message(part[...], row)


def coefficients(part, there, square_row, inverse_image, labels, offset, mask, scale, bias):
    n = part.shape[0]
    inverse = lax.rsqrt(square_row + row_of(there[n:], 0) + EPSILON)
    scores = (part + there[:n].astype(F32)) * inverse_image * inverse
    logits = scale * scores + bias
    columns = lax.broadcasted_iota(jnp.int32, (n, n), 1) + offset * n
    sign = jnp.where(labels == columns, 1.0, -1.0)
    weight = mask.astype(F32)
    result = (-LOSS_WEIGHT * scale * weight) * sign * jax.nn.sigmoid(-sign * logits)
    inner = jnp.sum(result * scores, axis=1, keepdims=True)
    back = result * inverse_image
    return (result * inverse).astype(BF16), inner, back, inverse


def some_kernel(
    core, scale, bias, mask, labels, own_part, own_squares, near_part, near_there, near_squares,
    cross_part, cross_there, cross_squares, texts, near, cross, later,
    pull, own_back, near_back, cross_back, inner, inverses, weights,
):
    @pl.when(pl.program_id(0) == 0)
    def _():
        n = own_part.shape[0]
        image_row = own_squares[1:2, :] + row_of(near_there[0][n:], 1)
        inverse_image = to_column(lax.rsqrt(image_row + EPSILON))
        label = to_column(labels[...].astype(F32)).astype(jnp.int32)
        rest = (inverse_image, label)
        total = jnp.zeros((n, 1), F32)
        which = 1 + 2 * core[0]
        tiles = (
            (own_part[...], near_there[0], own_squares[0:1, :], 0, own_back),
            (near_part[...], near_there[1], near_squares[0:1, :], 2, near_back),
            (cross_part[...], cross_there[...], cross_squares[0:1, :], which, cross_back),
        )
        for k, (part, there, row, offset, out) in enumerate(tiles):
            weight, dots, back, inverse = coefficients(
                part, there, row, *rest, offset, mask[0, offset], scale[0], bias[0]
            )
            weights[k] = weight
            out[...] = back.T.astype(BF16)
            total = total + dots
            if k == 0:
                inverses[:, 1:2] = to_column(inverse)
        inner[...] = total
        inverses[:, 0:1] = inverse_image

    pull[...] = (
        dot(weights[0], texts[...], 1, 0)
        + dot(weights[1], near[...], 1, 0)
        + dot(weights[2], cross[...], 1, 0)
    )


def unit_kernel(
    core, scale, bias, mask, labels, part, there, squares, far, pull, inner, inverses, projected,
    later, unit, back, weight, factor,
):
    @pl.when(pl.program_id(0) == 0)
    def _():
        inverse_image = inverses[:, 0:1]
        label = to_column(labels[...].astype(F32)).astype(jnp.int32)
        offset = 3 - 2 * core[0]
        weights, dots, backs, _ = coefficients(
            part[...], there[...], squares[0:1, :], inverse_image, label, offset,
            mask[0, offset], scale[0], bias[0],
        )
        weight[...] = weights
        back[...] = backs.astype(BF16)
        factor[...] = inverse_image * (inner[...] + dots)

    total = pull[...] + dot(weight[...], far[...], 1, 0)
    unit[...] = ((total - projected[...] * factor[...]) * inverses[:, 0:1]).astype(BF16)


def turned_kernel(place_ref, images, mine, theirs, turned):
    turned[...] = images[...].astype(F32).T.astype(BF16)
    unit = mine.shape[0] // (YS * XS * ZS)
    core, here_x, here_y = place_ref[0], place_ref[1], place_ref[2]
    for dy in range(YS):
        for dx in range(XS):
            x, y = (here_x + dx) & (XS - 1), (here_y + dy) & (YS - 1)
            for z in range(ZS):
                to = ((dy * XS + dx) * ZS + z) * unit
                block = ((y * XS + x) * ZS + z) * CORES
                for whose, out in ((core, mine), (1 - core, theirs)):
                    start = pl.multiple_of((block + whose) * unit, unit)
                    out[to : to + unit, :] = turned[pl.ds(start, unit), :]


def send_kernel(mine, theirs, own, pair, later, a1, a2, a3, send_b, left, right):
    slab = mine.shape[0] // (YS * XS)
    many = (XS - 1) * slab

    @pl.when(pl.program_id(0) == 0)
    def _():
        for dy in range(YS):
            rows = slice((dy * XS + 1) * slab, (dy * XS + XS) * slab)
            left[dy * many : (dy + 1) * many, :] = mine[rows, :]
            right[dy * many : (dy + 1) * many, :] = theirs[rows, :]

    @pl.when(pl.program_id(0) < pl.num_programs(0) // 2)
    def _():
        total = dot(left[...], own[...], 1, 0) + dot(right[...], pair[...], 1, 0)
        total = total.astype(BF16)
        for dy in range(YS):
            for k, out in enumerate((a1, a2, a3)):
                start = dy * many + k * slab
                out[dy * slab : (dy + 1) * slab, :] = total[start : start + slab]

    @pl.when(pl.program_id(0) >= pl.num_programs(0) // 2)
    def _():
        rows = slice(XS * slab, 2 * XS * slab)
        total = dot(mine[rows, :], own[...], 1, 0) + dot(theirs[rows, :], pair[...], 1, 0)
        send_b[...] = total.astype(BF16)


def sum_a_kernel(mine, theirs, own, pair, g1, g2, g3, keep, sent):
    slab = mine.shape[0] // (YS * XS)
    for dy in range(YS):
        rows = slice(dy * XS * slab, (dy * XS + 1) * slab)
        total = dot(mine[rows, :], own[...], 1, 0) + dot(theirs[rows, :], pair[...], 1, 0)
        for got in (g1, g2, g3):
            total = total + got[dy * slab : (dy + 1) * slab, :].astype(F32)
        if dy == 0:
            keep[...] = total
        else:
            sent[...] = total.astype(BF16)


def sum_b_kernel(mine, theirs, own, pair, got, later, keep, s1, s2, s3):
    slab = mine.shape[0] // (YS * XS)
    rows = slice(0, XS * slab)
    total = dot(mine[rows, :], own[...], 1, 0) + dot(theirs[rows, :], pair[...], 1, 0)
    total = total + got[...].astype(F32)
    keep[...] = total[:slab]
    for k, out in enumerate((s1, s2, s3)):
        out[...] = total[(k + 1) * slab : (k + 2) * slab].astype(BF16)


def last_kernel(keep_a, got_a, keep_b, g1, g2, g3, out):
    middle = keep_a.shape[1]
    out[:, :middle] = (keep_a[...] + got_a[...].astype(F32)).astype(BF16)
    total = keep_b[...]
    for got in (g1, g2, g3):
        total = total + got[...].astype(F32)
    out[:, middle:] = total.astype(BF16)


def line_kernel(blocks, out):
    total = blocks[0].astype(F32)
    for k in range(1, blocks.shape[0]):
        total = total + blocks[k].astype(F32)
    out[...] = total


def there_kernel(half, unit, head, later, out):
    out[...] = dot(unit[...], head[...], 1, 1).astype(BF16)


def here_kernel(half, unit, head, there, out):
    out[...] = (dot(unit[...], head[...], 1, 1) + there[...].astype(F32)).astype(BF16)


def term_kernel(back, rounded, later, out):
    out[...] = dot(back[...].astype(F32).T.astype(BF16), rounded[...], 1, 0).astype(BF16)


def gather_kernel(own_back, near_back, cross_back, own, near, cross, high, low):
    total = (
        dot(own_back[...], own[...], 1, 0)
        + dot(near_back[...], near[...], 1, 0)
        + dot(cross_back[...], cross[...], 1, 0)
    )
    rounded = total.astype(BF16)
    high[...] = rounded
    low[...] = (total - rounded.astype(F32)).astype(BF16)


def pull_kernel(high, low, head, far, texts, inverses, pull, inner, column):
    step = pl.program_id(0)
    total = dot(high[...], head[...], 1, 0) + dot(low[...], head[...], 1, 0)
    total = total + far[...].astype(F32)
    pull[...] = total
    unit = texts[...].astype(F32) * inverses[:, 1:2]
    dots = jnp.sum(unit * total, axis=1, keepdims=True)

    @pl.when(step == 0)
    def _():
        column[...] = dots

    @pl.when(step > 0)
    def _():
        column[...] += dots

    @pl.when(step == pl.num_programs(0) - 1)
    def _():
        inner[...] = to_row(column[...])


def text_kernel(pull, texts, inverses, inner, there, out):
    inverse = inverses[:, 1:2]
    unit = texts[...].astype(F32) * inverse
    out[...] = ((pull[...] - unit * to_column(inner[...] + there[...])) * inverse).astype(BF16)


def per_device(images, texts, head, pair_mask, labels, logit_scale, logit_bias):
    rows, depth = images.shape
    width = texts.shape[1]
    steps = 4
    piece = width // steps
    me = lax.axis_index("dp")
    core = (me & 1)[None]
    where = jnp.stack([me & 1, (me >> 4) & (XS - 1), me >> 6])
    half = lax.axis_index("tensor")[None]
    labels = labels.reshape(1, rows)
    tile, square = (rows + EXTRA, rows), (rows, rows)

    near_text = send(texts, lambda i: i + 2)
    near_image = send(images, lambda i: i - 2)
    count = YS * XS * ZS * CORES
    odd_up = [(i, (i + 1) % count) for i in range(1, count, 2)]
    even_up = [(i, i + 1) for i in range(0, count, 2)]

    mine, theirs = call(
        turned_kernel,
        [((depth // CORES, rows), BF16, whole((depth // CORES, rows)))] * 2,
        [SCALAR, whole((rows, depth))],
        (where, images),
        scratch=[pltpu.VMEM((depth, rows), BF16)],
    )
    theirs = send(theirs, other_core)

    projected, projected_b, own_part, own_sent, own_squares = call(
        project_kernel,
        [
            ((rows, width), F32, strip(rows, piece)),
            ((rows, width), BF16, strip(rows, piece)),
            (square, F32, whole(square)),
            (tile, BF16, whole(tile)),
            ((8, rows), F32, whole((8, rows))),
        ],
        [whole((rows, depth)), strip(depth, piece), strip(rows, piece)],
        (images, head, texts),
        grid=(steps,),
        scratch=[pltpu.VMEM((rows, 128), F32)],
    )
    far_second = lax.ppermute(texts, "dp", even_up)
    near_text = gate(near_text, own_sent, theirs, mine)
    near_text = gate(near_text, far_second)
    far_first = lax.ppermute(near_text, "dp", odd_up)
    cross_text = send(near_text, other_core)
    full = whole((rows, width))
    tile_outs = [
        (square, F32, whole(square)),
        (tile, BF16, whole(tile)),
        ((8, rows), F32, whole((8, rows))),
    ]
    pair_out = ((2, *tile), BF16, whole((2, *tile)))
    near_part, near_sent, near_squares = call(
        near_kernel,
        [tile_outs[0], pair_out, tile_outs[2]],
        [full, full, whole(tile)],
        (projected_b, near_text, own_sent),
    )
    near_there = swap_tensor(near_sent)
    cross_text = gate(cross_text, near_image)
    cross_part, cross_sent, cross_squares = call(
        tile_kernel, tile_outs, [full, full], (projected_b, cross_text)
    )
    cross_there = swap_tensor(cross_sent)
    cross_image = send(near_image, other_core)
    far_text, far_part, far_sent, far_squares = call(
        far_kernel,
        [((rows, width), BF16, full)] + tile_outs,
        [SCALAR, full, full, full],
        (core, projected_b, far_first, far_second),
    )
    far_there = swap_tensor(far_sent)

    scalars = [SCALAR] * 4
    known = (core, logit_scale, logit_bias, pair_mask, labels)
    halves = 2
    wide = width // halves
    some_pull, own_back, near_back, cross_back, inner, inverses = call(
        some_kernel,
        [
            ((rows, width), F32, strip(rows, wide)),
            (square, BF16, whole(square)),
            (square, BF16, whole(square)),
            (square, BF16, whole(square)),
            ((rows, 1), F32, whole((rows, 1))),
            ((rows, 2), F32, whole((rows, 2))),
        ],
        scalars
        + [whole((1, rows))]
        + [whole(square), whole((8, rows))]
        + [whole(square), whole((2, *tile)), whole((8, rows))]
        + [whole(square), whole(tile), whole((8, rows))]
        + [strip(rows, wide)] * 3
        + [LATER],
        known
        + (own_part, own_squares, near_part, near_there, near_squares)
        + (cross_part, cross_there, cross_squares)
        + (texts, near_text, cross_text, far_sent),
        grid=(halves,),
        scratch=[pltpu.VMEM((3, *square), BF16)],
    )
    grad_unit, far_back = call(
        unit_kernel,
        [((rows, width), BF16, strip(rows, wide)), (square, BF16, whole(square))],
        scalars
        + [whole((1, rows)), whole(square), whole(tile), whole((8, rows))]
        + [strip(rows, wide), strip(rows, wide), whole((rows, 1)), whole((rows, 2))]
        + [strip(rows, wide), LATER],
        known
        + (far_part, far_there, far_squares, far_text, some_pull, inner, inverses, projected)
        + (cross_image,),
        grid=(halves,),
        scratch=[pltpu.VMEM(square, BF16), pltpu.VMEM((rows, 1), F32)],
    )

    grad_pair = send(grad_unit, other_core)
    lines = depth // CORES
    parts_of = 2 * halves
    slab = width // parts_of
    first_half = lambda j: (0, jnp.minimum(j, halves - 1))
    second_half = lambda j: (0, jnp.maximum(j - halves, 0))
    a_spec = pl.BlockSpec((lines // XS, slab), first_half)
    b_spec = pl.BlockSpec((lines // YS, slab), second_half)
    a_shape, b_shape = (lines // XS, width // 2), (lines // YS, width // 2)
    sides = (mine, theirs, grad_unit, grad_pair)
    side_specs = [whole((lines, rows))] * 2
    far_term = call(
        term_kernel,
        [((rows, width), BF16, strip(rows, wide))],
        [whole(square), strip(rows, wide), LATER],
        (far_back, projected_b, grad_unit),
        grid=(halves,),
    )[0]
    send_1, send_2, send_3, send_b = call(
        send_kernel,
        [(a_shape, BF16, a_spec)] * 3 + [(b_shape, BF16, b_spec)],
        side_specs + [strip(rows, slab)] * 2 + [LATER],
        (*sides, far_term),
        grid=(parts_of,),
        scratch=[pltpu.VMEM((lines // XS * (XS - 1), rows), BF16)] * 2,
    )
    got_b = send(send_b, over_y)
    gots_a = [send(block, over_x(d)) for d, block in ((2, send_2), (1, send_1), (3, send_3))]

    span = depth // 2
    chunk = span // steps

    def image_call(kernel, dtype, other, extra, operands):
        return pl.pallas_call(
            kernel,
            out_shape=jax.ShapeDtypeStruct((rows, span), dtype),
            grid_spec=pltpu.PrefetchScalarGridSpec(
                num_scalar_prefetch=1,
                grid=(steps,),
                in_specs=[
                    pl.BlockSpec((rows, width), lambda j, half: (0, 0)),
                    pl.BlockSpec((chunk, width), lambda j, half: ((half[0] ^ other) * steps + j, 0)),
                ]
                + extra,
                out_specs=pl.BlockSpec((rows, chunk), lambda j, half: (0, j)),
            ),
            compiler_params=pltpu.CompilerParams(vmem_limit_bytes=48 * 1024 * 1024),
        )(half, *operands)

    there = image_call(there_kernel, BF16, 1, [LATER], (grad_unit, head, send_b))

    far_term = send(gate(far_term, send_b), lambda i: i - 1 if i % 2 else i - 3)
    near_back = send(gate(near_back, far_term), lambda i: i - 2)
    cross_back = send(gate(cross_back, far_term), lambda i: i - 3 if i % 2 else i - 1)
    deep = depth // halves
    high, low = call(
        gather_kernel,
        [((rows, depth), BF16, strip(rows, deep))] * 2,
        [whole(square)] * 3 + [strip(rows, deep)] * 3,
        (own_back, near_back, cross_back, images, near_image, cross_image),
        grid=(halves,),
    )
    text_pull, dot_text = call(
        pull_kernel,
        [((rows, width), F32, strip(rows, piece)), ((1, rows), F32, whole((1, rows)))],
        [whole((rows, depth))] * 2
        + [strip(depth, piece), strip(rows, piece), strip(rows, piece), whole((rows, 2))],
        (high, low, head, far_term, texts, inverses),
        grid=(steps,),
        scratch=[pltpu.VMEM((rows, 1), F32)],
    )
    gots_a[2] = gate(gots_a[2], high)
    short = lines // (YS * XS)
    keep_shape, keep_spec = (short, width // 2), strip(short, slab)
    keep_a, sent_a = call(
        sum_a_kernel,
        [(keep_shape, F32, keep_spec), (keep_shape, BF16, keep_spec)],
        side_specs + [strip(rows, slab)] * 2 + [strip(lines // XS, slab)] * 3,
        (*sides, *gots_a),
        grid=(halves,),
    )
    got_a = send(sent_a, over_y)
    second = pl.BlockSpec((rows, slab), lambda j: (0, j + halves))
    keep_b, *sends_b = call(
        sum_b_kernel,
        [(keep_shape, F32, keep_spec)] + [(keep_shape, BF16, keep_spec)] * 3,
        side_specs + [second] * 2 + [strip(lines // YS, slab), LATER],
        (*sides, got_b, sent_a),
        grid=(halves,),
    )
    gots_b = [send(sends_b[d - 1], over_x(d)) for d in (2, 1, 3)]
    there = swap_tensor(gate(there, keep_b))
    dot_there = swap_tensor(dot_text)
    gots_b[2] = gate(gots_b[2], text_pull)
    last = call(
        last_kernel,
        [((short, width), BF16, whole((short, width)))],
        [whole(keep_shape)] * 6,
        (keep_a, got_a, keep_b, *gots_b),
    )[0]
    last = gate(last, there, dot_there).reshape(ZS, short // ZS, width)
    line = [
        [index_of(y, x, z, c) for z in range(ZS)]
        for y in range(YS)
        for x in range(XS)
        for c in range(CORES)
    ]
    last = lax.all_to_all(last, "dp", 0, 0, axis_index_groups=line, tiled=True)
    grad_head = call(
        line_kernel,
        [((short // ZS, width), F32, whole((short // ZS, width)))],
        [whole(last.shape)],
        (last,),
    )[0]
    piece_spec = pl.BlockSpec((rows, chunk), lambda j, half: (0, j))
    grad_images = image_call(here_kernel, BF16, 0, [piece_spec], (grad_unit, head, there))

    grad_texts = call(
        text_kernel,
        [((rows, width), BF16, strip(rows, piece))],
        [strip(rows, piece)] * 2 + [whole((rows, 2)), whole((1, rows)), whole((1, rows))],
        (text_pull, texts, inverses, dot_text, dot_there),
        grid=(steps,),
    )[0]
    return (grad_images, grad_texts, grad_head)


def solution(mesh):
    return jax.shard_map(
        per_device,
        mesh=mesh,
        in_specs=(
            P("dp", None),
            P("dp", "tensor"),
            P(None, "tensor"),
            P("dp", None),
            P("dp"),
            P(),
            P(),
        ),
        out_specs=(P("dp", "tensor"), P("dp", "tensor"), P("dp", "tensor")),
        check_vma=False,
    )
```

```python
import jax
import jax.numpy as jnp
from jax import lax
from jax.experimental import pallas as pl
from jax.experimental.pallas import tpu as pltpu
from jax.sharding import PartitionSpec as P

EPSILON = 1e-06
LOSS_WEIGHT = 16.0
YS, XS, ZS, CORES = 2, 4, 8, 2

F32 = jnp.float32
BF16 = jnp.bfloat16


def place(index):
    return index // (XS * ZS * CORES), index // (ZS * CORES) % XS, index // CORES % ZS, index % CORES


def index_of(y, x, z, core):
    return (((y % YS) * XS + x % XS) * ZS + z % ZS) * CORES + core % CORES


def route(target):
    return [(i, target(i) % (YS * XS * ZS * CORES)) for i in range(YS * XS * ZS * CORES)]


def send(block, target):
    return lax.ppermute(block, "dp", route(target))


def swap_tensor(block):
    return lax.ppermute(block, "tensor", [(0, 1), (1, 0)])


def over_x(distance):
    def target(i):
        y, x, z, core = place(i)
        return index_of(y, x + distance, z, core)

    return target


def over_z(distance):
    def target(i):
        y, x, z, core = place(i)
        return index_of(y, x, z + distance, core)

    return target


def over_y(i):
    y, x, z, core = place(i)
    return index_of(y + 1, x, z, core)


def other_core(i):
    return i ^ 1


def dot(a, b, left, right):
    return lax.dot_general(a, b, (((left,), (right,)), ((), ())), preferred_element_type=F32)


EXTRA = 16


def nothing(*refs):
    pass


def gate(value, *earlier):
    spec = pl.BlockSpec(memory_space=pl.ANY)
    return pl.pallas_call(
        nothing,
        out_shape=jax.ShapeDtypeStruct(value.shape, value.dtype),
        in_specs=[spec] * (1 + len(earlier)),
        out_specs=spec,
        input_output_aliases={0: 0},
        compiler_params=pltpu.CompilerParams(vmem_limit_bytes=48 * 1024 * 1024),
    )(value, *earlier)


def call(kernel, outs, ins, operands, grid=None, scratch=(), vmem=48, cost=0):
    shapes = [jax.ShapeDtypeStruct(shape, dtype) for shape, dtype, _ in outs]
    return pl.pallas_call(
        kernel,
        out_shape=shapes,
        grid=grid or (1,),
        in_specs=ins,
        out_specs=[spec for _, _, spec in outs],
        scratch_shapes=list(scratch),
        compiler_params=pltpu.CompilerParams(vmem_limit_bytes=vmem * 1024 * 1024),
        cost_estimate=pl.CostEstimate(flops=cost, bytes_accessed=cost // 512, transcendentals=0),
    )(*operands)


def whole(shape):
    return pl.BlockSpec(shape, lambda j: (0,) * len(shape))


def strip(rows, columns):
    return pl.BlockSpec((rows, columns), lambda j: (0, j))


SCALAR = pl.BlockSpec(memory_space=pltpu.SMEM)
LATER = pl.BlockSpec(memory_space=pl.ANY)


def diagonal(n):
    return lax.broadcasted_iota(jnp.int32, (n, n), 0) == lax.broadcasted_iota(jnp.int32, (n, n), 1)


def to_row(column):
    return jnp.sum(jnp.where(diagonal(column.shape[0]), column, 0.0), axis=0, keepdims=True)


def to_column(row):
    return jnp.sum(jnp.where(diagonal(row.shape[1]), row, 0.0), axis=1, keepdims=True)


def message(part, *rows):
    n = part.shape[1]
    line = lax.broadcasted_iota(jnp.int32, (EXTRA, n), 0)
    extra = jnp.zeros((EXTRA, n), F32)
    for k, row in enumerate(rows):
        high = row.astype(BF16).astype(F32)
        extra = jnp.where(line == 2 * k, high, jnp.where(line == 2 * k + 1, row - high, extra))
    return jnp.concatenate([part.astype(BF16), extra.astype(BF16)], axis=0)


def row_of(extra, k):
    extra = extra.astype(F32)
    return extra[2 * k : 2 * k + 1] + extra[2 * k + 1 : 2 * k + 2]


def square_sum(block):
    block = block.astype(F32)
    return jnp.sum(block * block, axis=1, keepdims=True)


def project_kernel(images, head, texts, projected, projected_b, part, sent, squares, own):
    step = pl.program_id(0)
    product = jnp.dot(images[...], head[...], preferred_element_type=F32)
    projected[...] = product
    rounded = product.astype(BF16)
    projected_b[...] = rounded
    score = dot(rounded, texts[...], 1, 1)
    square_text = square_sum(texts[...])
    square_image = square_sum(product)

    @pl.when(step == 0)
    def _():
        part[...] = score
        own[:, 0:1] = square_text
        own[:, 1:2] = square_image

    @pl.when(step > 0)
    def _():
        part[...] += score
        own[:, 0:1] += square_text
        own[:, 1:2] += square_image

    @pl.when(step == pl.num_programs(0) - 1)
    def _():
        text_row, image_row = to_row(own[:, 0:1]), to_row(own[:, 1:2])
        line = lax.broadcasted_iota(jnp.int32, squares.shape, 0)
        squares[...] = jnp.where(line == 0, text_row, image_row)
        sent[...] = message(part[...], text_row, image_row)


def tile_kernel(rounded, text, part, sent, squares):
    part[...] = dot(rounded[...], text[...], 1, 1)
    row = to_row(square_sum(text[...]))
    squares[...] = jnp.broadcast_to(row, squares.shape)
    sent[...] = message(part[...], row)


def near_kernel(rounded, text, before, part, sent, squares):
    part[...] = dot(rounded[...], text[...], 1, 1)
    row = to_row(square_sum(text[...]))
    squares[...] = jnp.broadcast_to(row, squares.shape)
    sent[0] = before[...]
    sent[1] = message(part[...], row)


def far_kernel(core, rounded, first, second, far, part, sent, squares):
    @pl.when(core[0] == 0)
    def _():
        far[...] = first[...]

    @pl.when(core[0] != 0)
    def _():
        far[...] = second[...]

    part[...] = dot(rounded[...], far[...], 1, 1)
    row = to_row(square_sum(far[...]))
    squares[...] = jnp.broadcast_to(row, squares.shape)
    sent[...] = message(part[...], row)


def coefficients(part, there, square_row, inverse_image, labels, offset, mask, scale, bias):
    n = part.shape[0]
    inverse = lax.rsqrt(square_row + row_of(there[n:], 0) + EPSILON)
    scores = (part + there[:n].astype(F32)) * inverse_image * inverse
    logits = scale * scores + bias
    columns = lax.broadcasted_iota(jnp.int32, (n, n), 1) + offset * n
    sign = jnp.where(labels == columns, 1.0, -1.0)
    weight = mask.astype(F32)
    result = (-LOSS_WEIGHT * scale * weight) * sign * jax.nn.sigmoid(-sign * logits)
    inner = jnp.sum(result * scores, axis=1, keepdims=True)
    back = result * inverse_image
    return (result * inverse).astype(BF16), inner, back, inverse


def some_kernel(
    core, scale, bias, mask, labels, own_part, own_squares, near_part, near_there, near_squares,
    cross_part, cross_there, cross_squares, texts, near, cross, later,
    pull, own_back, near_back, cross_back, inner, inverses, weights,
):
    @pl.when(pl.program_id(0) == 0)
    def _():
        n = own_part.shape[0]
        image_row = own_squares[1:2, :] + row_of(near_there[0][n:], 1)
        inverse_image = to_column(lax.rsqrt(image_row + EPSILON))
        label = to_column(labels[...].astype(F32)).astype(jnp.int32)
        rest = (inverse_image, label)
        total = jnp.zeros((n, 1), F32)
        which = 1 + 2 * core[0]
        tiles = (
            (own_part[...], near_there[0], own_squares[0:1, :], 0, own_back),
            (near_part[...], near_there[1], near_squares[0:1, :], 2, near_back),
            (cross_part[...], cross_there[...], cross_squares[0:1, :], which, cross_back),
        )
        for k, (part, there, row, offset, out) in enumerate(tiles):
            weight, dots, back, inverse = coefficients(
                part, there, row, *rest, offset, mask[0, offset], scale[0], bias[0]
            )
            weights[k] = weight
            out[...] = back.T.astype(BF16)
            total = total + dots
            if k == 0:
                inverses[:, 1:2] = to_column(inverse)
        inner[...] = total
        inverses[:, 0:1] = inverse_image

    pull[...] = (
        dot(weights[0], texts[...], 1, 0)
        + dot(weights[1], near[...], 1, 0)
        + dot(weights[2], cross[...], 1, 0)
    )


def unit_kernel(
    core, scale, bias, mask, labels, part, there, squares, far, pull, inner, inverses, projected,
    later, unit, back, weight, factor,
):
    @pl.when(pl.program_id(0) == 0)
    def _():
        inverse_image = inverses[:, 0:1]
        label = to_column(labels[...].astype(F32)).astype(jnp.int32)
        offset = 3 - 2 * core[0]
        weights, dots, backs, _ = coefficients(
            part[...], there[...], squares[0:1, :], inverse_image, label, offset,
            mask[0, offset], scale[0], bias[0],
        )
        weight[...] = weights
        back[...] = backs.astype(BF16)
        factor[...] = inverse_image * (inner[...] + dots)

    total = pull[...] + dot(weight[...], far[...], 1, 0)
    unit[...] = ((total - projected[...] * factor[...]) * inverses[:, 0:1]).astype(BF16)


def turned_kernel(place_ref, images, mine, theirs, turned):
    turned[...] = images[...].astype(F32).T.astype(BF16)
    unit = mine.shape[0] // (YS * XS * ZS)
    core, here_x, here_y = place_ref[0], place_ref[1], place_ref[2]
    for dy in range(YS):
        for dx in range(XS):
            x, y = (here_x + dx) & (XS - 1), (here_y + dy) & (YS - 1)
            for z in range(ZS):
                to = ((dy * XS + dx) * ZS + z) * unit
                block = ((y * XS + x) * ZS + z) * CORES
                for whose, out in ((core, mine), (1 - core, theirs)):
                    start = pl.multiple_of((block + whose) * unit, unit)
                    out[to : to + unit, :] = turned[pl.ds(start, unit), :]


def send_kernel(place_ref, mine, theirs, own, pair, later, send_a, send_b, left, right):
    slab = mine.shape[0] // (YS * XS)
    many = (XS - 1) * slab

    @pl.when(pl.program_id(0) == 0)
    def _():
        for dy in range(YS):
            rows = slice((dy * XS + 1) * slab, (dy * XS + XS) * slab)
            left[dy * many : (dy + 1) * many, :] = mine[rows, :]
            right[dy * many : (dy + 1) * many, :] = theirs[rows, :]

    @pl.when(pl.program_id(0) < pl.num_programs(0) // 2)
    def _():
        total = dot(left[...], own[...], 1, 0) + dot(right[...], pair[...], 1, 0)
        total = total.astype(BF16)
        here = place_ref[1]
        send_a[here] = jnp.zeros(send_a.shape[1:], BF16)
        for dy in range(YS):
            for dx in range(1, XS):
                start = dy * many + (dx - 1) * slab
                target = (here + dx) & (XS - 1)
                send_a[target, dy * slab : (dy + 1) * slab, :] = total[start : start + slab]

    @pl.when(pl.program_id(0) >= pl.num_programs(0) // 2)
    def _():
        rows = slice(XS * slab, 2 * XS * slab)
        total = dot(mine[rows, :], own[...], 1, 0) + dot(theirs[rows, :], pair[...], 1, 0)
        send_b[...] = total.astype(BF16)


def sum_a_kernel(mine, theirs, own, pair, gots, keep, sent):
    slab = mine.shape[0] // (YS * XS)
    for dy in range(YS):
        rows = slice(dy * XS * slab, (dy * XS + 1) * slab)
        total = dot(mine[rows, :], own[...], 1, 0) + dot(theirs[rows, :], pair[...], 1, 0)
        for k in range(XS):
            total = total + gots[k, dy * slab : (dy + 1) * slab, :].astype(F32)
        if dy == 0:
            keep[...] = total
        else:
            sent[...] = total.astype(BF16)


def sum_b_kernel(mine, theirs, own, pair, got, later_a, later_b, keep, s1, s2, s3):
    slab = mine.shape[0] // (YS * XS)
    rows = slice(0, XS * slab)
    total = dot(mine[rows, :], own[...], 1, 0) + dot(theirs[rows, :], pair[...], 1, 0)
    total = total + got[...].astype(F32)
    keep[...] = total[:slab]
    for k, out in enumerate((s1, s2, s3)):
        out[...] = total[(k + 1) * slab : (k + 2) * slab].astype(BF16)


def last_kernel(keep_a, got_a, keep_b, g1, g2, g3, out):
    middle = keep_a.shape[1]
    out[:, :middle] = (keep_a[...] + got_a[...].astype(F32)).astype(BF16)
    total = keep_b[...]
    for got in (g1, g2, g3):
        total = total + got[...].astype(F32)
    out[:, middle:] = total.astype(BF16)


def line_kernel(blocks, out):
    total = blocks[0].astype(F32)
    for k in range(1, blocks.shape[0]):
        total = total + blocks[k].astype(F32)
    out[...] = total


def there_kernel(half, unit, head, later, out):
    out[...] = dot(unit[...], head[...], 1, 1).astype(BF16)


def here_kernel(half, unit, head, there, out):
    out[...] = (dot(unit[...], head[...], 1, 1) + there[...].astype(F32)).astype(BF16)


def term_kernel(back, rounded, later, out):
    out[...] = dot(back[...].astype(F32).T.astype(BF16), rounded[...], 1, 0).astype(BF16)


def gather_kernel(own_back, near_back, cross_back, own, near, cross, high, low):
    total = (
        dot(own_back[...], own[...], 1, 0)
        + dot(near_back[...], near[...], 1, 0)
        + dot(cross_back[...], cross[...], 1, 0)
    )
    rounded = total.astype(BF16)
    high[...] = rounded
    low[...] = (total - rounded.astype(F32)).astype(BF16)


def pull_kernel(high, low, head, far, texts, inverses, pull, inner, column):
    step = pl.program_id(0)
    total = dot(high[...], head[...], 1, 0) + dot(low[...], head[...], 1, 0)
    total = total + far[...].astype(F32)
    pull[...] = total
    unit = texts[...].astype(F32) * inverses[:, 1:2]
    dots = jnp.sum(unit * total, axis=1, keepdims=True)

    @pl.when(step == 0)
    def _():
        column[...] = dots

    @pl.when(step > 0)
    def _():
        column[...] += dots

    @pl.when(step == pl.num_programs(0) - 1)
    def _():
        inner[...] = to_row(column[...])


def text_kernel(pull, texts, inverses, inner, there, out):
    inverse = inverses[:, 1:2]
    unit = texts[...].astype(F32) * inverse
    out[...] = ((pull[...] - unit * to_column(inner[...] + there[...])) * inverse).astype(BF16)


def per_device(images, texts, head, pair_mask, labels, logit_scale, logit_bias):
    rows, depth = images.shape
    width = texts.shape[1]
    steps = 4
    piece = width // steps
    me = lax.axis_index("dp")
    core = (me & 1)[None]
    where = jnp.stack([me & 1, (me >> 4) & (XS - 1), me >> 6])
    half = lax.axis_index("tensor")[None]
    labels = labels.reshape(1, rows)
    tile, square = (rows + EXTRA, rows), (rows, rows)

    near_text = send(texts, lambda i: i + 2)
    near_image = send(images, lambda i: i - 2)
    count = YS * XS * ZS * CORES
    odd_up = [(i, (i + 1) % count) for i in range(1, count, 2)]
    even_up = [(i, i + 1) for i in range(0, count, 2)]

    mine, theirs = call(
        turned_kernel,
        [((depth // CORES, rows), BF16, whole((depth // CORES, rows)))] * 2,
        [SCALAR, whole((rows, depth))],
        (where, images),
        scratch=[pltpu.VMEM((depth, rows), BF16)],
    )
    theirs = send(theirs, other_core)

    projected, projected_b, own_part, own_sent, own_squares = call(
        project_kernel,
        [
            ((rows, width), F32, strip(rows, piece)),
            ((rows, width), BF16, strip(rows, piece)),
            (square, F32, whole(square)),
            (tile, BF16, whole(tile)),
            ((8, rows), F32, whole((8, rows))),
        ],
        [whole((rows, depth)), strip(depth, piece), strip(rows, piece)],
        (images, head, texts),
        grid=(steps,),
        scratch=[pltpu.VMEM((rows, 128), F32)],
    )
    far_second = lax.ppermute(texts, "dp", even_up)
    near_text = gate(near_text, own_sent, theirs, mine)
    near_text = gate(near_text, far_second)
    far_first = lax.ppermute(near_text, "dp", odd_up)
    cross_text = send(near_text, other_core)
    full = whole((rows, width))
    tile_outs = [
        (square, F32, whole(square)),
        (tile, BF16, whole(tile)),
        ((8, rows), F32, whole((8, rows))),
    ]
    pair_out = ((2, *tile), BF16, whole((2, *tile)))
    near_part, near_sent, near_squares = call(
        near_kernel,
        [tile_outs[0], pair_out, tile_outs[2]],
        [full, full, whole(tile)],
        (projected_b, near_text, own_sent),
    )
    near_there = swap_tensor(near_sent)
    cross_text = gate(cross_text, near_image)
    cross_part, cross_sent, cross_squares = call(
        tile_kernel, tile_outs, [full, full], (projected_b, cross_text)
    )
    cross_there = swap_tensor(cross_sent)
    cross_image = send(near_image, other_core)
    far_text, far_part, far_sent, far_squares = call(
        far_kernel,
        [((rows, width), BF16, full)] + tile_outs,
        [SCALAR, full, full, full],
        (core, projected_b, far_first, far_second),
    )
    far_there = swap_tensor(far_sent)

    scalars = [SCALAR] * 4
    known = (core, logit_scale, logit_bias, pair_mask, labels)
    halves = 2
    wide = width // halves
    some_pull, own_back, near_back, cross_back, inner, inverses = call(
        some_kernel,
        [
            ((rows, width), F32, strip(rows, wide)),
            (square, BF16, whole(square)),
            (square, BF16, whole(square)),
            (square, BF16, whole(square)),
            ((rows, 1), F32, whole((rows, 1))),
            ((rows, 2), F32, whole((rows, 2))),
        ],
        scalars
        + [whole((1, rows))]
        + [whole(square), whole((8, rows))]
        + [whole(square), whole((2, *tile)), whole((8, rows))]
        + [whole(square), whole(tile), whole((8, rows))]
        + [strip(rows, wide)] * 3
        + [LATER],
        known
        + (own_part, own_squares, near_part, near_there, near_squares)
        + (cross_part, cross_there, cross_squares)
        + (texts, near_text, cross_text, far_sent),
        grid=(halves,),
        scratch=[pltpu.VMEM((3, *square), BF16)],
    )
    grad_unit, far_back = call(
        unit_kernel,
        [((rows, width), BF16, strip(rows, wide)), (square, BF16, whole(square))],
        scalars
        + [whole((1, rows)), whole(square), whole(tile), whole((8, rows))]
        + [strip(rows, wide), strip(rows, wide), whole((rows, 1)), whole((rows, 2))]
        + [strip(rows, wide), LATER],
        known
        + (far_part, far_there, far_squares, far_text, some_pull, inner, inverses, projected)
        + (cross_image,),
        grid=(halves,),
        scratch=[pltpu.VMEM(square, BF16), pltpu.VMEM((rows, 1), F32)],
    )

    grad_pair = send(grad_unit, other_core)
    lines = depth // CORES
    parts_of = 2 * halves
    slab = width // parts_of
    first_half = lambda j: (0, jnp.minimum(j, halves - 1))
    second_half = lambda j: (0, jnp.maximum(j - halves, 0))
    a_spec = pl.BlockSpec((XS, lines // XS, slab), lambda j: (0, *first_half(j)))
    b_spec = pl.BlockSpec((lines // YS, slab), second_half)
    a_shape, b_shape = (lines // XS, width // 2), (lines // YS, width // 2)
    sides = (mine, theirs, grad_unit, grad_pair)
    side_specs = [whole((lines, rows))] * 2
    far_term = call(
        term_kernel,
        [((rows, width), BF16, strip(rows, wide))],
        [whole(square), strip(rows, wide), LATER],
        (far_back, projected_b, grad_unit),
        grid=(halves,),
    )[0]
    send_a, send_b = call(
        send_kernel,
        [((XS, *a_shape), BF16, a_spec), (b_shape, BF16, b_spec)],
        [SCALAR] + side_specs + [strip(rows, slab)] * 2 + [LATER],
        (where, *sides, far_term),
        grid=(parts_of,),
        scratch=[pltpu.VMEM((lines // XS * (XS - 1), rows), BF16)] * 2,
    )
    got_b = send(send_b, over_y)
    squares_x = [
        [index_of(y, x, z, c) for x in range(XS)]
        for y in range(YS)
        for z in range(ZS)
        for c in range(CORES)
    ]
    gots_a = lax.all_to_all(send_a, "dp", 0, 0, axis_index_groups=squares_x, tiled=True)

    span = depth // 2
    chunk = span // steps

    def image_call(kernel, dtype, other, extra, operands):
        return pl.pallas_call(
            kernel,
            out_shape=jax.ShapeDtypeStruct((rows, span), dtype),
            grid_spec=pltpu.PrefetchScalarGridSpec(
                num_scalar_prefetch=1,
                grid=(steps,),
                in_specs=[
                    pl.BlockSpec((rows, width), lambda j, half: (0, 0)),
                    pl.BlockSpec((chunk, width), lambda j, half: ((half[0] ^ other) * steps + j, 0)),
                ]
                + extra,
                out_specs=pl.BlockSpec((rows, chunk), lambda j, half: (0, j)),
            ),
            compiler_params=pltpu.CompilerParams(vmem_limit_bytes=48 * 1024 * 1024),
        )(half, *operands)

    there = image_call(there_kernel, BF16, 1, [LATER], (grad_unit, head, send_b))

    near_back = send(gate(near_back, send_b), lambda i: i - 2)
    cross_back = send(gate(cross_back, send_b), lambda i: i - 3 if i % 2 else i - 1)
    far_term = send(gate(far_term, send_b), lambda i: i - 1 if i % 2 else i - 3)
    deep = depth // halves
    high, low = call(
        gather_kernel,
        [((rows, depth), BF16, strip(rows, deep))] * 2,
        [whole(square)] * 3 + [strip(rows, deep)] * 3,
        (own_back, near_back, cross_back, images, near_image, cross_image),
        grid=(halves,),
    )
    text_pull, dot_text = call(
        pull_kernel,
        [((rows, width), F32, strip(rows, piece)), ((1, rows), F32, whole((1, rows)))],
        [whole((rows, depth))] * 2
        + [strip(depth, piece), strip(rows, piece), strip(rows, piece), whole((rows, 2))],
        (high, low, head, far_term, texts, inverses),
        grid=(steps,),
        scratch=[pltpu.VMEM((rows, 1), F32)],
    )
    gots_a = gate(gots_a, high)
    short = lines // (YS * XS)
    keep_shape, keep_spec = (short, width // 2), strip(short, slab)
    keep_a, sent_a = call(
        sum_a_kernel,
        [(keep_shape, F32, keep_spec), (keep_shape, BF16, keep_spec)],
        side_specs + [strip(rows, slab)] * 2
        + [pl.BlockSpec((XS, lines // XS, slab), lambda j: (0, 0, j))],
        (*sides, gots_a),
        grid=(halves,),
    )
    got_a = send(sent_a, over_y)
    second = pl.BlockSpec((rows, slab), lambda j: (0, j + halves))
    keep_b, *sends_b = call(
        sum_b_kernel,
        [(keep_shape, F32, keep_spec)] + [(keep_shape, BF16, keep_spec)] * 3,
        side_specs + [second] * 2 + [strip(lines // YS, slab), LATER, LATER],
        (*sides, got_b, sent_a, far_term),
        grid=(halves,),
    )
    gots_b = [send(sends_b[d - 1], over_x(d)) for d in (2, 1, 3)]
    there = swap_tensor(gate(there, keep_b))
    dot_there = swap_tensor(dot_text)
    gots_b[2] = gate(gots_b[2], text_pull)
    last = call(
        last_kernel,
        [((short, width), BF16, whole((short, width)))],
        [whole(keep_shape)] * 6,
        (keep_a, got_a, keep_b, *gots_b),
    )[0]
    last = gate(last, there, dot_there).reshape(ZS, short // ZS, width)
    line = [
        [index_of(y, x, z, c) for z in range(ZS)]
        for y in range(YS)
        for x in range(XS)
        for c in range(CORES)
    ]
    last = lax.all_to_all(last, "dp", 0, 0, axis_index_groups=line, tiled=True)
    grad_head = call(
        line_kernel,
        [((short // ZS, width), F32, whole((short // ZS, width)))],
        [whole(last.shape)],
        (last,),
    )[0]
    piece_spec = pl.BlockSpec((rows, chunk), lambda j, half: (0, j))
    grad_images = image_call(here_kernel, BF16, 0, [piece_spec], (grad_unit, head, there))

    grad_texts = call(
        text_kernel,
        [((rows, width), BF16, strip(rows, piece))],
        [strip(rows, piece)] * 2 + [whole((rows, 2)), whole((1, rows)), whole((1, rows))],
        (text_pull, texts, inverses, dot_text, dot_there),
        grid=(steps,),
    )[0]
    return (grad_images, grad_texts, grad_head)


def solution(mesh):
    return jax.shard_map(
        per_device,
        mesh=mesh,
        in_specs=(
            P("dp", None),
            P("dp", "tensor"),
            P(None, "tensor"),
            P("dp", None),
            P("dp"),
            P(),
            P(),
        ),
        out_specs=(P("dp", "tensor"), P("dp", "tensor"), P("dp", "tensor")),
        check_vma=False,
    )
```

```python
import jax
import jax.numpy as jnp
from jax import lax
from jax.experimental import pallas as pl
from jax.experimental.pallas import tpu as pltpu
from jax.sharding import PartitionSpec as P

EPSILON = 1e-06
LOSS_WEIGHT = 16.0
YS, XS, ZS, CORES = 2, 4, 8, 2

F32 = jnp.float32
BF16 = jnp.bfloat16


def place(index):
    return index // (XS * ZS * CORES), index // (ZS * CORES) % XS, index // CORES % ZS, index % CORES


def index_of(y, x, z, core):
    return (((y % YS) * XS + x % XS) * ZS + z % ZS) * CORES + core % CORES


def route(target):
    return [(i, target(i) % (YS * XS * ZS * CORES)) for i in range(YS * XS * ZS * CORES)]


def send(block, target):
    return lax.ppermute(block, "dp", route(target))


def swap_tensor(block):
    return lax.ppermute(block, "tensor", [(0, 1), (1, 0)])


def over_x(distance):
    def target(i):
        y, x, z, core = place(i)
        return index_of(y, x + distance, z, core)

    return target


def over_z(distance):
    def target(i):
        y, x, z, core = place(i)
        return index_of(y, x, z + distance, core)

    return target


def over_y(i):
    y, x, z, core = place(i)
    return index_of(y + 1, x, z, core)


def other_core(i):
    return i ^ 1


def dot(a, b, left, right):
    return lax.dot_general(a, b, (((left,), (right,)), ((), ())), preferred_element_type=F32)


EXTRA = 16


def nothing(*refs):
    pass


def gate(value, *earlier):
    spec = pl.BlockSpec(memory_space=pl.ANY)
    return pl.pallas_call(
        nothing,
        out_shape=jax.ShapeDtypeStruct(value.shape, value.dtype),
        in_specs=[spec] * (1 + len(earlier)),
        out_specs=spec,
        input_output_aliases={0: 0},
        compiler_params=pltpu.CompilerParams(vmem_limit_bytes=48 * 1024 * 1024),
    )(value, *earlier)


def call(kernel, outs, ins, operands, grid=None, scratch=(), vmem=48, cost=0):
    shapes = [jax.ShapeDtypeStruct(shape, dtype) for shape, dtype, _ in outs]
    return pl.pallas_call(
        kernel,
        out_shape=shapes,
        grid=grid or (1,),
        in_specs=ins,
        out_specs=[spec for _, _, spec in outs],
        scratch_shapes=list(scratch),
        compiler_params=pltpu.CompilerParams(vmem_limit_bytes=vmem * 1024 * 1024),
        cost_estimate=pl.CostEstimate(flops=cost, bytes_accessed=cost // 512, transcendentals=0),
    )(*operands)


def whole(shape):
    return pl.BlockSpec(shape, lambda j: (0,) * len(shape))


def strip(rows, columns):
    return pl.BlockSpec((rows, columns), lambda j: (0, j))


SCALAR = pl.BlockSpec(memory_space=pltpu.SMEM)
LATER = pl.BlockSpec(memory_space=pl.ANY)


def diagonal(n):
    return lax.broadcasted_iota(jnp.int32, (n, n), 0) == lax.broadcasted_iota(jnp.int32, (n, n), 1)


def to_row(column):
    return jnp.sum(jnp.where(diagonal(column.shape[0]), column, 0.0), axis=0, keepdims=True)


def to_column(row):
    return jnp.sum(jnp.where(diagonal(row.shape[1]), row, 0.0), axis=1, keepdims=True)


def message(part, *rows):
    n = part.shape[1]
    line = lax.broadcasted_iota(jnp.int32, (EXTRA, n), 0)
    extra = jnp.zeros((EXTRA, n), F32)
    for k, row in enumerate(rows):
        high = row.astype(BF16).astype(F32)
        extra = jnp.where(line == 2 * k, high, jnp.where(line == 2 * k + 1, row - high, extra))
    return jnp.concatenate([part.astype(BF16), extra.astype(BF16)], axis=0)


def row_of(extra, k):
    extra = extra.astype(F32)
    return extra[2 * k : 2 * k + 1] + extra[2 * k + 1 : 2 * k + 2]


def square_sum(block):
    block = block.astype(F32)
    return jnp.sum(block * block, axis=1, keepdims=True)


def project_kernel(images, head, texts, projected, projected_b, part, sent, squares, own):
    step = pl.program_id(0)
    product = jnp.dot(images[...], head[...], preferred_element_type=F32)
    projected[...] = product
    rounded = product.astype(BF16)
    projected_b[...] = rounded
    score = dot(rounded, texts[...], 1, 1)
    square_text = square_sum(texts[...])
    square_image = square_sum(product)

    @pl.when(step == 0)
    def _():
        part[...] = score
        own[:, 0:1] = square_text
        own[:, 1:2] = square_image

    @pl.when(step > 0)
    def _():
        part[...] += score
        own[:, 0:1] += square_text
        own[:, 1:2] += square_image

    @pl.when(step == pl.num_programs(0) - 1)
    def _():
        text_row, image_row = to_row(own[:, 0:1]), to_row(own[:, 1:2])
        line = lax.broadcasted_iota(jnp.int32, squares.shape, 0)
        squares[...] = jnp.where(line == 0, text_row, image_row)
        sent[...] = message(part[...], text_row, image_row)


def tile_kernel(rounded, text, part, sent, squares):
    part[...] = dot(rounded[...], text[...], 1, 1)
    row = to_row(square_sum(text[...]))
    squares[...] = jnp.broadcast_to(row, squares.shape)
    sent[...] = message(part[...], row)


def near_kernel(rounded, text, before, part, sent, squares):
    part[...] = dot(rounded[...], text[...], 1, 1)
    row = to_row(square_sum(text[...]))
    squares[...] = jnp.broadcast_to(row, squares.shape)
    sent[0] = before[...]
    sent[1] = message(part[...], row)


def far_kernel(core, rounded, first, second, far, part, sent, squares):
    @pl.when(core[0] == 0)
    def _():
        far[...] = first[...]

    @pl.when(core[0] != 0)
    def _():
        far[...] = second[...]

    part[...] = dot(rounded[...], far[...], 1, 1)
    row = to_row(square_sum(far[...]))
    squares[...] = jnp.broadcast_to(row, squares.shape)
    sent[...] = message(part[...], row)


def coefficients(part, there, square_row, inverse_image, labels, offset, mask, scale, bias):
    n = part.shape[0]
    inverse = lax.rsqrt(square_row + row_of(there[n:], 0) + EPSILON)
    scores = (part + there[:n].astype(F32)) * inverse_image * inverse
    logits = scale * scores + bias
    columns = lax.broadcasted_iota(jnp.int32, (n, n), 1) + offset * n
    sign = jnp.where(labels == columns, 1.0, -1.0)
    weight = mask.astype(F32)
    result = (-LOSS_WEIGHT * scale * weight) * sign * jax.nn.sigmoid(-sign * logits)
    inner = jnp.sum(result * scores, axis=1, keepdims=True)
    back = result * inverse_image
    return (result * inverse).astype(BF16), inner, back, inverse


def some_kernel(
    core, scale, bias, mask, labels, own_part, own_squares, near_part, near_there, near_squares,
    cross_part, cross_there, cross_squares, texts, near, cross, later,
    pull, own_back, near_back, cross_back, inner, inverses, weights,
):
    @pl.when(pl.program_id(0) == 0)
    def _():
        n = own_part.shape[0]
        image_row = own_squares[1:2, :] + row_of(near_there[0][n:], 1)
        inverse_image = to_column(lax.rsqrt(image_row + EPSILON))
        label = to_column(labels[...].astype(F32)).astype(jnp.int32)
        rest = (inverse_image, label)
        total = jnp.zeros((n, 1), F32)
        which = 1 + 2 * core[0]
        tiles = (
            (own_part[...], near_there[0], own_squares[0:1, :], 0, own_back),
            (near_part[...], near_there[1], near_squares[0:1, :], 2, near_back),
            (cross_part[...], cross_there[...], cross_squares[0:1, :], which, cross_back),
        )
        for k, (part, there, row, offset, out) in enumerate(tiles):
            weight, dots, back, inverse = coefficients(
                part, there, row, *rest, offset, mask[0, offset], scale[0], bias[0]
            )
            weights[k] = weight
            out[...] = back.T.astype(BF16)
            total = total + dots
            if k == 0:
                inverses[:, 1:2] = to_column(inverse)
        inner[...] = total
        inverses[:, 0:1] = inverse_image

    pull[...] = (
        dot(weights[0], texts[...], 1, 0)
        + dot(weights[1], near[...], 1, 0)
        + dot(weights[2], cross[...], 1, 0)
    )


def unit_kernel(
    core, scale, bias, mask, labels, part, there, squares, far, pull, inner, inverses, projected,
    later, unit, back, weight, factor,
):
    @pl.when(pl.program_id(0) == 0)
    def _():
        inverse_image = inverses[:, 0:1]
        label = to_column(labels[...].astype(F32)).astype(jnp.int32)
        offset = 3 - 2 * core[0]
        weights, dots, backs, _ = coefficients(
            part[...], there[...], squares[0:1, :], inverse_image, label, offset,
            mask[0, offset], scale[0], bias[0],
        )
        weight[...] = weights
        back[...] = backs.astype(BF16)
        factor[...] = inverse_image * (inner[...] + dots)

    total = pull[...] + dot(weight[...], far[...], 1, 0)
    unit[...] = ((total - projected[...] * factor[...]) * inverses[:, 0:1]).astype(BF16)


def turned_kernel(place_ref, images, mine, theirs, turned):
    turned[...] = images[...].astype(F32).T.astype(BF16)
    unit = mine.shape[0] // (YS * XS * ZS)
    core, here_x, here_y = place_ref[0], place_ref[1], place_ref[2]
    for dy in range(YS):
        for dx in range(XS):
            x, y = (here_x + dx) & (XS - 1), (here_y + dy) & (YS - 1)
            for z in range(ZS):
                to = ((dy * XS + dx) * ZS + z) * unit
                block = ((y * XS + x) * ZS + z) * CORES
                for whose, out in ((core, mine), (1 - core, theirs)):
                    start = pl.multiple_of((block + whose) * unit, unit)
                    out[to : to + unit, :] = turned[pl.ds(start, unit), :]


def send_kernel(place_ref, mine, theirs, own, pair, later, send_a, send_b, left, right):
    slab = mine.shape[0] // (YS * XS)
    many = (XS - 1) * slab

    @pl.when(pl.program_id(0) == 0)
    def _():
        for dy in range(YS):
            rows = slice((dy * XS + 1) * slab, (dy * XS + XS) * slab)
            left[dy * many : (dy + 1) * many, :] = mine[rows, :]
            right[dy * many : (dy + 1) * many, :] = theirs[rows, :]

    @pl.when(pl.program_id(0) < pl.num_programs(0) // 2)
    def _():
        total = dot(left[...], own[...], 1, 0) + dot(right[...], pair[...], 1, 0)
        total = total.astype(BF16)
        here = place_ref[1]
        send_a[here] = jnp.zeros(send_a.shape[1:], BF16)
        for dy in range(YS):
            for dx in range(1, XS):
                start = dy * many + (dx - 1) * slab
                target = (here + dx) & (XS - 1)
                send_a[target, dy * slab : (dy + 1) * slab, :] = total[start : start + slab]

    @pl.when(pl.program_id(0) >= pl.num_programs(0) // 2)
    def _():
        rows = slice(XS * slab, 2 * XS * slab)
        total = dot(mine[rows, :], own[...], 1, 0) + dot(theirs[rows, :], pair[...], 1, 0)
        send_b[...] = total.astype(BF16)


def sum_a_kernel(mine, theirs, own, pair, gots, keep, sent):
    slab = mine.shape[0] // (YS * XS)
    for dy in range(YS):
        rows = slice(dy * XS * slab, (dy * XS + 1) * slab)
        total = dot(mine[rows, :], own[...], 1, 0) + dot(theirs[rows, :], pair[...], 1, 0)
        for k in range(XS):
            total = total + gots[k, dy * slab : (dy + 1) * slab, :].astype(F32)
        if dy == 0:
            keep[...] = total
        else:
            sent[...] = total.astype(BF16)


def sum_b_kernel(mine, theirs, own, pair, got, later_a, later_b, keep, s1, s2, s3):
    slab = mine.shape[0] // (YS * XS)
    rows = slice(0, XS * slab)
    total = dot(mine[rows, :], own[...], 1, 0) + dot(theirs[rows, :], pair[...], 1, 0)
    total = total + got[...].astype(F32)
    keep[...] = total[:slab]
    for k, out in enumerate((s1, s2, s3)):
        out[...] = total[(k + 1) * slab : (k + 2) * slab].astype(BF16)


def last_kernel(keep_a, got_a, keep_b, g1, g2, g3, out):
    middle = keep_a.shape[1]
    out[:, :middle] = (keep_a[...] + got_a[...].astype(F32)).astype(BF16)
    total = keep_b[...]
    for got in (g1, g2, g3):
        total = total + got[...].astype(F32)
    out[:, middle:] = total.astype(BF16)


def line_kernel(blocks, out):
    total = blocks[0].astype(F32)
    for k in range(1, blocks.shape[0]):
        total = total + blocks[k].astype(F32)
    out[...] = total


def there_kernel(half, unit, head, later, out):
    out[...] = dot(unit[...], head[...], 1, 1).astype(BF16)


def here_kernel(half, unit, head, there, out):
    out[...] = (dot(unit[...], head[...], 1, 1) + there[...].astype(F32)).astype(BF16)


def term_kernel(back, rounded, later, out):
    out[...] = dot(back[...].astype(F32).T.astype(BF16), rounded[...], 1, 0).astype(BF16)


def gather_kernel(own_back, near_back, cross_back, own, near, cross, high, low):
    total = (
        dot(own_back[...], own[...], 1, 0)
        + dot(near_back[...], near[...], 1, 0)
        + dot(cross_back[...], cross[...], 1, 0)
    )
    rounded = total.astype(BF16)
    high[...] = rounded
    low[...] = (total - rounded.astype(F32)).astype(BF16)


def pull_kernel(high, low, head, far, texts, inverses, pull, inner, column):
    step = pl.program_id(0)
    total = dot(high[...], head[...], 1, 0) + dot(low[...], head[...], 1, 0)
    total = total + far[...].astype(F32)
    pull[...] = total
    unit = texts[...].astype(F32) * inverses[:, 1:2]
    dots = jnp.sum(unit * total, axis=1, keepdims=True)

    @pl.when(step == 0)
    def _():
        column[...] = dots

    @pl.when(step > 0)
    def _():
        column[...] += dots

    @pl.when(step == pl.num_programs(0) - 1)
    def _():
        inner[...] = to_row(column[...])


def text_kernel(pull, texts, inverses, inner, there, out):
    inverse = inverses[:, 1:2]
    unit = texts[...].astype(F32) * inverse
    out[...] = ((pull[...] - unit * to_column(inner[...] + there[...])) * inverse).astype(BF16)


def per_device(images, texts, head, pair_mask, labels, logit_scale, logit_bias):
    rows, depth = images.shape
    width = texts.shape[1]
    steps = 4
    piece = width // steps
    me = lax.axis_index("dp")
    core = (me & 1)[None]
    where = jnp.stack([me & 1, (me >> 4) & (XS - 1), me >> 6])
    half = lax.axis_index("tensor")[None]
    labels = labels.reshape(1, rows)
    tile, square = (rows + EXTRA, rows), (rows, rows)

    near_text = send(texts, lambda i: i + 2)
    near_image = send(images, lambda i: i - 2)
    count = YS * XS * ZS * CORES
    odd_up = [(i, (i + 1) % count) for i in range(1, count, 2)]
    even_up = [(i, i + 1) for i in range(0, count, 2)]

    mine, theirs = call(
        turned_kernel,
        [((depth // CORES, rows), BF16, whole((depth // CORES, rows)))] * 2,
        [SCALAR, whole((rows, depth))],
        (where, images),
        scratch=[pltpu.VMEM((depth, rows), BF16)],
    )
    theirs = send(theirs, other_core)

    projected, projected_b, own_part, own_sent, own_squares = call(
        project_kernel,
        [
            ((rows, width), F32, strip(rows, piece)),
            ((rows, width), BF16, strip(rows, piece)),
            (square, F32, whole(square)),
            (tile, BF16, whole(tile)),
            ((8, rows), F32, whole((8, rows))),
        ],
        [whole((rows, depth)), strip(depth, piece), strip(rows, piece)],
        (images, head, texts),
        grid=(steps,),
        scratch=[pltpu.VMEM((rows, 128), F32)],
    )
    far_second = lax.ppermute(texts, "dp", even_up)
    near_text = gate(near_text, own_sent, theirs, mine)
    near_text = gate(near_text, far_second)
    far_first = lax.ppermute(near_text, "dp", odd_up)
    cross_text = send(near_text, other_core)
    full = whole((rows, width))
    tile_outs = [
        (square, F32, whole(square)),
        (tile, BF16, whole(tile)),
        ((8, rows), F32, whole((8, rows))),
    ]
    pair_out = ((2, *tile), BF16, whole((2, *tile)))
    near_part, near_sent, near_squares = call(
        near_kernel,
        [tile_outs[0], pair_out, tile_outs[2]],
        [full, full, whole(tile)],
        (projected_b, near_text, own_sent),
    )
    near_there = swap_tensor(near_sent)
    cross_text = gate(cross_text, near_image)
    cross_part, cross_sent, cross_squares = call(
        tile_kernel, tile_outs, [full, full], (projected_b, cross_text)
    )
    cross_there = swap_tensor(cross_sent)
    cross_image = send(near_image, other_core)
    far_text, far_part, far_sent, far_squares = call(
        far_kernel,
        [((rows, width), BF16, full)] + tile_outs,
        [SCALAR, full, full, full],
        (core, projected_b, far_first, far_second),
    )
    far_there = swap_tensor(far_sent)

    scalars = [SCALAR] * 4
    known = (core, logit_scale, logit_bias, pair_mask, labels)
    halves = 2
    wide = width // halves
    some_pull, own_back, near_back, cross_back, inner, inverses = call(
        some_kernel,
        [
            ((rows, width), F32, strip(rows, wide)),
            (square, BF16, whole(square)),
            (square, BF16, whole(square)),
            (square, BF16, whole(square)),
            ((rows, 1), F32, whole((rows, 1))),
            ((rows, 2), F32, whole((rows, 2))),
        ],
        scalars
        + [whole((1, rows))]
        + [whole(square), whole((8, rows))]
        + [whole(square), whole((2, *tile)), whole((8, rows))]
        + [whole(square), whole(tile), whole((8, rows))]
        + [strip(rows, wide)] * 3
        + [LATER],
        known
        + (own_part, own_squares, near_part, near_there, near_squares)
        + (cross_part, cross_there, cross_squares)
        + (texts, near_text, cross_text, far_sent),
        grid=(halves,),
        scratch=[pltpu.VMEM((3, *square), BF16)],
    )
    grad_unit, far_back = call(
        unit_kernel,
        [((rows, width), BF16, strip(rows, wide)), (square, BF16, whole(square))],
        scalars
        + [whole((1, rows)), whole(square), whole(tile), whole((8, rows))]
        + [strip(rows, wide), strip(rows, wide), whole((rows, 1)), whole((rows, 2))]
        + [strip(rows, wide), LATER],
        known
        + (far_part, far_there, far_squares, far_text, some_pull, inner, inverses, projected)
        + (cross_image,),
        grid=(halves,),
        scratch=[pltpu.VMEM(square, BF16), pltpu.VMEM((rows, 1), F32)],
    )

    grad_pair = send(grad_unit, other_core)
    lines = depth // CORES
    parts_of = 2 * halves
    slab = width // parts_of
    first_half = lambda j: (0, jnp.minimum(j, halves - 1))
    second_half = lambda j: (0, jnp.maximum(j - halves, 0))
    a_spec = pl.BlockSpec((XS, lines // XS, slab), lambda j: (0, *first_half(j)))
    b_spec = pl.BlockSpec((lines // YS, slab), second_half)
    a_shape, b_shape = (lines // XS, width // 2), (lines // YS, width // 2)
    sides = (mine, theirs, grad_unit, grad_pair)
    side_specs = [whole((lines, rows))] * 2
    far_term = call(
        term_kernel,
        [((rows, width), BF16, strip(rows, wide))],
        [whole(square), strip(rows, wide), LATER],
        (far_back, projected_b, grad_unit),
        grid=(halves,),
    )[0]
    send_a, send_b = call(
        send_kernel,
        [((XS, *a_shape), BF16, a_spec), (b_shape, BF16, b_spec)],
        [SCALAR] + side_specs + [strip(rows, slab)] * 2 + [LATER],
        (where, *sides, far_term),
        grid=(parts_of,),
        scratch=[pltpu.VMEM((lines // XS * (XS - 1), rows), BF16)] * 2,
    )
    got_b = send(send_b, over_y)
    squares_x = [
        [index_of(y, x, z, c) for x in range(XS)]
        for y in range(YS)
        for z in range(ZS)
        for c in range(CORES)
    ]
    gots_a = lax.all_to_all(send_a, "dp", 0, 0, axis_index_groups=squares_x, tiled=True)

    span = depth // 2
    chunk = span // steps

    def image_call(kernel, dtype, other, extra, operands):
        return pl.pallas_call(
            kernel,
            out_shape=jax.ShapeDtypeStruct((rows, span), dtype),
            grid_spec=pltpu.PrefetchScalarGridSpec(
                num_scalar_prefetch=1,
                grid=(steps,),
                in_specs=[
                    pl.BlockSpec((rows, width), lambda j, half: (0, 0)),
                    pl.BlockSpec((chunk, width), lambda j, half: ((half[0] ^ other) * steps + j, 0)),
                ]
                + extra,
                out_specs=pl.BlockSpec((rows, chunk), lambda j, half: (0, j)),
            ),
            compiler_params=pltpu.CompilerParams(vmem_limit_bytes=48 * 1024 * 1024),
        )(half, *operands)

    there = swap_tensor(image_call(there_kernel, BF16, 1, [LATER], (grad_unit, head, send_b)))

    near_back = send(gate(near_back, send_b), lambda i: i - 2)
    cross_back = send(gate(cross_back, send_b), lambda i: i - 3 if i % 2 else i - 1)
    far_term = send(gate(far_term, near_back, cross_back), lambda i: i - 1 if i % 2 else i - 3)
    deep = depth // halves
    high, low = call(
        gather_kernel,
        [((rows, depth), BF16, strip(rows, deep))] * 2,
        [whole(square)] * 3 + [strip(rows, deep)] * 3,
        (own_back, near_back, cross_back, images, near_image, cross_image),
        grid=(halves,),
    )
    text_pull, dot_text = call(
        pull_kernel,
        [((rows, width), F32, strip(rows, piece)), ((1, rows), F32, whole((1, rows)))],
        [whole((rows, depth))] * 2
        + [strip(depth, piece), strip(rows, piece), strip(rows, piece), whole((rows, 2))],
        (high, low, head, far_term, texts, inverses),
        grid=(steps,),
        scratch=[pltpu.VMEM((rows, 1), F32)],
    )
    gots_a = gate(gots_a, high)
    short = lines // (YS * XS)
    keep_shape, keep_spec = (short, width // 2), strip(short, slab)
    keep_a, sent_a = call(
        sum_a_kernel,
        [(keep_shape, F32, keep_spec), (keep_shape, BF16, keep_spec)],
        side_specs + [strip(rows, slab)] * 2
        + [pl.BlockSpec((XS, lines // XS, slab), lambda j: (0, 0, j))],
        (*sides, gots_a),
        grid=(halves,),
    )
    got_a = send(sent_a, over_y)
    second = pl.BlockSpec((rows, slab), lambda j: (0, j + halves))
    keep_b, *sends_b = call(
        sum_b_kernel,
        [(keep_shape, F32, keep_spec)] + [(keep_shape, BF16, keep_spec)] * 3,
        side_specs + [second] * 2 + [strip(lines // YS, slab), LATER, LATER],
        (*sides, got_b, sent_a, there),
        grid=(halves,),
    )
    gots_b = [send(sends_b[d - 1], over_x(d)) for d in (2, 1, 3)]
    dot_there = swap_tensor(dot_text)
    gots_b[2] = gate(gots_b[2], text_pull)
    last = call(
        last_kernel,
        [((short, width), BF16, whole((short, width)))],
        [whole(keep_shape)] * 6,
        (keep_a, got_a, keep_b, *gots_b),
    )[0]
    last = gate(last, there, dot_there).reshape(ZS, short // ZS, width)
    line = [
        [index_of(y, x, z, c) for z in range(ZS)]
        for y in range(YS)
        for x in range(XS)
        for c in range(CORES)
    ]
    last = lax.all_to_all(last, "dp", 0, 0, axis_index_groups=line, tiled=True)
    grad_head = call(
        line_kernel,
        [((short // ZS, width), F32, whole((short // ZS, width)))],
        [whole(last.shape)],
        (last,),
    )[0]
    piece_spec = pl.BlockSpec((rows, chunk), lambda j, half: (0, j))
    grad_images = image_call(here_kernel, BF16, 0, [piece_spec], (grad_unit, head, there))

    grad_texts = call(
        text_kernel,
        [((rows, width), BF16, strip(rows, piece))],
        [strip(rows, piece)] * 2 + [whole((rows, 2)), whole((1, rows)), whole((1, rows))],
        (text_pull, texts, inverses, dot_text, dot_there),
        grid=(steps,),
    )[0]
    return (grad_images, grad_texts, grad_head)


def solution(mesh):
    return jax.shard_map(
        per_device,
        mesh=mesh,
        in_specs=(
            P("dp", None),
            P("dp", "tensor"),
            P(None, "tensor"),
            P("dp", None),
            P("dp"),
            P(),
            P(),
        ),
        out_specs=(P("dp", "tensor"), P("dp", "tensor"), P("dp", "tensor")),
        check_vma=False,
    )
```

```python
import jax
import jax.numpy as jnp
from jax import lax
from jax.experimental import pallas as pl
from jax.experimental.pallas import tpu as pltpu
from jax.sharding import PartitionSpec as P

EPSILON = 1e-06
LOSS_WEIGHT = 16.0
YS, XS, ZS, CORES = 2, 4, 8, 2

F32 = jnp.float32
BF16 = jnp.bfloat16


def place(index):
    return index // (XS * ZS * CORES), index // (ZS * CORES) % XS, index // CORES % ZS, index % CORES


def index_of(y, x, z, core):
    return (((y % YS) * XS + x % XS) * ZS + z % ZS) * CORES + core % CORES


def route(target):
    return [(i, target(i) % (YS * XS * ZS * CORES)) for i in range(YS * XS * ZS * CORES)]


def send(block, target):
    return lax.ppermute(block, "dp", route(target))


def swap_tensor(block):
    return lax.ppermute(block, "tensor", [(0, 1), (1, 0)])


def over_x(distance):
    def target(i):
        y, x, z, core = place(i)
        return index_of(y, x + distance, z, core)

    return target


def over_z(distance):
    def target(i):
        y, x, z, core = place(i)
        return index_of(y, x, z + distance, core)

    return target


def over_y(i):
    y, x, z, core = place(i)
    return index_of(y + 1, x, z, core)


def other_core(i):
    return i ^ 1


def dot(a, b, left, right):
    return lax.dot_general(a, b, (((left,), (right,)), ((), ())), preferred_element_type=F32)


EXTRA = 16


def nothing(*refs):
    pass


def gate(value, *earlier):
    spec = pl.BlockSpec(memory_space=pl.ANY)
    return pl.pallas_call(
        nothing,
        out_shape=jax.ShapeDtypeStruct(value.shape, value.dtype),
        in_specs=[spec] * (1 + len(earlier)),
        out_specs=spec,
        input_output_aliases={0: 0},
        compiler_params=pltpu.CompilerParams(vmem_limit_bytes=48 * 1024 * 1024),
    )(value, *earlier)


def call(kernel, outs, ins, operands, grid=None, scratch=(), vmem=48, cost=0):
    shapes = [jax.ShapeDtypeStruct(shape, dtype) for shape, dtype, _ in outs]
    return pl.pallas_call(
        kernel,
        out_shape=shapes,
        grid=grid or (1,),
        in_specs=ins,
        out_specs=[spec for _, _, spec in outs],
        scratch_shapes=list(scratch),
        compiler_params=pltpu.CompilerParams(vmem_limit_bytes=vmem * 1024 * 1024),
        cost_estimate=pl.CostEstimate(flops=cost, bytes_accessed=cost // 512, transcendentals=0),
    )(*operands)


def whole(shape):
    return pl.BlockSpec(shape, lambda j: (0,) * len(shape))


def strip(rows, columns):
    return pl.BlockSpec((rows, columns), lambda j: (0, j))


SCALAR = pl.BlockSpec(memory_space=pltpu.SMEM)
LATER = pl.BlockSpec(memory_space=pl.ANY)


def diagonal(n):
    return lax.broadcasted_iota(jnp.int32, (n, n), 0) == lax.broadcasted_iota(jnp.int32, (n, n), 1)


def to_row(column):
    return jnp.sum(jnp.where(diagonal(column.shape[0]), column, 0.0), axis=0, keepdims=True)


def to_column(row):
    return jnp.sum(jnp.where(diagonal(row.shape[1]), row, 0.0), axis=1, keepdims=True)


def message(part, *rows):
    n = part.shape[1]
    line = lax.broadcasted_iota(jnp.int32, (EXTRA, n), 0)
    extra = jnp.zeros((EXTRA, n), F32)
    for k, row in enumerate(rows):
        high = row.astype(BF16).astype(F32)
        extra = jnp.where(line == 2 * k, high, jnp.where(line == 2 * k + 1, row - high, extra))
    return jnp.concatenate([part.astype(BF16), extra.astype(BF16)], axis=0)


def row_of(extra, k):
    extra = extra.astype(F32)
    return extra[2 * k : 2 * k + 1] + extra[2 * k + 1 : 2 * k + 2]


def square_sum(block):
    block = block.astype(F32)
    return jnp.sum(block * block, axis=1, keepdims=True)


def project_kernel(images, head, texts, projected, projected_b, part, sent, squares, own):
    step = pl.program_id(0)
    product = jnp.dot(images[...], head[...], preferred_element_type=F32)
    projected[...] = product
    rounded = product.astype(BF16)
    projected_b[...] = rounded
    score = dot(rounded, texts[...], 1, 1)
    square_text = square_sum(texts[...])
    square_image = square_sum(product)

    @pl.when(step == 0)
    def _():
        part[...] = score
        own[:, 0:1] = square_text
        own[:, 1:2] = square_image

    @pl.when(step > 0)
    def _():
        part[...] += score
        own[:, 0:1] += square_text
        own[:, 1:2] += square_image

    @pl.when(step == pl.num_programs(0) - 1)
    def _():
        text_row, image_row = to_row(own[:, 0:1]), to_row(own[:, 1:2])
        line = lax.broadcasted_iota(jnp.int32, squares.shape, 0)
        squares[...] = jnp.where(line == 0, text_row, image_row)
        sent[...] = message(part[...], text_row, image_row)


def tile_kernel(rounded, text, part, sent, squares):
    part[...] = dot(rounded[...], text[...], 1, 1)
    row = to_row(square_sum(text[...]))
    squares[...] = jnp.broadcast_to(row, squares.shape)
    sent[...] = message(part[...], row)


def near_kernel(rounded, text, before, part, sent, squares):
    part[...] = dot(rounded[...], text[...], 1, 1)
    row = to_row(square_sum(text[...]))
    squares[...] = jnp.broadcast_to(row, squares.shape)
    sent[0] = before[...]
    sent[1] = message(part[...], row)


def far_kernel(core, rounded, first, second, far, part, sent, squares):
    @pl.when(core[0] == 0)
    def _():
        far[...] = first[...]

    @pl.when(core[0] != 0)
    def _():
        far[...] = second[...]

    part[...] = dot(rounded[...], far[...], 1, 1)
    row = to_row(square_sum(far[...]))
    squares[...] = jnp.broadcast_to(row, squares.shape)
    sent[...] = message(part[...], row)


def coefficients(part, there, square_row, inverse_image, labels, offset, mask, scale, bias):
    n = part.shape[0]
    inverse = lax.rsqrt(square_row + row_of(there[n:], 0) + EPSILON)
    scores = (part + there[:n].astype(F32)) * inverse_image * inverse
    logits = scale * scores + bias
    columns = lax.broadcasted_iota(jnp.int32, (n, n), 1) + offset * n
    sign = jnp.where(labels == columns, 1.0, -1.0)
    weight = mask.astype(F32)
    result = (-LOSS_WEIGHT * scale * weight) * sign * jax.nn.sigmoid(-sign * logits)
    inner = jnp.sum(result * scores, axis=1, keepdims=True)
    back = result * inverse_image
    return (result * inverse).astype(BF16), inner, back, inverse


def some_kernel(
    core, scale, bias, mask, labels, own_part, own_squares, near_part, near_there, near_squares,
    cross_part, cross_there, cross_squares, texts, near, cross, later,
    pull, own_back, near_back, cross_back, inner, inverses, weights,
):
    @pl.when(pl.program_id(0) == 0)
    def _():
        n = own_part.shape[0]
        image_row = own_squares[1:2, :] + row_of(near_there[0][n:], 1)
        inverse_image = to_column(lax.rsqrt(image_row + EPSILON))
        label = to_column(labels[...].astype(F32)).astype(jnp.int32)
        rest = (inverse_image, label)
        total = jnp.zeros((n, 1), F32)
        which = 1 + 2 * core[0]
        tiles = (
            (own_part[...], near_there[0], own_squares[0:1, :], 0, own_back),
            (near_part[...], near_there[1], near_squares[0:1, :], 2, near_back),
            (cross_part[...], cross_there[...], cross_squares[0:1, :], which, cross_back),
        )
        for k, (part, there, row, offset, out) in enumerate(tiles):
            weight, dots, back, inverse = coefficients(
                part, there, row, *rest, offset, mask[0, offset], scale[0], bias[0]
            )
            weights[k] = weight
            out[...] = back.T.astype(BF16)
            total = total + dots
            if k == 0:
                inverses[:, 1:2] = to_column(inverse)
        inner[...] = total
        inverses[:, 0:1] = inverse_image

    pull[...] = (
        dot(weights[0], texts[...], 1, 0)
        + dot(weights[1], near[...], 1, 0)
        + dot(weights[2], cross[...], 1, 0)
    )


def unit_kernel(
    core, scale, bias, mask, labels, part, there, squares, far, pull, inner, inverses, projected,
    later_a, later_b, unit, back, weight, factor,
):
    @pl.when(pl.program_id(0) == 0)
    def _():
        inverse_image = inverses[:, 0:1]
        label = to_column(labels[...].astype(F32)).astype(jnp.int32)
        offset = 3 - 2 * core[0]
        weights, dots, backs, _ = coefficients(
            part[...], there[...], squares[0:1, :], inverse_image, label, offset,
            mask[0, offset], scale[0], bias[0],
        )
        weight[...] = weights
        back[...] = backs.astype(BF16)
        factor[...] = inverse_image * (inner[...] + dots)

    total = pull[...] + dot(weight[...], far[...], 1, 0)
    unit[...] = ((total - projected[...] * factor[...]) * inverses[:, 0:1]).astype(BF16)


def turned_kernel(place_ref, images, mine, theirs, turned):
    turned[...] = images[...].astype(F32).T.astype(BF16)
    unit = mine.shape[0] // (YS * XS * ZS)
    core, here_x, here_y = place_ref[0], place_ref[1], place_ref[2]
    for dy in range(YS):
        for dx in range(XS):
            x, y = (here_x + dx) & (XS - 1), (here_y + dy) & (YS - 1)
            for z in range(ZS):
                to = ((dy * XS + dx) * ZS + z) * unit
                block = ((y * XS + x) * ZS + z) * CORES
                for whose, out in ((core, mine), (1 - core, theirs)):
                    start = pl.multiple_of((block + whose) * unit, unit)
                    out[to : to + unit, :] = turned[pl.ds(start, unit), :]


def send_kernel(mine, theirs, own, pair, a1, a2, a3, send_b, left, right):
    slab = mine.shape[0] // (YS * XS)
    many = (XS - 1) * slab

    @pl.when(pl.program_id(0) == 0)
    def _():
        for dy in range(YS):
            rows = slice((dy * XS + 1) * slab, (dy * XS + XS) * slab)
            left[dy * many : (dy + 1) * many, :] = mine[rows, :]
            right[dy * many : (dy + 1) * many, :] = theirs[rows, :]

    @pl.when(pl.program_id(0) < pl.num_programs(0) // 2)
    def _():
        total = dot(left[...], own[...], 1, 0) + dot(right[...], pair[...], 1, 0)
        total = total.astype(BF16)
        for dy in range(YS):
            for k, out in enumerate((a1, a2, a3)):
                start = dy * many + k * slab
                out[dy * slab : (dy + 1) * slab, :] = total[start : start + slab]

    @pl.when(pl.program_id(0) >= pl.num_programs(0) // 2)
    def _():
        rows = slice(XS * slab, 2 * XS * slab)
        total = dot(mine[rows, :], own[...], 1, 0) + dot(theirs[rows, :], pair[...], 1, 0)
        send_b[...] = total.astype(BF16)


def sum_a_kernel(mine, theirs, own, pair, g1, g2, g3, keep, sent):
    slab = mine.shape[0] // (YS * XS)
    for dy in range(YS):
        rows = slice(dy * XS * slab, (dy * XS + 1) * slab)
        total = dot(mine[rows, :], own[...], 1, 0) + dot(theirs[rows, :], pair[...], 1, 0)
        for got in (g1, g2, g3):
            total = total + got[dy * slab : (dy + 1) * slab, :].astype(F32)
        if dy == 0:
            keep[...] = total
        else:
            sent[...] = total.astype(BF16)


def sum_b_kernel(mine, theirs, own, pair, got, later, keep, s1, s2, s3):
    slab = mine.shape[0] // (YS * XS)
    rows = slice(0, XS * slab)
    total = dot(mine[rows, :], own[...], 1, 0) + dot(theirs[rows, :], pair[...], 1, 0)
    total = total + got[...].astype(F32)
    keep[...] = total[:slab]
    for k, out in enumerate((s1, s2, s3)):
        out[...] = total[(k + 1) * slab : (k + 2) * slab].astype(BF16)


def last_kernel(keep_a, got_a, keep_b, g1, g2, g3, out):
    middle = keep_a.shape[1]
    out[:, :middle] = (keep_a[...] + got_a[...].astype(F32)).astype(BF16)
    total = keep_b[...]
    for got in (g1, g2, g3):
        total = total + got[...].astype(F32)
    out[:, middle:] = total.astype(BF16)


def line_kernel(blocks, out):
    total = blocks[0].astype(F32)
    for k in range(1, blocks.shape[0]):
        total = total + blocks[k].astype(F32)
    out[...] = total


def there_kernel(half, unit, head, later, out):
    out[...] = dot(unit[...], head[...], 1, 1).astype(BF16)


def here_kernel(half, unit, head, there, out):
    out[...] = (dot(unit[...], head[...], 1, 1) + there[...].astype(F32)).astype(BF16)


def gather_kernel(
    own_back, near_back, cross_back, far_back, own, near, cross, first, second, high, low
):
    far_turned = far_back[...].astype(F32).T.astype(BF16)
    total = (
        dot(own_back[...], own[...], 1, 0)
        + dot(near_back[...], near[...], 1, 0)
        + dot(cross_back[...], cross[...], 1, 0)
        + dot(far_turned, first[...], 1, 0)
        + dot(far_turned, second[...], 1, 0)
    )
    rounded = total.astype(BF16)
    high[...] = rounded
    low[...] = (total - rounded.astype(F32)).astype(BF16)


def pull_kernel(high, low, head, texts, inverses, pull, inner, column):
    step = pl.program_id(0)
    total = dot(high[...], head[...], 1, 0) + dot(low[...], head[...], 1, 0)
    pull[...] = total
    unit = texts[...].astype(F32) * inverses[:, 1:2]
    dots = jnp.sum(unit * total, axis=1, keepdims=True)

    @pl.when(step == 0)
    def _():
        column[...] = dots

    @pl.when(step > 0)
    def _():
        column[...] += dots

    @pl.when(step == pl.num_programs(0) - 1)
    def _():
        inner[...] = to_row(column[...])


def text_kernel(pull, texts, inverses, inner, there, out):
    inverse = inverses[:, 1:2]
    unit = texts[...].astype(F32) * inverse
    out[...] = ((pull[...] - unit * to_column(inner[...] + there[...])) * inverse).astype(BF16)


def per_device(images, texts, head, pair_mask, labels, logit_scale, logit_bias):
    rows, depth = images.shape
    width = texts.shape[1]
    steps = 4
    piece = width // steps
    me = lax.axis_index("dp")
    core = (me & 1)[None]
    where = jnp.stack([me & 1, (me >> 4) & (XS - 1), me >> 6])
    half = lax.axis_index("tensor")[None]
    labels = labels.reshape(1, rows)
    tile, square = (rows + EXTRA, rows), (rows, rows)

    near_text = send(texts, lambda i: i + 2)
    near_image = send(images, lambda i: i - 2)
    count = YS * XS * ZS * CORES
    odd_up = [(i, (i + 1) % count) for i in range(1, count, 2)]
    even_up = [(i, i + 1) for i in range(0, count, 2)]
    odd_down = [(i, i - 1) for i in range(1, count, 2)]
    even_down = [(i, (i - 1) % count) for i in range(0, count, 2)]

    mine, theirs = call(
        turned_kernel,
        [((depth // CORES, rows), BF16, whole((depth // CORES, rows)))] * 2,
        [SCALAR, whole((rows, depth))],
        (where, images),
        scratch=[pltpu.VMEM((depth, rows), BF16)],
    )
    theirs = send(theirs, other_core)

    projected, projected_b, own_part, own_sent, own_squares = call(
        project_kernel,
        [
            ((rows, width), F32, strip(rows, piece)),
            ((rows, width), BF16, strip(rows, piece)),
            (square, F32, whole(square)),
            (tile, BF16, whole(tile)),
            ((8, rows), F32, whole((8, rows))),
        ],
        [whole((rows, depth)), strip(depth, piece), strip(rows, piece)],
        (images, head, texts),
        grid=(steps,),
        scratch=[pltpu.VMEM((rows, 128), F32)],
    )
    far_second = lax.ppermute(texts, "dp", even_up)
    far_image_second = lax.ppermute(images, "dp", odd_down)
    near_text = gate(near_text, own_sent, theirs, mine)
    near_text = gate(near_text, far_second, far_image_second)
    far_first = lax.ppermute(near_text, "dp", odd_up)
    cross_text = send(near_text, other_core)
    full = whole((rows, width))
    tile_outs = [
        (square, F32, whole(square)),
        (tile, BF16, whole(tile)),
        ((8, rows), F32, whole((8, rows))),
    ]
    pair_out = ((2, *tile), BF16, whole((2, *tile)))
    near_part, near_sent, near_squares = call(
        near_kernel,
        [tile_outs[0], pair_out, tile_outs[2]],
        [full, full, whole(tile)],
        (projected_b, near_text, own_sent),
    )
    near_there = swap_tensor(near_sent)
    near_image = gate(near_image, near_there)
    cross_text = gate(cross_text, near_image)
    cross_part, cross_sent, cross_squares = call(
        tile_kernel, tile_outs, [full, full], (projected_b, cross_text)
    )
    cross_there = swap_tensor(cross_sent)
    near_image = gate(near_image, cross_sent)
    far_image_first = lax.ppermute(near_image, "dp", even_down)
    cross_image = send(near_image, other_core)
    far_text, far_part, far_sent, far_squares = call(
        far_kernel,
        [((rows, width), BF16, full)] + tile_outs,
        [SCALAR, full, full, full],
        (core, projected_b, far_first, far_second),
    )
    far_there = swap_tensor(far_sent)

    scalars = [SCALAR] * 4
    known = (core, logit_scale, logit_bias, pair_mask, labels)
    halves = 2
    wide = width // halves
    some_pull, own_back, near_back, cross_back, inner, inverses = call(
        some_kernel,
        [
            ((rows, width), F32, strip(rows, wide)),
            (square, BF16, whole(square)),
            (square, BF16, whole(square)),
            (square, BF16, whole(square)),
            ((rows, 1), F32, whole((rows, 1))),
            ((rows, 2), F32, whole((rows, 2))),
        ],
        scalars
        + [whole((1, rows))]
        + [whole(square), whole((8, rows))]
        + [whole(square), whole((2, *tile)), whole((8, rows))]
        + [whole(square), whole(tile), whole((8, rows))]
        + [strip(rows, wide)] * 3
        + [LATER],
        known
        + (own_part, own_squares, near_part, near_there, near_squares)
        + (cross_part, cross_there, cross_squares)
        + (texts, near_text, cross_text, far_sent),
        grid=(halves,),
        scratch=[pltpu.VMEM((3, *square), BF16)],
    )
    grad_unit, far_back = call(
        unit_kernel,
        [((rows, width), BF16, strip(rows, wide)), (square, BF16, whole(square))],
        scalars
        + [whole((1, rows)), whole(square), whole(tile), whole((8, rows))]
        + [strip(rows, wide), strip(rows, wide), whole((rows, 1)), whole((rows, 2))]
        + [strip(rows, wide), LATER, LATER],
        known
        + (far_part, far_there, far_squares, far_text, some_pull, inner, inverses, projected)
        + (far_image_first, cross_image),
        grid=(halves,),
        scratch=[pltpu.VMEM(square, BF16), pltpu.VMEM((rows, 1), F32)],
    )

    grad_pair = send(grad_unit, other_core)
    lines = depth // CORES
    parts_of = 2 * halves
    slab = width // parts_of
    first_half = lambda j: (0, jnp.minimum(j, halves - 1))
    second_half = lambda j: (0, jnp.maximum(j - halves, 0))
    a_spec = pl.BlockSpec((lines // XS, slab), first_half)
    b_spec = pl.BlockSpec((lines // YS, slab), second_half)
    a_shape, b_shape = (lines // XS, width // 2), (lines // YS, width // 2)
    sides = (mine, theirs, grad_unit, grad_pair)
    side_specs = [whole((lines, rows))] * 2
    send_1, send_2, send_3, send_b = call(
        send_kernel,
        [(a_shape, BF16, a_spec)] * 3 + [(b_shape, BF16, b_spec)],
        side_specs + [strip(rows, slab)] * 2,
        sides,
        grid=(parts_of,),
        scratch=[pltpu.VMEM((lines // XS * (XS - 1), rows), BF16)] * 2,
    )
    got_b = send(send_b, over_y)
    gots_a = [send(block, over_x(d)) for d, block in ((2, send_2), (1, send_1), (3, send_3))]

    span = depth // 2
    chunk = span // steps

    def image_call(kernel, dtype, other, extra, operands):
        return pl.pallas_call(
            kernel,
            out_shape=jax.ShapeDtypeStruct((rows, span), dtype),
            grid_spec=pltpu.PrefetchScalarGridSpec(
                num_scalar_prefetch=1,
                grid=(steps,),
                in_specs=[
                    pl.BlockSpec((rows, width), lambda j, half: (0, 0)),
                    pl.BlockSpec((chunk, width), lambda j, half: ((half[0] ^ other) * steps + j, 0)),
                ]
                + extra,
                out_specs=pl.BlockSpec((rows, chunk), lambda j, half: (0, j)),
            ),
            compiler_params=pltpu.CompilerParams(vmem_limit_bytes=48 * 1024 * 1024),
        )(half, *operands)

    there = image_call(there_kernel, BF16, 1, [LATER], (grad_unit, head, send_b))

    near_back = send(gate(near_back, send_b), lambda i: i - 2)
    cross_back = send(gate(cross_back, send_b), lambda i: i - 3 if i % 2 else i - 1)
    far_back = send(gate(far_back, send_b), lambda i: i - 1 if i % 2 else i - 3)
    deep = depth // halves
    high, low = call(
        gather_kernel,
        [((rows, depth), BF16, strip(rows, deep))] * 2,
        [whole(square)] * 4 + [strip(rows, deep)] * 5,
        (own_back, near_back, cross_back, far_back)
        + (images, near_image, cross_image, far_image_first, far_image_second),
        grid=(halves,),
    )
    text_pull, dot_text = call(
        pull_kernel,
        [((rows, width), F32, strip(rows, piece)), ((1, rows), F32, whole((1, rows)))],
        [whole((rows, depth))] * 2
        + [strip(depth, piece), strip(rows, piece), whole((rows, 2))],
        (high, low, head, texts, inverses),
        grid=(steps,),
        scratch=[pltpu.VMEM((rows, 1), F32)],
    )
    gots_a[2] = gate(gots_a[2], high)
    short = lines // (YS * XS)
    keep_shape, keep_spec = (short, width // 2), strip(short, slab)
    keep_a, sent_a = call(
        sum_a_kernel,
        [(keep_shape, F32, keep_spec), (keep_shape, BF16, keep_spec)],
        side_specs + [strip(rows, slab)] * 2 + [strip(lines // XS, slab)] * 3,
        (*sides, *gots_a),
        grid=(halves,),
    )
    got_a = send(sent_a, over_y)
    second = pl.BlockSpec((rows, slab), lambda j: (0, j + halves))
    keep_b, *sends_b = call(
        sum_b_kernel,
        [(keep_shape, F32, keep_spec)] + [(keep_shape, BF16, keep_spec)] * 3,
        side_specs + [second] * 2 + [strip(lines // YS, slab), LATER],
        (*sides, got_b, sent_a),
        grid=(halves,),
    )
    gots_b = [send(sends_b[d - 1], over_x(d)) for d in (2, 1, 3)]
    there = swap_tensor(gate(there, keep_b))
    dot_there = swap_tensor(dot_text)
    gots_b[2] = gate(gots_b[2], text_pull)
    last = call(
        last_kernel,
        [((short, width), BF16, whole((short, width)))],
        [whole(keep_shape)] * 6,
        (keep_a, got_a, keep_b, *gots_b),
    )[0]
    last = gate(last, there, dot_there).reshape(ZS, short // ZS, width)
    line = [
        [index_of(y, x, z, c) for z in range(ZS)]
        for y in range(YS)
        for x in range(XS)
        for c in range(CORES)
    ]
    last = lax.all_to_all(last, "dp", 0, 0, axis_index_groups=line, tiled=True)
    grad_head = call(
        line_kernel,
        [((short // ZS, width), F32, whole((short // ZS, width)))],
        [whole(last.shape)],
        (last,),
    )[0]
    piece_spec = pl.BlockSpec((rows, chunk), lambda j, half: (0, j))
    grad_images = image_call(here_kernel, BF16, 0, [piece_spec], (grad_unit, head, there))

    grad_texts = call(
        text_kernel,
        [((rows, width), BF16, strip(rows, piece))],
        [strip(rows, piece)] * 2 + [whole((rows, 2)), whole((1, rows)), whole((1, rows))],
        (text_pull, texts, inverses, dot_text, dot_there),
        grid=(steps,),
    )[0]
    return (grad_images, grad_texts, grad_head)


def solution(mesh):
    return jax.shard_map(
        per_device,
        mesh=mesh,
        in_specs=(
            P("dp", None),
            P("dp", "tensor"),
            P(None, "tensor"),
            P("dp", None),
            P("dp"),
            P(),
            P(),
        ),
        out_specs=(P("dp", "tensor"), P("dp", "tensor"), P("dp", "tensor")),
        check_vma=False,
    )
```
